512 devices in a mesh: gx: 16 (over z_lo, core), gy: 4 (over x), gz: 8 (over z_hi, y).
Axes of the slice: x: 4, y: 4, z: 16 (z_hi: 2, z_lo: 8; z = z_hi * 8 + z_lo), core: 2. Of those that a mesh axis runs over, the one named last changes fastest.
Arguments:
- velocity: float32 [3, 5242880], P(None, ('gx', 'gy', 'gz')), may hold values from -6 to 6
- position: int32 [2, 3, 5242880], P(None, None, ('gx', 'gy', 'gz')), may hold values from 0 to 511, as said below
- bead_velocity: float32 [3, 524288], P(None, ('gx', 'gy', 'gz')), may hold values from -6 to 6
- bead_mass: float32 [524288], P(('gx', 'gy', 'gz')), may hold values from 1 to 10
- bead_position: int32 [2, 3, 524288], P(None, None, ('gx', 'gy', 'gz')), may hold values from 0 to 511, as said below
- grid_shift: int32 [2, 3], replicated, may hold values from -8 to 8, as said below
- rot_axis: int32 [2, 64, 128, 128], P(None, 'gx', 'gy', 'gz'), may hold values from 0 to 63
- leave_count: int32 [3, 2, 512], P(None, None, ('gx', 'gy', 'gz')), may hold values from 1 to 256, as said below
- leave_index: int32 [3, 2, 131072], P(None, None, ('gx', 'gy', 'gz')), may hold values from -1 to 10239, as said below
Outputs:
- velocity_out: float32 [3, 5242880], P(None, ('gx', 'gy', 'gz'))
- bead_out: float32 [3, 524288], P(None, ('gx', 'gy', 'gz'))
- arrivals: float32 [3, 2, 3, 131072], P(None, None, None, ('gx', 'gy', 'gz'))
The draws below stay inside these ranges and needn't reach their ends.
Inputs may be any that keep to these rules, and one draw needn't show every extreme that they name: `position`: coordinates of a device's own particles: along the dimensions 0 to 63, 0 to 511 and 0 to 255. `bead_position`: coordinates of a device's own beads, in the same ranges as the particles. `grid_shift`: never zero; along each dimension the two steps shift in opposite directions, and along one dimension both by 8. `leave_count`: for every dimension and side, some device's count is exactly 256. `leave_index`: entries before a face's count are indices of the device's own particles; the rest are -1.
All inputs are finite; a program needn't handle non-finite values.
Results may differ from the reference program's by a relative error of at most 0.00013.
Values sent between devices are 32-bit elements; how exact they have to be, the bound alone decides.
A program may use at most 64 MiB of HBM per device.

```python
import math
import jax
import jax.numpy as jnp
from jax import lax

CX = 4
CY = 32
CZ = 16
STEPS = 2
SUB = 16
AXES = 64
CAP = 256
SLOTS = 10240
BEADS_DEV = 1024
TOTAL = 5242880
BEADS = 524288
NX = 64
NY = 128
NZ = 128
N_GX = 16
N_GY = 4
N_GZ = 8
DEVICES = 512


def draw_coordinates(key, count):
    limits = jnp.array([SUB * CX, SUB * CY, SUB * CZ], jnp.int32)
    return jax.random.randint(key, (STEPS, 3, count), 0, limits[None, :, None], dtype=jnp.int32)


def draw_position(key, part):
    key = jax.random.fold_in(key, 1)
    return draw_coordinates(key, TOTAL)


def draw_bead_position(key, part):
    key = jax.random.fold_in(key, 2)
    return draw_coordinates(key, BEADS)


def draw_grid_shift(key, part):
    key = jax.random.fold_in(key, 3)
    subkeys = jax.random.split(key, 3)
    direction = 2 * jax.random.randint(subkeys[0], (3,), 0, 2, dtype=jnp.int32) - 1
    magnitude = jax.random.randint(subkeys[1], (2, 3), 1, SUB // 2 + 1, dtype=jnp.int32)
    widest = jax.random.randint(subkeys[2], (), 0, 3, dtype=jnp.int32)
    magnitude = jnp.where(jnp.arange(3, dtype=jnp.int32)[None, :] == widest, SUB // 2, magnitude)
    return jnp.stack([direction * magnitude[0], -direction * magnitude[1]])


def leaving_counts(key):
    key = jax.random.fold_in(key, 11)
    subkeys = jax.random.split(key, 2)
    rolled = jax.random.randint(subkeys[0], (3, 2, DEVICES), 1, CAP + 1, dtype=jnp.int32)
    counts = (rolled * rolled + CAP - 1) // CAP
    fullest = jax.random.randint(subkeys[1], (3, 2, 1), 0, DEVICES, dtype=jnp.int32)
    return jnp.where(jnp.arange(DEVICES, dtype=jnp.int32)[None, None, :] == fullest, CAP, counts)


def draw_leave_count(key, part):
    counts = leaving_counts(key)
    return counts


def draw_leave_index(key, part):
    counts = leaving_counts(key)
    key = jax.random.fold_in(key, 4)
    subkeys = jax.random.split(key, 3)
    chosen = jax.random.randint(subkeys[0], (3, 2, DEVICES, CAP), 0, SLOTS, dtype=jnp.int32)
    marked_face = jax.random.randint(subkeys[1], (), 0, 6, dtype=jnp.int32)
    marked_device = jax.random.randint(subkeys[2], (), 0, DEVICES, dtype=jnp.int32)
    face_number = (jnp.arange(3, dtype=jnp.int32)[:, None] * 2 + jnp.arange(2, dtype=jnp.int32)[None, :])[:, :, None, None]
    device_number = jnp.arange(DEVICES, dtype=jnp.int32)[None, None, :, None]
    slot_number = jnp.arange(CAP, dtype=jnp.int32)[None, None, None, :]
    is_marked = (face_number == marked_face) & (device_number == marked_device) & (slot_number == 0)
    chosen = jnp.where(is_marked, SLOTS - 1, chosen)
    usable = slot_number < counts[:, :, :, None]
    return jnp.where(usable, chosen, -1).reshape(3, 2, DEVICES * CAP)


def with_ends(values, stream_key, least, top_value):
    longest = values.shape.index(max(values.shape))
    spots = []
    for shift in (0, 1):
        where = [jax.random.randint(jax.random.fold_in(stream_key, axis), (), 0, length) for axis, length in enumerate(values.shape)]
        where[longest] = (where[longest] + shift) % values.shape[longest]
        spots.append(tuple(where))
    return values.at[spots[0]].set(least).at[spots[1]].set(top_value)


def block_levels(own_key, dims, shards, low, largest):
    gain, own = 1.0, jax.random.fold_in(own_key, 6)
    for dim, parts in shards:
        heights = jnp.exp(jax.random.uniform(jax.random.fold_in(own, dim), (parts,), jnp.float32, low / len(shards), largest / len(shards)))
        gain = gain * jnp.repeat(heights, dims[dim] // parts).reshape([-1 if axis == dim else 1 for axis in range(len(dims))])
    return gain


def bell_draw(stream_key, shape, width, limit, cuts=(), kind=jnp.bfloat16):
    level = block_levels(stream_key, shape, cuts, -0.22, 0.18) if cuts else 1.0
    drawn = jax.random.normal(stream_key, shape, jnp.float32) * width * level
    return jnp.minimum(jnp.maximum(drawn, -limit), limit).astype(kind)


def setup_inputs(seed: int = 0) -> dict:
    streams_of = jax.random.split(jax.random.key(seed), 10)
    return {
        "velocity": bell_draw(streams_of[0], (3, TOTAL), 1.0, 6.0, ((1, 512),), jnp.float32),
        "position": draw_position(jax.random.fold_in(streams_of[9], 71), 0),
        "bead_velocity": bell_draw(streams_of[2], (3, BEADS), 0.5, 6.0, ((1, 512),), jnp.float32),
        "bead_mass": jnp.clip(jnp.exp(math.log(10.0) - 2.3025851 * jax.random.uniform(streams_of[3], (BEADS,), jnp.float32) ** block_levels(streams_of[3], (BEADS,), ((0, 512),), -0.2, 0.2)), 1.0, 10.0),
        "bead_position": draw_bead_position(jax.random.fold_in(streams_of[9], 71), 0),
        "grid_shift": draw_grid_shift(jax.random.fold_in(streams_of[9], 71), 0),
        "rot_axis": with_ends(jax.random.randint(streams_of[6], (STEPS, NX, NY, NZ), 0, AXES), jax.random.fold_in(streams_of[6], 1), 0, AXES - 1).astype(jnp.int32),
        "leave_count": draw_leave_count(jax.random.fold_in(streams_of[9], 71), 0),
        "leave_index": draw_leave_index(jax.random.fold_in(streams_of[9], 71), 0),
    }


COSINE = math.cos(130.0 * math.pi / 180.0)
SINE = math.sin(130.0 * math.pi / 180.0)
GOLDEN = math.pi * (3.0 - math.sqrt(5.0))

def axis_table():
    ordinal = jnp.arange(AXES, dtype=jnp.float32) + 0.5
    height = 1.0 - 2.0 * ordinal / AXES
    radius = jnp.sqrt(1.0 - height * height)
    turning = ordinal * GOLDEN
    return jnp.stack([radius * jnp.cos(turning), radius * jnp.sin(turning), height])

def cells_of(coords, shift, bricks, counts):
    combined = jnp.zeros(coords.shape[1:], jnp.int32)
    for axis_number in range(3):
        layer_index = jnp.floor_divide(coords[axis_number] - shift[axis_number], SUB)
        device_place = lax.broadcasted_iota(jnp.int32, coords.shape[1:], axis_number)
        cells_along = bricks[axis_number] * counts[axis_number]
        global_cell = jnp.mod(device_place * bricks[axis_number] + layer_index, cells_along)
        combined = combined * cells_along + global_cell
    return combined.reshape(-1)

def reference(velocity, position, bead_velocity, bead_mass, bead_position, grid_shift, rot_axis, leave_count, leave_index):
    device_grid = (N_GX, N_GY, N_GZ)
    bricks = (CX, CY, CZ)
    total_cells = NX * NY * NZ
    table = axis_table()
    weights = jnp.concatenate([jnp.ones((TOTAL,), jnp.float32), bead_mass])
    for step_index in range(STEPS):
        shift = grid_shift[step_index]
        solvent_cells = cells_of(position[step_index].reshape((3,) + device_grid + (SLOTS,)), shift, bricks, device_grid)
        bead_cells = cells_of(bead_position[step_index].reshape((3,) + device_grid + (BEADS_DEV,)), shift, bricks, device_grid)
        all_cells = jnp.concatenate([solvent_cells, bead_cells])
        moving = jnp.concatenate([velocity, bead_velocity], axis=1)
        masses = jax.ops.segment_sum(weights, all_cells, num_segments=total_cells)
        momenta = jnp.stack([jax.ops.segment_sum(moving[component] * weights, all_cells, num_segments=total_cells) for component in range(3)])
        means = momenta / jnp.maximum(masses, 1.0)[None]
        normals = table[:, rot_axis[step_index].reshape(-1)]
        cell_mean = jnp.take(means, all_cells, axis=1)
        cell_normal = jnp.take(normals, all_cells, axis=1)
        relative = moving - cell_mean
        along = lax.optimization_barrier(jnp.sum(cell_normal * relative, axis=0))
        crossed = jnp.stack([cell_normal[1] * relative[2] - cell_normal[2] * relative[1], cell_normal[2] * relative[0] - cell_normal[0] * relative[2], cell_normal[0] * relative[1] - cell_normal[1] * relative[0]])
        moving = cell_mean + COSINE * relative + SINE * crossed + (1.0 - COSINE) * along[None] * cell_normal
        velocity = moving[:, :TOTAL]
        bead_velocity = moving[:, TOTAL:]
    per_device = velocity.reshape((3,) + device_grid + (SLOTS,))
    counts = leave_count.reshape((3, 2) + device_grid)
    lists = leave_index.reshape((3, 2) + device_grid + (CAP,))
    slot_number = jnp.arange(CAP, dtype=jnp.int32)
    received = []
    for axis_number in range(3):
        sent = []
        for side in range(2):
            chosen = jnp.take_along_axis(per_device, jnp.maximum(lists[axis_number, side], 0)[None], axis=4)
            usable = slot_number < counts[axis_number, side][..., None]
            sent.append(jnp.where(usable[None], chosen, 0.0))
        from_lower = jnp.roll(sent[1], 1, axis=1 + axis_number)
        from_upper = jnp.roll(sent[0], -1, axis=1 + axis_number)
        received.append(jnp.stack([from_lower, from_upper]))
    arrivals = jnp.stack(received).reshape(3, 2, 3, DEVICES * CAP)
    return (velocity, bead_velocity, arrivals)
```

```python
import math

import jax
import jax.numpy as jnp
import numpy as np
from jax import lax
from jax.experimental import pallas as pl
from jax.experimental.pallas import tpu as pltpu
from jax.sharding import PartitionSpec as P

STEPS = 2
AXES = 64
CAP = 256
COSINE = math.cos(130.0 * math.pi / 180.0)
SINE = math.sin(130.0 * math.pi / 180.0)
GOLDEN = math.pi * (3.0 - math.sqrt(5.0))

LANES = 128
CHUNK = 1024
COLUMNS = 176
LAYERS = 18
WIDE = 256
MESH = pl.DeviceIdType.MESH
F32 = jnp.float32
BF16 = jnp.bfloat16
I32 = jnp.int32


def rotation_table():
    ordinal = np.arange(AXES) + 0.5
    height = 1.0 - 2.0 * ordinal / AXES
    radius = np.sqrt(1.0 - height * height)
    n = np.stack([radius * np.cos(ordinal * GOLDEN), radius * np.sin(ordinal * GOLDEN), height])
    zero = np.zeros(AXES)
    skew = np.array([[zero, -n[2], n[1]], [n[2], zero, -n[0]], [-n[1], n[0], zero]])
    matrix = COSINE * np.eye(3)[:, :, None] + SINE * skew + (1.0 - COSINE) * n[:, None] * n[None]
    table = np.zeros((3, 8, LANES), np.float32)
    for c in range(3):
        table[c, 0:3, :AXES] = matrix[:, c]
        table[c, 4:7, :AXES] = matrix[:, c]
    return table


def rows_of(shape):
    return lax.broadcasted_iota(I32, shape, 0)


def lanes_of(shape):
    return lax.broadcasted_iota(I32, shape, 1)


def cell_rows(coords, shift_ref, step):
    layer = []
    for d in range(3):
        shift = shift_ref[step, d]
        offset = jnp.where(shift > 0, 1, 0)
        layer.append(lax.shift_right_arithmetic(coords[d] - shift, 4) + offset)
    return column_of(layer[0], layer[1]), layer[2]


def column_of(first, second):
    inner = first * 32 + second
    return jnp.where(second == 32, first + 160, jnp.where(second == 0, first + 165, inner))


def one_hot(column):
    n = column.shape[1]
    rest = column.astype(F32) - rows_of((16, n)).astype(F32)
    rest = rest.astype(BF16)
    one, zero = jnp.ones((16, n), BF16), jnp.zeros((16, n), BF16)
    return jnp.concatenate(
        [jnp.where(rest == float(16 * j), one, zero) for j in range(COLUMNS // 16)], axis=0
    )


def deposit_rows(moving, weight, layer):
    n = moving.shape[1]
    row8 = rows_of((8, n))
    summand = moving * weight
    high = summand.astype(BF16).astype(F32)
    parts = jnp.where(row8 < 4, high, summand - high)
    parts = jnp.concatenate([parts, parts], axis=0).astype(BF16)
    half = lax.shift_right_logical(rows_of((16, n)), 3)
    rest = (layer - half).astype(F32).astype(BF16)
    zero = jnp.zeros((16, n), BF16)
    return jnp.concatenate(
        [jnp.where(rest == float(2 * j), parts, zero) for j in range(LAYERS // 2)], axis=0
    )


def collide(moving, layer, gathered, tables):
    n = moving.shape[1]
    chosen = gathered[0:8]
    for z in range(1, 17):
        chosen = jnp.where(layer == z, gathered[8 * z : 8 * z + 8], chosen)
    mean = chosen + pltpu.roll(chosen, 4, 0)
    axis = jnp.broadcast_to(mean[3:4], (8, n)).astype(I32)
    relative = moving - mean
    result = mean
    for c in range(3):
        columns = jnp.concatenate(
            [
                jnp.take_along_axis(tables[c], axis[:, i : i + LANES], axis=1)
                for i in range(0, n, LANES)
            ],
            axis=1,
        )
        result = result + columns * relative[c : c + 1]
    row8 = rows_of((8, n))
    return jnp.where((row8 & 3) == 3, 1.0, result)


def kernel(
    shift_ref, count_ref, velocity_ref, position_ref, bead_velocity_ref, bead_mass_ref,
    bead_position_ref, rot_ref, leave_ref, table_ref,
    velocity_out, bead_out, arrivals_out,
    moving, weight, cols, lays, onehots, totals, cells, results,
    send_y, send_x, recv_z, recv_y, recv_x,
    leave_table, leave_moving, leave_layer, leave_onehot, leave_send, leave_recv,
    send_sem, recv_sem,
):
    solvent = velocity_ref.shape[1]
    beads = bead_velocity_ref.shape[1]
    count = solvent + beads
    chunks = count // CHUNK

    names = ("gx", "gy", "gz")
    neighbour = []
    for name in names:
        size, me = lax.axis_size(name), lax.axis_index(name)
        neighbour.append((lax.rem(me + size - 1, size), lax.rem(me + 1, size)))

    barrier = pltpu.get_barrier_semaphore()
    for d in range(3):
        for side in range(2):
            pl.semaphore_signal(
                barrier, inc=1, device_id={names[d]: neighbour[d][side]}, device_id_type=MESH
            )

    def remote(src, dst, number, d, side):
        return pltpu.make_async_remote_copy(
            src_ref=src,
            dst_ref=dst,
            send_sem=send_sem.at[number],
            recv_sem=recv_sem.at[number],
            device_id={names[d]: neighbour[d][side]},
            device_id_type=MESH,
        )

    def load(velocity, where, length):
        moving[0:3, pl.ds(where, length)] = velocity
        moving[3:4, pl.ds(where, length)] = jnp.ones((1, length), F32)
        moving[4:7, pl.ds(where, length)] = velocity
        moving[7:8, pl.ds(where, length)] = jnp.ones((1, length), F32)

    load(velocity_ref[...], 0, solvent)
    load(bead_velocity_ref[...], solvent, beads)
    weight[:, 0:solvent] = jnp.ones((1, solvent), F32)
    weight[:, solvent:count] = bead_mass_ref[...]

    def place(step, first, number):
        def body(i, carry):
            here = pl.ds(pl.multiple_of(i * CHUNK, CHUNK), CHUNK)
            coords = [position_ref[d, step : step + 1, here] for d in range(3)]
            column, layer = cell_rows(coords, shift_ref, step)
            cols[step, :, here] = column
            lays[step, :, here] = layer
            onehots[step, :, here] = one_hot(column)
            return carry

        lax.fori_loop(first, first + number, body, 0)

    def place_beads(step):
        here = pl.ds(solvent, beads)
        coords = [bead_position_ref[d, step : step + 1, :] for d in range(3)]
        column, layer = cell_rows(coords, shift_ref, step)
        cols[step, :, here] = column
        lays[step, :, here] = layer
        onehots[step, :, here] = one_hot(column)

    def deposit(step, here, moved):
        rows = deposit_rows(moved, weight[:, here], lays[step, :, here])
        totals[...] += lax.dot_general(
            rows, onehots[step, :, here], (((1,), (1,)), ((), ())), preferred_element_type=F32
        )

    lane = lanes_of((8, LANES))

    def own_axes(step):
        offset = [jnp.where(shift_ref[step, d] > 0, 1, 0) for d in range(3)]
        local = rows_of((LANES, WIDE))
        target = column_of(
            lax.shift_right_logical(local, 5) + offset[0], (local & 31) + offset[1]
        )
        spread = jnp.where(lanes_of((LANES, WIDE)) == target, 1.0, 0.0).astype(BF16)
        held = jnp.concatenate([rot_ref[step, x] for x in range(4)], axis=1)
        by_layer = jnp.dot(
            held.astype(F32).astype(BF16), spread, preferred_element_type=F32
        )
        above = jnp.concatenate([jnp.zeros((1, WIDE), F32), by_layer], axis=0)
        below = jnp.concatenate([by_layer, jnp.zeros((1, WIDE), F32)], axis=0)
        return jnp.where(offset[2] > 0, above, below)

    def exchange(step, between):
        axes = own_axes(step)
        row8 = rows_of((8, WIDE))
        cells[:, :, COLUMNS:WIDE] = jnp.zeros((LAYERS, 8, WIDE - COLUMNS), F32)
        for z in range(17):
            part = totals[8 * z : 8 * z + 8, :]
            cells[z, :, 0:COLUMNS] = part + pltpu.roll(part, 4, 0)
            cells[z] = jnp.where(row8 == 7, axes[z : z + 1], cells[z])
        base = 6 * step
        if step == 0:
            pl.semaphore_wait(barrier, 6)

        low = remote(cells.at[0], recv_z.at[step, 1], base, 2, 0)
        high = remote(cells.at[16], recv_z.at[step, 0], base + 1, 2, 1)
        low.start()
        high.start()
        between(0)
        low.wait()
        high.wait()
        cells[0] += recv_z[step, 0]
        cells[16] += recv_z[step, 1]

        for group in range(2):
            packed = jnp.zeros((8, LANES), F32)
            for j in range(9):
                z = 9 * group + j
                if z < 17:
                    turned = pltpu.roll(cells[z, :, LANES:WIDE], (12 * j - 32) % LANES, 1)
                    packed = jnp.where((lane >= 12 * j) & (lane < 12 * j + 10), turned, packed)
            send_y[step, group] = packed
        low = remote(send_y.at[step], recv_y.at[step, 1], base + 2, 1, 0)
        high = remote(send_y.at[step], recv_y.at[step, 0], base + 3, 1, 1)
        low.start()
        high.start()
        between(1)
        low.wait()
        high.wait()
        place12 = lax.rem(lane, 12)
        for group in range(2):
            from_low = pltpu.roll(recv_y[step, 0, group], 5, 1)
            from_high = pltpu.roll(recv_y[step, 1, group], LANES - 5, 1)
            both = jnp.where(place12 < 5, from_high, from_low)
            for j in range(9):
                z = 9 * group + j
                if z < 17:
                    turned = pltpu.roll(both, (32 - 12 * j) % LANES, 1)
                    cells[z, :, LANES:WIDE] += jnp.where((lane >= 32) & (lane < 42), turned, 0.0)

        for group in range(6):
            packed_low = jnp.zeros((8, LANES), F32)
            packed_high = jnp.zeros((8, LANES), F32)
            for j in range(3):
                z = 3 * group + j
                if z < 17:
                    near, far = cells[z, :, 0:LANES], cells[z, :, LANES:WIDE]
                    face_low = jnp.where(lane < 32, near, far)
                    face_high = jnp.where(lane < 32, far, pltpu.roll(far, LANES - 4, 1))
                    if j:
                        face_low = pltpu.roll(face_low, 42 * j, 1)
                        face_high = pltpu.roll(face_high, 42 * j, 1)
                    inside = (lane >= 42 * j) & (lane < 42 * j + 38)
                    packed_low = jnp.where(inside, face_low, packed_low)
                    packed_high = jnp.where(inside, face_high, packed_high)
            send_x[step, 0, group] = packed_low
            send_x[step, 1, group] = packed_high
        low = remote(send_x.at[step, 0], recv_x.at[step, 1], base + 4, 0, 0)
        high = remote(send_x.at[step, 1], recv_x.at[step, 0], base + 5, 0, 1)
        low.start()
        high.start()
        between(2)
        low.wait()
        high.wait()
        ends = (lane == 32) | (lane == 37)
        ends_high = (lane == 36) | (lane == 41)
        row8 = rows_of((8, LANES))
        pending = None
        for group in range(6):
            for j in range(3):
                z = 3 * group + j
                if z < 17:
                    from_low, from_high = recv_x[step, 0, group], recv_x[step, 1, group]
                    if j:
                        from_low = pltpu.roll(from_low, LANES - 42 * j, 1)
                        from_high = pltpu.roll(from_high, LANES - 42 * j, 1)
                    near = cells[z, :, 0:LANES] + jnp.where(lane < 32, from_low, 0.0)
                    far = cells[z, :, LANES:WIDE] + jnp.where(
                        lane < 32,
                        from_high,
                        jnp.where(
                            ends,
                            from_low,
                            jnp.where(ends_high, pltpu.roll(from_high, 4, 1), 0.0),
                        ),
                    )
                    full = jnp.concatenate([near, far], axis=1)
                    row = rows_of((8, WIDE))
                    mean = full / jnp.maximum(full[3:4], 1.0)
                    rounded = mean.astype(BF16).astype(F32)
                    entry = jnp.where(row < 4, rounded, mean - rounded)
                    entry = jnp.where(row == 3, full[7:8], jnp.where(row == 7, 0.0, entry))
                else:
                    entry = jnp.zeros((8, WIDE), F32)
                if z % 2 == 0:
                    pending = entry
                else:
                    pair = jnp.concatenate([pending, entry], axis=0).astype(BF16)
                    results[8 * (z - 1) : 8 * (z + 1), :] = pair[:, 0:COLUMNS]

    tables = [table_ref[c] for c in range(3)]

    def gather_collide(step, here):
        gathered = jnp.dot(results[...], onehots[step, :, here], preferred_element_type=F32)
        return collide(moving[:, here], lays[step, :, here], gathered, tables)

    solvent_chunks = solvent // CHUNK
    totals[...] = jnp.zeros_like(totals)
    place(0, 0, solvent_chunks)
    place_beads(0)

    def first_deposit(i, carry):
        here = pl.ds(pl.multiple_of(i * CHUNK, CHUNK), CHUNK)
        deposit(0, here, moving[:, here])
        return carry

    lax.fori_loop(0, chunks, first_deposit, 0)

    def between_first(number):
        if number == 0:
            place(1, 0, 4)
        elif number == 1:
            place(1, 4, 4)
        else:
            place(1, 8, solvent_chunks - 8)
            place_beads(1)

    exchange(0, between_first)

    totals[...] = jnp.zeros_like(totals)

    def turn(i, carry):
        here = pl.ds(pl.multiple_of(i * CHUNK, CHUNK), CHUNK)
        moved = gather_collide(0, here)
        moving[:, here] = moved
        deposit(1, here, moved)
        return carry

    lax.fori_loop(0, chunks, turn, 0)

    tiles = solvent // LANES

    def between_second(number):
        if number == 0:
            row8 = rows_of((8, LANES))

            def body(i, carry):
                parts = []
                for k in range(2):
                    here = pl.ds(pl.multiple_of((2 * i + k) * LANES, LANES), LANES)
                    now = moving[:, here]
                    rounded = now.astype(BF16).astype(F32)
                    entry = jnp.where(row8 < 4, rounded, now - rounded)
                    entry = jnp.where(row8 == 3, cols[1, :, here].astype(F32), entry)
                    parts.append(jnp.where(row8 == 7, lays[1, :, here].astype(F32), entry))
                leave_table[pl.ds(pl.multiple_of(16 * i, 16), 16), :] = jnp.concatenate(
                    parts, axis=0
                ).astype(BF16)
                return carry

            lax.fori_loop(0, tiles // 2, body, 0)
        elif number == 1:

            def body(d, carry):
                for side in range(2):
                    index = jnp.maximum(leave_ref[d, side : side + 1, :], 0)
                    offset = (index & (LANES - 1)).astype(F32)
                    rest = (offset - rows_of((16, CAP)).astype(F32)).astype(BF16)
                    one, zero = jnp.ones((16, CAP), BF16), jnp.zeros((16, CAP), BF16)
                    spot = jnp.concatenate(
                        [jnp.where(rest == float(16 * j), one, zero) for j in range(8)], axis=0
                    )
                    found = jnp.dot(leave_table[...], spot, preferred_element_type=F32)
                    tile = lax.shift_right_logical(index, 7)
                    chosen = found[0:8]
                    for i in range(1, tiles):
                        chosen = jnp.where(tile == i, found[8 * i : 8 * i + 8], chosen)
                    leave_moving[d, side] = chosen + pltpu.roll(chosen, 4, 0)
                    leave_layer[d, side] = chosen[7:8].astype(I32)
                    leave_onehot[d, side] = one_hot(chosen[3:4].astype(I32))
                return carry

            lax.fori_loop(0, 3, body, 0)

    exchange(1, between_second)

    slot = lanes_of((8, CAP))
    travels = []
    for d in range(3):
        for side in range(2):
            gathered = jnp.dot(
                results[...], leave_onehot[d, side], preferred_element_type=F32
            )
            moved = collide(leave_moving[d, side], leave_layer[d, side], gathered, tables)
            leave_send[d, side] = jnp.where(slot < count_ref[side, d], moved, 0.0)
            travel = remote(
                leave_send.at[d, side], leave_recv.at[d, 1 - side], 12 + 2 * d + side, d, side
            )
            travel.start()
            travels.append(travel)

    def finish(i, carry):
        here = pl.ds(pl.multiple_of(i * CHUNK, CHUNK), CHUNK)
        velocity_out[:, here] = gather_collide(1, here)[0:3]
        return carry

    lax.fori_loop(0, solvent_chunks, finish, 0)
    bead_out[...] = gather_collide(1, pl.ds(solvent, beads))[0:3]

    for travel in travels:
        travel.wait()
    for d in range(3):
        for side in range(2):
            arrivals_out[d, :, side, :] = leave_recv[d, side, 0:3, :]


def per_device(
    velocity, position, bead_velocity, bead_mass, bead_position, grid_shift, rot_axis,
    leave_count, leave_index,
):
    solvent, beads = velocity.shape[1], bead_velocity.shape[1]
    count = solvent + beads
    vmem = pl.BlockSpec(memory_space=pltpu.VMEM)
    smem = pl.BlockSpec(memory_space=pltpu.SMEM)
    velocity_out, bead_out, arrivals = pl.pallas_call(
        kernel,
        out_shape=(
            jax.ShapeDtypeStruct((3, solvent), F32),
            jax.ShapeDtypeStruct((3, beads), F32),
            jax.ShapeDtypeStruct((3, 3, 2, CAP), F32),
        ),
        in_specs=[smem, smem] + [vmem] * 8,
        out_specs=(vmem, vmem, vmem),
        scratch_shapes=[
            pltpu.VMEM((8, count), F32),
            pltpu.VMEM((1, count), F32),
            pltpu.VMEM((2, 1, count), I32),
            pltpu.VMEM((2, 1, count), I32),
            pltpu.VMEM((2, COLUMNS, count), BF16),
            pltpu.VMEM((8 * LAYERS, COLUMNS), F32),
            pltpu.VMEM((LAYERS, 8, WIDE), F32),
            pltpu.VMEM((8 * LAYERS, COLUMNS), BF16),
            pltpu.VMEM((2, 2, 8, LANES), F32),
            pltpu.VMEM((2, 2, 6, 8, LANES), F32),
            pltpu.VMEM((2, 2, 8, WIDE), F32),
            pltpu.VMEM((2, 2, 2, 8, LANES), F32),
            pltpu.VMEM((2, 2, 6, 8, LANES), F32),
            pltpu.VMEM((8 * solvent // LANES, LANES), BF16),
            pltpu.VMEM((3, 2, 8, CAP), F32),
            pltpu.VMEM((3, 2, 1, CAP), I32),
            pltpu.VMEM((3, 2, COLUMNS, CAP), BF16),
            pltpu.VMEM((3, 2, 8, CAP), F32),
            pltpu.VMEM((3, 2, 8, CAP), F32),
            pltpu.SemaphoreType.DMA((18,)),
            pltpu.SemaphoreType.DMA((18,)),
        ],
        compiler_params=pltpu.CompilerParams(
            collective_id=0, has_side_effects=True, vmem_limit_bytes=40 * 1024 * 1024
        ),
        cost_estimate=pl.CostEstimate(flops=10**9, bytes_accessed=10**6, transcendentals=0),
        name="collisions",
    )(
        grid_shift,
        leave_count.reshape(3, 2).T,
        velocity,
        jnp.transpose(position, (1, 0, 2)),
        bead_velocity,
        bead_mass.reshape(1, beads),
        jnp.transpose(bead_position, (1, 0, 2)),
        jnp.swapaxes(rot_axis, 2, 3),
        leave_index,
        jnp.asarray(rotation_table()),
    )
    return velocity_out, bead_out, jnp.transpose(arrivals, (0, 2, 1, 3))


def solution(mesh):
    return jax.shard_map(
        per_device,
        mesh=mesh,
        in_specs=(
            P(None, ("gx", "gy", "gz")),
            P(None, None, ("gx", "gy", "gz")),
            P(None, ("gx", "gy", "gz")),
            P(("gx", "gy", "gz")),
            P(None, None, ("gx", "gy", "gz")),
            P(),
            P(None, "gx", "gy", "gz"),
            P(None, None, ("gx", "gy", "gz")),
            P(None, None, ("gx", "gy", "gz")),
        ),
        out_specs=(
            P(None, ("gx", "gy", "gz")),
            P(None, ("gx", "gy", "gz")),
            P(None, None, None, ("gx", "gy", "gz")),
        ),
        check_vma=False,
    )
```

```python
import math

import jax
import jax.numpy as jnp
import numpy as np
from jax import lax
from jax.experimental import pallas as pl
from jax.experimental.pallas import tpu as pltpu
from jax.sharding import PartitionSpec as P

STEPS = 2
AXES = 64
CAP = 256
COSINE = math.cos(130.0 * math.pi / 180.0)
SINE = math.sin(130.0 * math.pi / 180.0)
GOLDEN = math.pi * (3.0 - math.sqrt(5.0))

LANES = 128
CHUNK = 1024
COLUMNS = 176
LAYERS = 18
WIDE = 256
MESH = pl.DeviceIdType.MESH
F32 = jnp.float32
BF16 = jnp.bfloat16
I32 = jnp.int32


def rotation_table():
    ordinal = np.arange(AXES) + 0.5
    height = 1.0 - 2.0 * ordinal / AXES
    radius = np.sqrt(1.0 - height * height)
    n = np.stack([radius * np.cos(ordinal * GOLDEN), radius * np.sin(ordinal * GOLDEN), height])
    zero = np.zeros(AXES)
    skew = np.array([[zero, -n[2], n[1]], [n[2], zero, -n[0]], [-n[1], n[0], zero]])
    matrix = COSINE * np.eye(3)[:, :, None] + SINE * skew + (1.0 - COSINE) * n[:, None] * n[None]
    table = np.zeros((3, 8, LANES), np.float32)
    for c in range(3):
        table[c, 0:3, :AXES] = matrix[:, c]
        table[c, 4:7, :AXES] = matrix[:, c]
    return table


OFFSETS = [
    (dx, dy, dz)
    for dx in (-1, 0, 1)
    for dy in (-1, 0, 1)
    for dz in (-1, 0, 1)
    if (dx, dy, dz) != (0, 0, 0)
]
EDGES = [(dx, dy) for dx in (-1, 0, 1) for dy in (-1, 1)]


def moved_edge(edge, place):
    dx, dy = edge
    target = {1: 0, -1: 5}[dy] + (4 if dx == 1 else 0)
    source = {1: 5, -1: 0}[dy] + (4 if dx == -1 else 0)
    if dx == 0:
        chosen = (place >= target) & (place < target + 5)
    else:
        chosen = place == target
    return (target - source) % LANES, chosen


def rows_of(shape):
    return lax.broadcasted_iota(I32, shape, 0)


def lanes_of(shape):
    return lax.broadcasted_iota(I32, shape, 1)


def lanes_from(tile, source):
    return jnp.take_along_axis(tile, source & (LANES - 1), axis=1)


def cell_rows(coords, shift_ref, step):
    layer = []
    for d in range(3):
        shift = shift_ref[step, d]
        offset = jnp.where(shift > 0, 1, 0)
        layer.append(lax.shift_right_arithmetic(coords[d] - shift, 4) + offset)
    return column_of(layer[0], layer[1]), layer[2]


def column_of(first, second):
    inner = first * 32 + second
    return jnp.where(second == 32, first + 160, jnp.where(second == 0, first + 165, inner))


def one_hot(column):
    n = column.shape[1]
    rest = column.astype(F32) - rows_of((16, n)).astype(F32)
    rest = rest.astype(BF16)
    one, zero = jnp.ones((16, n), BF16), jnp.zeros((16, n), BF16)
    return jnp.concatenate(
        [jnp.where(rest == float(16 * j), one, zero) for j in range(COLUMNS // 16)], axis=0
    )


def deposit_rows(moving, weight, layer):
    n = moving.shape[1]
    row8 = rows_of((8, n))
    summand = moving * weight
    high = summand.astype(BF16).astype(F32)
    parts = jnp.where(row8 < 4, high, summand - high)
    parts = jnp.concatenate([parts, parts], axis=0).astype(BF16)
    half = lax.shift_right_logical(rows_of((16, n)), 3)
    rest = (layer - half).astype(F32).astype(BF16)
    zero = jnp.zeros((16, n), BF16)
    return jnp.concatenate(
        [jnp.where(rest == float(2 * j), parts, zero) for j in range(LAYERS // 2)], axis=0
    )


def collide(moving, layer, gathered, tables):
    n = moving.shape[1]
    chosen = gathered[0:8]
    for z in range(1, 17):
        chosen = jnp.where(layer == z, gathered[8 * z : 8 * z + 8], chosen)
    mean = chosen + pltpu.roll(chosen, 4, 0)
    axis = jnp.broadcast_to(mean[3:4], (8, n)).astype(I32)
    relative = moving - mean
    result = mean
    for c in range(3):
        columns = jnp.concatenate(
            [
                jnp.take_along_axis(tables[c], axis[:, i : i + LANES], axis=1)
                for i in range(0, n, LANES)
            ],
            axis=1,
        )
        result = result + columns * relative[c : c + 1]
    row8 = rows_of((8, n))
    return jnp.where((row8 & 3) == 3, 1.0, result)


def kernel(
    shift_hbm, count_hbm, velocity_hbm, position_hbm, bead_velocity_hbm, bead_mass_hbm,
    bead_position_hbm, rot_hbm, leave_hbm, table_hbm,
    velocity_out, bead_out, arrivals_out,
    shift_ref, count_ref, velocity_ref, position_ref, bead_velocity_ref, bead_mass_ref,
    bead_position_ref, rot_ref, leave_ref, table_ref, load_sem,
    moving, weight, cols, lays, onehots, totals, cells, results,
    send_z, send_y, send_x, recv_edge, recv_line, recv_z, recv_y, recv_x,
    leave_table, leave_moving, leave_layer, leave_onehot, leave_send, leave_recv,
    send_sem, recv_sem,
):
    solvent = velocity_ref.shape[1]
    beads = bead_velocity_ref.shape[1]
    count = solvent + beads
    chunks = count // CHUNK

    names = ("gx", "gy", "gz")

    def device_at(offset):
        where = {}
        for name, step_by in zip(names, offset):
            if step_by:
                size, me = lax.axis_size(name), lax.axis_index(name)
                where[name] = lax.rem(me + size + step_by, size)
        return where

    barrier = pltpu.get_barrier_semaphore()
    for offset in OFFSETS:
        pl.semaphore_signal(barrier, inc=1, device_id=device_at(offset), device_id_type=MESH)

    loads = [
        pltpu.make_async_copy(src, dst, load_sem.at[i])
        for i, (src, dst) in enumerate(
            (
                (shift_hbm, shift_ref),
                (position_hbm, position_ref),
                (bead_position_hbm, bead_position_ref),
                (velocity_hbm, velocity_ref),
                (bead_velocity_hbm, bead_velocity_ref),
                (bead_mass_hbm, bead_mass_ref),
                (rot_hbm, rot_ref),
                (leave_hbm, leave_ref),
                (count_hbm, count_ref),
                (table_hbm, table_ref),
            )
        )
    ]
    for copy in loads:
        copy.start()
    for copy in loads:
        copy.wait()

    def remote(src, dst, number, offset):
        return pltpu.make_async_remote_copy(
            src_ref=src,
            dst_ref=dst,
            send_sem=send_sem.at[number],
            recv_sem=recv_sem.at[number],
            device_id=device_at(offset),
            device_id_type=MESH,
        )

    def load(velocity, where, length):
        moving[0:3, pl.ds(where, length)] = velocity
        moving[3:4, pl.ds(where, length)] = jnp.ones((1, length), F32)
        moving[4:7, pl.ds(where, length)] = velocity
        moving[7:8, pl.ds(where, length)] = jnp.ones((1, length), F32)

    load(velocity_ref[...], 0, solvent)
    load(bead_velocity_ref[...], solvent, beads)
    weight[:, 0:solvent] = jnp.ones((1, solvent), F32)
    weight[:, solvent:count] = bead_mass_ref[...]

    def place(step, first, number):
        def body(i, carry):
            here = pl.ds(pl.multiple_of(i * CHUNK, CHUNK), CHUNK)
            coords = [position_ref[d, step : step + 1, here] for d in range(3)]
            column, layer = cell_rows(coords, shift_ref, step)
            cols[step, :, here] = column
            lays[step, :, here] = layer
            onehots[step, :, here] = one_hot(column)
            return carry

        lax.fori_loop(first, first + number, body, 0)

    def place_beads(step):
        here = pl.ds(solvent, beads)
        coords = [bead_position_ref[d, step : step + 1, :] for d in range(3)]
        column, layer = cell_rows(coords, shift_ref, step)
        cols[step, :, here] = column
        lays[step, :, here] = layer
        onehots[step, :, here] = one_hot(column)

    def deposit(step, here, moved):
        rows = deposit_rows(moved, weight[:, here], lays[step, :, here])
        totals[...] += lax.dot_general(
            rows, onehots[step, :, here], (((1,), (1,)), ((), ())), preferred_element_type=F32
        )

    lane = lanes_of((8, LANES))

    def own_axes(step):
        offset = [jnp.where(shift_ref[step, d] > 0, 1, 0) for d in range(3)]
        local = rows_of((LANES, WIDE))
        target = column_of(
            lax.shift_right_logical(local, 5) + offset[0], (local & 31) + offset[1]
        )
        spread = jnp.where(lanes_of((LANES, WIDE)) == target, 1.0, 0.0).astype(BF16)
        held = jnp.concatenate([rot_ref[step, x] for x in range(4)], axis=1)
        by_layer = jnp.dot(
            held.astype(F32).astype(BF16), spread, preferred_element_type=F32
        )
        above = jnp.concatenate([jnp.zeros((1, WIDE), F32), by_layer], axis=0)
        below = jnp.concatenate([by_layer, jnp.zeros((1, WIDE), F32)], axis=0)
        return jnp.where(offset[2] > 0, above, below)

    def exchange(step, between):
        axes = own_axes(step)
        row8w = rows_of((8, WIDE))
        row8 = rows_of((8, LANES))
        cells[:, :, COLUMNS:WIDE] = jnp.zeros((LAYERS, 8, WIDE - COLUMNS), F32)

        def settle(z):
            part = totals[8 * z : 8 * z + 8, :]
            cells[z, :, 0:COLUMNS] = part + pltpu.roll(part, 4, 0)
            cells[z] = jnp.where(row8w == 7, axes[z : z + 1], cells[z])

        settle(0)
        settle(16)
        for side in range(2):
            near, far = cells[16 * side, :, 0:LANES], cells[16 * side, :, LANES:WIDE]
            edge = lanes_from(far, lane + 32 - 10 * row8)
            edge = jnp.where((lane >= 10 * row8) & (lane < 10 * row8 + 10), edge, 0.0)
            send_z[step, side, 2:3] = jnp.sum(edge, axis=0, keepdims=True)
            for at, tile in ((0, near), (3, far)):
                line = lanes_from(tile, lane & 31)
                line = jnp.where(lax.shift_right_logical(lane, 5) == (row8 & 3), line, 0.0)
                for half in range(2):
                    send_z[step, side, at + half : at + half + 1] = jnp.sum(
                        line[4 * half : 4 * half + 4], axis=0, keepdims=True
                    )
            send_z[step, side, 5:9] = near[0:4]
            send_z[step, side, 9:10] = near[7:8]

        if step == 0:
            pl.semaphore_wait(barrier, len(OFFSETS))

        travels = {}

        def send(src, dst, offset):
            travel = remote(src, dst, len(OFFSETS) * step + OFFSETS.index(offset), offset)
            travel.start()
            travels[offset] = travel

        for side in range(2):
            dz = 2 * side - 1
            for dx in (-1, 0, 1):
                for dy in (-1, 1):
                    back = EDGES.index((-dx, -dy))
                    send(
                        send_z.at[step, side, pl.ds(2, 1)],
                        recv_edge.at[step, 1 - side, back],
                        (dx, dy, dz),
                    )
            for dx in (-1, 1):
                send(
                    send_z.at[step, side, pl.ds(1 + dx, 3)],
                    recv_line.at[step, 1 - side, (1 - dx) // 2],
                    (dx, 0, dz),
                )
            send(send_z.at[step, side, pl.ds(2, 8)], recv_z.at[step, 1 - side], (0, 0, dz))

        for z in range(1, 16):
            settle(z)
        for group in range(2):
            packed = jnp.zeros((8, LANES), F32)
            for j in range(9):
                z = 9 * group + j
                if z < 17:
                    turned = pltpu.roll(cells[z, :, LANES:WIDE], (12 * j - 32) % LANES, 1)
                    packed = jnp.where((lane >= 12 * j) & (lane < 12 * j + 10), turned, packed)
            send_y[step, group] = packed
        for dx in (-1, 0, 1):
            for dy in (-1, 1):
                back = EDGES.index((-dx, -dy))
                send(send_y.at[step], recv_y.at[step, back], (dx, dy, 0))

        for group in range(6):
            packed_low = jnp.zeros((8, LANES), F32)
            packed_high = jnp.zeros((8, LANES), F32)
            for j in range(3):
                z = 3 * group + j
                if z < 17:
                    near, far = cells[z, :, 0:LANES], cells[z, :, LANES:WIDE]
                    face_low = jnp.where(lane < 32, near, far)
                    face_high = jnp.where(lane < 32, far, pltpu.roll(far, LANES - 4, 1))
                    if j:
                        face_low = pltpu.roll(face_low, 42 * j, 1)
                        face_high = pltpu.roll(face_high, 42 * j, 1)
                    inside = (lane >= 42 * j) & (lane < 42 * j + 38)
                    packed_low = jnp.where(inside, face_low, packed_low)
                    packed_high = jnp.where(inside, face_high, packed_high)
            send_x[step, 0, group] = packed_low
            send_x[step, 1, group] = packed_high
        send(send_x.at[step, 0], recv_x.at[step, 1], (-1, 0, 0))
        send(send_x.at[step, 1], recv_x.at[step, 0], (1, 0, 0))

        between()

        for offset, travel in travels.items():
            if offset[2] == 0:
                travel.wait()
        place12 = lax.rem(lane, 12)
        both_groups = []
        for group in range(2):
            both = jnp.zeros((8, LANES), F32)
            for k, edge in enumerate(EDGES):
                turn_by, chosen = moved_edge(edge, place12)
                both += jnp.where(chosen, pltpu.roll(recv_y[step, k, group], turn_by, 1), 0.0)
            both_groups.append(both)
        ends = (lane == 32) | (lane == 37)
        ends_high = (lane == 36) | (lane == 41)
        for group in range(6):
            for j in range(3):
                z = 3 * group + j
                if z < 17:
                    from_low, from_high = recv_x[step, 0, group], recv_x[step, 1, group]
                    if j:
                        from_low = pltpu.roll(from_low, LANES - 42 * j, 1)
                        from_high = pltpu.roll(from_high, LANES - 42 * j, 1)
                    shift_by = (32 - 12 * (z % 9)) % LANES
                    from_second = pltpu.roll(both_groups[z // 9], shift_by, 1)
                    cells[z, :, 0:LANES] += jnp.where(lane < 32, from_low, 0.0)
                    cells[z, :, LANES:WIDE] += (
                        jnp.where(
                            lane < 32,
                            from_high,
                            jnp.where(
                                ends,
                                from_low,
                                jnp.where(ends_high, pltpu.roll(from_high, 4, 1), 0.0),
                            ),
                        )
                        + jnp.where((lane >= 32) & (lane < 42), from_second, 0.0)
                    )

        def entry_of(z):
            if z == 17:
                return jnp.zeros((8, WIDE), F32)
            full = cells[z]
            full = jnp.where((row8w >= 4) & (row8w < 7), pltpu.roll(full, 4, 0), full)
            mean = full / jnp.maximum(full[3:4], 1.0)
            rounded = mean.astype(BF16).astype(F32)
            entry = jnp.where(row8w < 4, rounded, mean - rounded)
            return jnp.where(row8w == 3, full[7:8], jnp.where(row8w == 7, 0.0, entry))

        def finish_pair(z):
            pair = jnp.concatenate([entry_of(z), entry_of(z + 1)], axis=0).astype(BF16)
            results[8 * z : 8 * z + 16, :] = pair[:, 0:COLUMNS]

        for z in range(2, 16, 2):
            finish_pair(z)

        for offset, travel in travels.items():
            if offset[2] != 0:
                travel.wait()
        for side in range(2):
            face = recv_z[step, side]
            lane1 = lanes_of((1, LANES))
            place10 = lax.rem(lane1, 10)
            edge = face[0:1]
            for k, offset in enumerate(EDGES):
                turn_by, chosen = moved_edge(offset, place10)
                edge += jnp.where(chosen, pltpu.roll(recv_edge[step, side, k], turn_by, 1), 0.0)
            low, high = recv_line[step, side, 0], recv_line[step, side, 1]
            at_low, at_high = (place10 == 0) | (place10 == 5), (place10 == 4) | (place10 == 9)
            edge += jnp.where(at_low, pltpu.roll(low[0:1], LANES - 4, 1), 0.0)
            edge += jnp.where(at_high, pltpu.roll(high[2:3], 4, 1), 0.0)
            edge = lanes_from(jnp.broadcast_to(edge, (8, LANES)), lane - 32 + 10 * row8)
            lines = []
            for line in (low[1:3], face[1:3] + high[0:2]):
                wide = jnp.where(row8 < 4, line[0:1], line[1:2])
                lines.append(lanes_from(wide, (lane & 31) + 32 * (row8 & 3)))
            rest = jnp.where(row8 == 7, face, pltpu.roll(face, 5, 0))
            near = rest + jnp.where(lane < 32, lines[0], 0.0)
            far = jnp.where(lane < 32, lines[1], jnp.where(lane < 42, edge, 0.0))
            cells[16 * side, :, 0:LANES] += near
            cells[16 * side, :, LANES:WIDE] += far
            finish_pair(16 * side)

    tables = [table_ref[c] for c in range(3)]

    def gather_collide(step, here):
        gathered = jnp.dot(results[...], onehots[step, :, here], preferred_element_type=F32)
        return collide(moving[:, here], lays[step, :, here], gathered, tables)

    solvent_chunks = solvent // CHUNK
    totals[...] = jnp.zeros_like(totals)
    place(0, 0, solvent_chunks)
    place_beads(0)

    def first_deposit(i, carry):
        here = pl.ds(pl.multiple_of(i * CHUNK, CHUNK), CHUNK)
        deposit(0, here, moving[:, here])
        return carry

    lax.fori_loop(0, chunks, first_deposit, 0)

    def between_first():
        place(1, 0, solvent_chunks)
        place_beads(1)

    exchange(0, between_first)

    totals[...] = jnp.zeros_like(totals)

    def turn(i, carry):
        here = pl.ds(pl.multiple_of(i * CHUNK, CHUNK), CHUNK)
        moved = gather_collide(0, here)
        moving[:, here] = moved
        deposit(1, here, moved)
        return carry

    lax.fori_loop(0, chunks, turn, 0)

    tiles = solvent // LANES

    def between_second():
        row8 = rows_of((8, LANES))

        def fill(i, carry):
            parts = []
            for k in range(2):
                here = pl.ds(pl.multiple_of((2 * i + k) * LANES, LANES), LANES)
                now = moving[:, here]
                rounded = now.astype(BF16).astype(F32)
                entry = jnp.where(row8 < 4, rounded, now - rounded)
                entry = jnp.where(row8 == 3, cols[1, :, here].astype(F32), entry)
                parts.append(jnp.where(row8 == 7, lays[1, :, here].astype(F32), entry))
            leave_table[pl.ds(pl.multiple_of(16 * i, 16), 16), :] = jnp.concatenate(
                parts, axis=0
            ).astype(BF16)
            return carry

        lax.fori_loop(0, tiles // 2, fill, 0)

        def pick(d, carry):
            for side in range(2):
                index = jnp.maximum(leave_ref[d, side : side + 1, :], 0)
                offset = (index & (LANES - 1)).astype(F32)
                rest = (offset - rows_of((16, CAP)).astype(F32)).astype(BF16)
                one, zero = jnp.ones((16, CAP), BF16), jnp.zeros((16, CAP), BF16)
                spot = jnp.concatenate(
                    [jnp.where(rest == float(16 * j), one, zero) for j in range(8)], axis=0
                )
                found = jnp.dot(leave_table[...], spot, preferred_element_type=F32)
                tile = lax.shift_right_logical(index, 7)
                chosen = found[0:8]
                for i in range(1, tiles):
                    chosen = jnp.where(tile == i, found[8 * i : 8 * i + 8], chosen)
                leave_moving[d, side] = chosen + pltpu.roll(chosen, 4, 0)
                leave_layer[d, side] = chosen[7:8].astype(I32)
                leave_onehot[d, side] = one_hot(chosen[3:4].astype(I32))
            return carry

        lax.fori_loop(0, 3, pick, 0)

    exchange(1, between_second)

    slot = lanes_of((8, CAP))
    travels = []
    for d in range(3):
        for side in range(2):
            gathered = jnp.dot(
                results[...], leave_onehot[d, side], preferred_element_type=F32
            )
            moved = collide(leave_moving[d, side], leave_layer[d, side], gathered, tables)
            leave_send[d, side] = jnp.where(slot < count_ref[side, d], moved, 0.0)
            offset = tuple(2 * side - 1 if axis == d else 0 for axis in range(3))
            travel = remote(
                leave_send.at[d, side],
                leave_recv.at[d, 1 - side],
                2 * len(OFFSETS) + 2 * d + side,
                offset,
            )
            travel.start()
            travels.append(travel)

    def finish(i, carry):
        here = pl.ds(pl.multiple_of(i * CHUNK, CHUNK), CHUNK)
        velocity_out[:, here] = gather_collide(1, here)[0:3]
        return carry

    lax.fori_loop(0, solvent_chunks, finish, 0)
    bead_out[...] = gather_collide(1, pl.ds(solvent, beads))[0:3]

    for travel in travels:
        travel.wait()
    for d in range(3):
        for side in range(2):
            arrivals_out[d, :, side, :] = leave_recv[d, side, 0:3, :]


def per_device(
    velocity, position, bead_velocity, bead_mass, bead_position, grid_shift, rot_axis,
    leave_count, leave_index,
):
    solvent, beads = velocity.shape[1], bead_velocity.shape[1]
    count = solvent + beads
    vmem = pl.BlockSpec(memory_space=pltpu.VMEM)
    velocity_out, bead_out, arrivals = pl.pallas_call(
        kernel,
        out_shape=(
            jax.ShapeDtypeStruct((3, solvent), F32),
            jax.ShapeDtypeStruct((3, beads), F32),
            jax.ShapeDtypeStruct((3, 3, 2, CAP), F32),
        ),
        in_specs=[pl.BlockSpec(memory_space=pltpu.HBM)] * 10,
        out_specs=(vmem, vmem, vmem),
        scratch_shapes=[
            pltpu.SMEM((2, 3), I32),
            pltpu.SMEM((2, 3), I32),
            pltpu.VMEM((3, solvent), F32),
            pltpu.VMEM((3, 2, solvent), I32),
            pltpu.VMEM((3, beads), F32),
            pltpu.VMEM((1, beads), F32),
            pltpu.VMEM((3, 2, beads), I32),
            pltpu.VMEM((2, 4, 16, 32), I32),
            pltpu.VMEM((3, 2, CAP), I32),
            pltpu.VMEM((3, 8, LANES), F32),
            pltpu.SemaphoreType.DMA((10,)),
            pltpu.VMEM((8, count), F32),
            pltpu.VMEM((1, count), F32),
            pltpu.VMEM((2, 1, count), I32),
            pltpu.VMEM((2, 1, count), I32),
            pltpu.VMEM((2, COLUMNS, count), BF16),
            pltpu.VMEM((8 * LAYERS, COLUMNS), F32),
            pltpu.VMEM((LAYERS, 8, WIDE), F32),
            pltpu.VMEM((8 * LAYERS, COLUMNS), BF16),
            pltpu.VMEM((2, 2, 16, LANES), F32),
            pltpu.VMEM((2, 2, 8, LANES), F32),
            pltpu.VMEM((2, 2, 6, 8, LANES), F32),
            pltpu.VMEM((2, 2, 6, 1, LANES), F32),
            pltpu.VMEM((2, 2, 2, 3, LANES), F32),
            pltpu.VMEM((2, 2, 8, LANES), F32),
            pltpu.VMEM((2, 6, 2, 8, LANES), F32),
            pltpu.VMEM((2, 2, 6, 8, LANES), F32),
            pltpu.VMEM((8 * solvent // LANES, LANES), BF16),
            pltpu.VMEM((3, 2, 8, CAP), F32),
            pltpu.VMEM((3, 2, 1, CAP), I32),
            pltpu.VMEM((3, 2, COLUMNS, CAP), BF16),
            pltpu.VMEM((3, 2, 8, CAP), F32),
            pltpu.VMEM((3, 2, 8, CAP), F32),
            pltpu.SemaphoreType.DMA((2 * len(OFFSETS) + 6,)),
            pltpu.SemaphoreType.DMA((2 * len(OFFSETS) + 6,)),
        ],
        compiler_params=pltpu.CompilerParams(
            collective_id=0, has_side_effects=True, vmem_limit_bytes=64 * 1024 * 1024
        ),
        cost_estimate=pl.CostEstimate(flops=10**9, bytes_accessed=10**6, transcendentals=0),
        name="collisions",
    )(
        grid_shift,
        leave_count.reshape(3, 2).T,
        velocity,
        jnp.transpose(position, (1, 0, 2)),
        bead_velocity,
        bead_mass.reshape(1, beads),
        jnp.transpose(bead_position, (1, 0, 2)),
        jnp.swapaxes(rot_axis, 2, 3),
        leave_index,
        jnp.asarray(rotation_table()),
    )
    return velocity_out, bead_out, jnp.transpose(arrivals, (0, 2, 1, 3))


def solution(mesh):
    return jax.shard_map(
        per_device,
        mesh=mesh,
        in_specs=(
            P(None, ("gx", "gy", "gz")),
            P(None, None, ("gx", "gy", "gz")),
            P(None, ("gx", "gy", "gz")),
            P(("gx", "gy", "gz")),
            P(None, None, ("gx", "gy", "gz")),
            P(),
            P(None, "gx", "gy", "gz"),
            P(None, None, ("gx", "gy", "gz")),
            P(None, None, ("gx", "gy", "gz")),
        ),
        out_specs=(
            P(None, ("gx", "gy", "gz")),
            P(None, ("gx", "gy", "gz")),
            P(None, None, None, ("gx", "gy", "gz")),
        ),
        check_vma=False,
    )
```

```python
import math

import jax
import jax.numpy as jnp
import numpy as np
from jax import lax
from jax.experimental import pallas as pl
from jax.experimental.pallas import tpu as pltpu
from jax.sharding import PartitionSpec as P

STEPS = 2
AXES = 64
CAP = 256
COSINE = math.cos(130.0 * math.pi / 180.0)
SINE = math.sin(130.0 * math.pi / 180.0)
GOLDEN = math.pi * (3.0 - math.sqrt(5.0))

LANES = 128
CHUNK = 1024
COLUMNS = 176
LAYERS = 18
WIDE = 256
MESH = pl.DeviceIdType.MESH
F32 = jnp.float32
BF16 = jnp.bfloat16
I32 = jnp.int32


def rotation_table():
    ordinal = np.arange(AXES) + 0.5
    height = 1.0 - 2.0 * ordinal / AXES
    radius = np.sqrt(1.0 - height * height)
    n = np.stack([radius * np.cos(ordinal * GOLDEN), radius * np.sin(ordinal * GOLDEN), height])
    zero = np.zeros(AXES)
    skew = np.array([[zero, -n[2], n[1]], [n[2], zero, -n[0]], [-n[1], n[0], zero]])
    matrix = COSINE * np.eye(3)[:, :, None] + SINE * skew + (1.0 - COSINE) * n[:, None] * n[None]
    table = np.zeros((3, 8, LANES), np.float32)
    for c in range(3):
        table[c, 0:3, :AXES] = matrix[:, c]
        table[c, 4:7, :AXES] = matrix[:, c]
    return table


OFFSETS = [
    (dx, dy, dz)
    for dx in (-1, 0, 1)
    for dy in (-1, 0, 1)
    for dz in (-1, 0, 1)
    if (dx, dy, dz) != (0, 0, 0)
]
EDGES = [(dx, dy) for dx in (-1, 0, 1) for dy in (-1, 1)]


def moved_edge(edge, place):
    dx, dy = edge
    target = {1: 0, -1: 5}[dy] + (4 if dx == 1 else 0)
    source = {1: 5, -1: 0}[dy] + (4 if dx == -1 else 0)
    if dx == 0:
        chosen = (place >= target) & (place < target + 5)
    else:
        chosen = place == target
    return (target - source) % LANES, chosen


def rows_of(shape):
    return lax.broadcasted_iota(I32, shape, 0)


def lanes_of(shape):
    return lax.broadcasted_iota(I32, shape, 1)


def lanes_from(tile, source):
    return jnp.take_along_axis(tile, source & (LANES - 1), axis=1)


def cell_rows(coords, shift_ref, step):
    layer = []
    for d in range(3):
        shift = shift_ref[step, d]
        offset = jnp.where(shift > 0, 1, 0)
        layer.append(lax.shift_right_arithmetic(coords[d] - shift, 4) + offset)
    return column_of(layer[0], layer[1]), layer[2]


def column_of(first, second):
    inner = first * 32 + second
    return jnp.where(second == 32, first + 160, jnp.where(second == 0, first + 165, inner))


def one_hot(column):
    n = column.shape[1]
    rest = column.astype(F32) - rows_of((16, n)).astype(F32)
    rest = rest.astype(BF16)
    one, zero = jnp.ones((16, n), BF16), jnp.zeros((16, n), BF16)
    return jnp.concatenate(
        [jnp.where(rest == float(16 * j), one, zero) for j in range(COLUMNS // 16)], axis=0
    )


def deposit_rows(moving, weight, layer):
    n = moving.shape[1]
    row8 = rows_of((8, n))
    summand = moving * weight
    high = summand.astype(BF16).astype(F32)
    parts = jnp.where(row8 < 4, high, summand - high)
    parts = jnp.concatenate([parts, parts], axis=0).astype(BF16)
    half = lax.shift_right_logical(rows_of((16, n)), 3)
    rest = (layer - half).astype(F32).astype(BF16)
    zero = jnp.zeros((16, n), BF16)
    return jnp.concatenate(
        [jnp.where(rest == float(2 * j), parts, zero) for j in range(LAYERS // 2)], axis=0
    )


def collide(moving, layer, gathered, tables):
    n = moving.shape[1]
    chosen = gathered[0:8]
    for z in range(1, 17):
        chosen = jnp.where(layer == z, gathered[8 * z : 8 * z + 8], chosen)
    mean = chosen + pltpu.roll(chosen, 4, 0)
    axis = jnp.broadcast_to(mean[3:4], (8, n)).astype(I32)
    relative = moving - mean
    result = mean
    for c in range(3):
        columns = jnp.concatenate(
            [
                jnp.take_along_axis(tables[c], axis[:, i : i + LANES], axis=1)
                for i in range(0, n, LANES)
            ],
            axis=1,
        )
        result = result + columns * relative[c : c + 1]
    row8 = rows_of((8, n))
    return jnp.where((row8 & 3) == 3, 1.0, result)


def kernel(
    shift_hbm, count_hbm, velocity_hbm, position_hbm, bead_velocity_hbm, bead_mass_hbm,
    bead_position_hbm, rot_hbm, leave_hbm, table_hbm,
    velocity_out, bead_out, arrivals_out,
    shift_ref, count_ref, velocity_ref, position_ref, bead_velocity_ref, bead_mass_ref,
    bead_position_ref, rot_ref, leave_ref, table_ref, load_sem,
    moving, weight, cols, lays, onehots, totals, cells, results,
    send_z, send_y, send_x, recv_edge, recv_line, recv_z, recv_y, recv_x,
    leave_table, leave_moving, leave_layer, leave_onehot, leave_send, leave_recv,
    send_sem, recv_sem,
):
    solvent = velocity_ref.shape[1]
    beads = bead_velocity_ref.shape[1]
    count = solvent + beads
    chunks = count // CHUNK

    names = ("gx", "gy", "gz")

    def device_at(offset):
        where = {}
        for name, step_by in zip(names, offset):
            if step_by:
                size, me = lax.axis_size(name), lax.axis_index(name)
                where[name] = lax.rem(me + size + step_by, size)
        return where

    barrier = pltpu.get_barrier_semaphore()
    for offset in OFFSETS:
        pl.semaphore_signal(barrier, inc=1, device_id=device_at(offset), device_id_type=MESH)

    loads = [
        pltpu.make_async_copy(src, dst, load_sem.at[i])
        for i, (src, dst) in enumerate(
            (
                (shift_hbm, shift_ref),
                (position_hbm, position_ref),
                (bead_position_hbm, bead_position_ref),
                (velocity_hbm, velocity_ref),
                (bead_velocity_hbm, bead_velocity_ref),
                (bead_mass_hbm, bead_mass_ref),
                (rot_hbm, rot_ref),
                (leave_hbm, leave_ref),
                (count_hbm, count_ref),
                (table_hbm, table_ref),
            )
        )
    ]
    for copy in loads:
        copy.start()
    for copy in loads:
        copy.wait()

    def remote(src, dst, number, offset):
        return pltpu.make_async_remote_copy(
            src_ref=src,
            dst_ref=dst,
            send_sem=send_sem.at[number],
            recv_sem=recv_sem.at[number],
            device_id=device_at(offset),
            device_id_type=MESH,
        )

    def load(velocity, where, length):
        moving[0:3, pl.ds(where, length)] = velocity
        moving[3:4, pl.ds(where, length)] = jnp.ones((1, length), F32)
        moving[4:7, pl.ds(where, length)] = velocity
        moving[7:8, pl.ds(where, length)] = jnp.ones((1, length), F32)

    load(velocity_ref[...], 0, solvent)
    load(bead_velocity_ref[...], solvent, beads)
    weight[:, 0:solvent] = jnp.ones((1, solvent), F32)
    weight[:, solvent:count] = bead_mass_ref[...]

    def place(step, first, number):
        def body(i, carry):
            here = pl.ds(pl.multiple_of(i * CHUNK, CHUNK), CHUNK)
            coords = [position_ref[d, step : step + 1, here] for d in range(3)]
            column, layer = cell_rows(coords, shift_ref, step)
            cols[step, :, here] = column
            lays[step, :, here] = layer
            onehots[step, :, here] = one_hot(column)
            return carry

        lax.fori_loop(first, first + number, body, 0, unroll=number)

    def place_beads(step):
        here = pl.ds(solvent, beads)
        coords = [bead_position_ref[d, step : step + 1, :] for d in range(3)]
        column, layer = cell_rows(coords, shift_ref, step)
        cols[step, :, here] = column
        lays[step, :, here] = layer
        onehots[step, :, here] = one_hot(column)

    def deposit(step, here, moved):
        rows = deposit_rows(moved, weight[:, here], lays[step, :, here])
        totals[...] += lax.dot_general(
            rows, onehots[step, :, here], (((1,), (1,)), ((), ())), preferred_element_type=F32
        )

    lane = lanes_of((8, LANES))

    def own_axes(step):
        offset = [jnp.where(shift_ref[step, d] > 0, 1, 0) for d in range(3)]
        local = rows_of((LANES, WIDE))
        target = column_of(
            lax.shift_right_logical(local, 5) + offset[0], (local & 31) + offset[1]
        )
        spread = jnp.where(lanes_of((LANES, WIDE)) == target, 1.0, 0.0).astype(BF16)
        held = jnp.concatenate([rot_ref[step, x] for x in range(4)], axis=1)
        by_layer = jnp.dot(
            held.astype(F32).astype(BF16), spread, preferred_element_type=F32
        )
        above = jnp.concatenate([jnp.zeros((1, WIDE), F32), by_layer], axis=0)
        below = jnp.concatenate([by_layer, jnp.zeros((1, WIDE), F32)], axis=0)
        return jnp.where(offset[2] > 0, above, below)

    def exchange(step, between):
        axes = own_axes(step)
        row8w = rows_of((8, WIDE))
        row8 = rows_of((8, LANES))
        cells[:, :, COLUMNS:WIDE] = jnp.zeros((LAYERS, 8, WIDE - COLUMNS), F32)

        def settle(z):
            part = totals[8 * z : 8 * z + 8, :]
            cells[z, :, 0:COLUMNS] = part + pltpu.roll(part, 4, 0)
            cells[z] = jnp.where(row8w == 7, axes[z : z + 1], cells[z])

        settle(0)
        settle(16)
        for side in range(2):
            near, far = cells[16 * side, :, 0:LANES], cells[16 * side, :, LANES:WIDE]
            edge = lanes_from(far, lane + 32 - 10 * row8)
            edge = jnp.where((lane >= 10 * row8) & (lane < 10 * row8 + 10), edge, 0.0)
            send_z[step, side, 2:3] = jnp.sum(edge, axis=0, keepdims=True)
            for at, tile in ((0, near), (3, far)):
                line = lanes_from(tile, lane & 31)
                line = jnp.where(lax.shift_right_logical(lane, 5) == (row8 & 3), line, 0.0)
                for half in range(2):
                    send_z[step, side, at + half : at + half + 1] = jnp.sum(
                        line[4 * half : 4 * half + 4], axis=0, keepdims=True
                    )
            send_z[step, side, 5:9] = near[0:4]
            send_z[step, side, 9:10] = near[7:8]

        if step == 0:
            pl.semaphore_wait(barrier, len(OFFSETS))

        travels = {}

        def send(src, dst, offset):
            travel = remote(src, dst, len(OFFSETS) * step + OFFSETS.index(offset), offset)
            travel.start()
            travels[offset] = travel

        for side in range(2):
            dz = 2 * side - 1
            for dx in (-1, 0, 1):
                for dy in (-1, 1):
                    back = EDGES.index((-dx, -dy))
                    send(
                        send_z.at[step, side, pl.ds(2, 1)],
                        recv_edge.at[step, 1 - side, back],
                        (dx, dy, dz),
                    )
            for dx in (-1, 1):
                send(
                    send_z.at[step, side, pl.ds(1 + dx, 3)],
                    recv_line.at[step, 1 - side, (1 - dx) // 2],
                    (dx, 0, dz),
                )
            send(send_z.at[step, side, pl.ds(2, 8)], recv_z.at[step, 1 - side], (0, 0, dz))

        for z in range(1, 16):
            settle(z)
        for group in range(2):
            packed = jnp.zeros((8, LANES), F32)
            for j in range(9):
                z = 9 * group + j
                if z < 17:
                    turned = pltpu.roll(cells[z, :, LANES:WIDE], (12 * j - 32) % LANES, 1)
                    packed = jnp.where((lane >= 12 * j) & (lane < 12 * j + 10), turned, packed)
            send_y[step, group] = packed
        for dx in (-1, 0, 1):
            for dy in (-1, 1):
                back = EDGES.index((-dx, -dy))
                send(send_y.at[step], recv_y.at[step, back], (dx, dy, 0))

        for group in range(6):
            packed_low = jnp.zeros((8, LANES), F32)
            packed_high = jnp.zeros((8, LANES), F32)
            for j in range(3):
                z = 3 * group + j
                if z < 17:
                    near, far = cells[z, :, 0:LANES], cells[z, :, LANES:WIDE]
                    face_low = jnp.where(lane < 32, near, far)
                    face_high = jnp.where(lane < 32, far, pltpu.roll(far, LANES - 4, 1))
                    if j:
                        face_low = pltpu.roll(face_low, 42 * j, 1)
                        face_high = pltpu.roll(face_high, 42 * j, 1)
                    inside = (lane >= 42 * j) & (lane < 42 * j + 38)
                    packed_low = jnp.where(inside, face_low, packed_low)
                    packed_high = jnp.where(inside, face_high, packed_high)
            send_x[step, 0, group] = packed_low
            send_x[step, 1, group] = packed_high
        send(send_x.at[step, 0], recv_x.at[step, 1], (-1, 0, 0))
        send(send_x.at[step, 1], recv_x.at[step, 0], (1, 0, 0))

        between()

        for offset, travel in travels.items():
            if offset[2] == 0:
                travel.wait()
        place12 = lax.rem(lane, 12)
        both_groups = []
        for group in range(2):
            both = jnp.zeros((8, LANES), F32)
            for k, edge in enumerate(EDGES):
                turn_by, chosen = moved_edge(edge, place12)
                both += jnp.where(chosen, pltpu.roll(recv_y[step, k, group], turn_by, 1), 0.0)
            both_groups.append(both)
        ends = (lane == 32) | (lane == 37)
        ends_high = (lane == 36) | (lane == 41)
        for group in range(6):
            for j in range(3):
                z = 3 * group + j
                if z < 17:
                    from_low, from_high = recv_x[step, 0, group], recv_x[step, 1, group]
                    if j:
                        from_low = pltpu.roll(from_low, LANES - 42 * j, 1)
                        from_high = pltpu.roll(from_high, LANES - 42 * j, 1)
                    shift_by = (32 - 12 * (z % 9)) % LANES
                    from_second = pltpu.roll(both_groups[z // 9], shift_by, 1)
                    cells[z, :, 0:LANES] += jnp.where(lane < 32, from_low, 0.0)
                    cells[z, :, LANES:WIDE] += (
                        jnp.where(
                            lane < 32,
                            from_high,
                            jnp.where(
                                ends,
                                from_low,
                                jnp.where(ends_high, pltpu.roll(from_high, 4, 1), 0.0),
                            ),
                        )
                        + jnp.where((lane >= 32) & (lane < 42), from_second, 0.0)
                    )

        def entry_of(z):
            if z == 17:
                return jnp.zeros((8, WIDE), F32)
            full = cells[z]
            full = jnp.where((row8w >= 4) & (row8w < 7), pltpu.roll(full, 4, 0), full)
            mean = full / jnp.maximum(full[3:4], 1.0)
            rounded = mean.astype(BF16).astype(F32)
            entry = jnp.where(row8w < 4, rounded, mean - rounded)
            return jnp.where(row8w == 3, full[7:8], jnp.where(row8w == 7, 0.0, entry))

        def finish_pair(z):
            pair = jnp.concatenate([entry_of(z), entry_of(z + 1)], axis=0).astype(BF16)
            results[8 * z : 8 * z + 16, :] = pair[:, 0:COLUMNS]

        for z in range(2, 16, 2):
            finish_pair(z)

        for offset, travel in travels.items():
            if offset[2] != 0:
                travel.wait()
        for side in range(2):
            face = recv_z[step, side]
            lane1 = lanes_of((1, LANES))
            place10 = lax.rem(lane1, 10)
            edge = face[0:1]
            for k, offset in enumerate(EDGES):
                turn_by, chosen = moved_edge(offset, place10)
                edge += jnp.where(chosen, pltpu.roll(recv_edge[step, side, k], turn_by, 1), 0.0)
            low, high = recv_line[step, side, 0], recv_line[step, side, 1]
            at_low, at_high = (place10 == 0) | (place10 == 5), (place10 == 4) | (place10 == 9)
            edge += jnp.where(at_low, pltpu.roll(low[0:1], LANES - 4, 1), 0.0)
            edge += jnp.where(at_high, pltpu.roll(high[2:3], 4, 1), 0.0)
            edge = lanes_from(jnp.broadcast_to(edge, (8, LANES)), lane - 32 + 10 * row8)
            lines = []
            for line in (low[1:3], face[1:3] + high[0:2]):
                wide = jnp.where(row8 < 4, line[0:1], line[1:2])
                lines.append(lanes_from(wide, (lane & 31) + 32 * (row8 & 3)))
            rest = jnp.where(row8 == 7, face, pltpu.roll(face, 5, 0))
            near = rest + jnp.where(lane < 32, lines[0], 0.0)
            far = jnp.where(lane < 32, lines[1], jnp.where(lane < 42, edge, 0.0))
            cells[16 * side, :, 0:LANES] += near
            cells[16 * side, :, LANES:WIDE] += far
            finish_pair(16 * side)

    tables = [table_ref[c] for c in range(3)]

    def gather_collide(step, here):
        gathered = jnp.dot(results[...], onehots[step, :, here], preferred_element_type=F32)
        return collide(moving[:, here], lays[step, :, here], gathered, tables)

    solvent_chunks = solvent // CHUNK
    totals[...] = jnp.zeros_like(totals)
    place(0, 0, solvent_chunks)
    place_beads(0)

    def first_deposit(i, carry):
        here = pl.ds(pl.multiple_of(i * CHUNK, CHUNK), CHUNK)
        deposit(0, here, moving[:, here])
        return carry

    lax.fori_loop(0, chunks, first_deposit, 0, unroll=chunks)

    def between_first():
        place(1, 0, solvent_chunks)
        place_beads(1)

    exchange(0, between_first)

    totals[...] = jnp.zeros_like(totals)

    def turn(i, carry):
        here = pl.ds(pl.multiple_of(i * CHUNK, CHUNK), CHUNK)
        moved = gather_collide(0, here)
        moving[:, here] = moved
        deposit(1, here, moved)
        return carry

    lax.fori_loop(0, chunks, turn, 0, unroll=chunks)

    tiles = solvent // LANES

    def between_second():
        row8 = rows_of((8, LANES))

        def fill(i, carry):
            parts = []
            for k in range(2):
                here = pl.ds(pl.multiple_of((2 * i + k) * LANES, LANES), LANES)
                now = moving[:, here]
                rounded = now.astype(BF16).astype(F32)
                entry = jnp.where(row8 < 4, rounded, now - rounded)
                entry = jnp.where(row8 == 3, cols[1, :, here].astype(F32), entry)
                parts.append(jnp.where(row8 == 7, lays[1, :, here].astype(F32), entry))
            leave_table[pl.ds(pl.multiple_of(16 * i, 16), 16), :] = jnp.concatenate(
                parts, axis=0
            ).astype(BF16)
            return carry

        lax.fori_loop(0, tiles // 2, fill, 0, unroll=8)

        def pick(d, carry):
            for side in range(2):
                index = jnp.maximum(leave_ref[d, side : side + 1, :], 0)
                offset = (index & (LANES - 1)).astype(F32)
                rest = (offset - rows_of((16, CAP)).astype(F32)).astype(BF16)
                one, zero = jnp.ones((16, CAP), BF16), jnp.zeros((16, CAP), BF16)
                spot = jnp.concatenate(
                    [jnp.where(rest == float(16 * j), one, zero) for j in range(8)], axis=0
                )
                found = jnp.dot(leave_table[...], spot, preferred_element_type=F32)
                tile = lax.shift_right_logical(index, 7)
                chosen = found[0:8]
                for i in range(1, tiles):
                    chosen = jnp.where(tile == i, found[8 * i : 8 * i + 8], chosen)
                leave_moving[d, side] = chosen + pltpu.roll(chosen, 4, 0)
                leave_layer[d, side] = chosen[7:8].astype(I32)
                leave_onehot[d, side] = one_hot(chosen[3:4].astype(I32))
            return carry

        lax.fori_loop(0, 3, pick, 0, unroll=3)

    exchange(1, between_second)

    slot = lanes_of((8, CAP))
    travels = []
    for d in (2, 0, 1):
        for side in range(2):
            gathered = jnp.dot(
                results[...], leave_onehot[d, side], preferred_element_type=F32
            )
            moved = collide(leave_moving[d, side], leave_layer[d, side], gathered, tables)
            leave_send[d, side] = jnp.where(slot < count_ref[side, d], moved, 0.0)
            offset = tuple(2 * side - 1 if axis == d else 0 for axis in range(3))
            travel = remote(
                leave_send.at[d, side],
                leave_recv.at[d, 1 - side],
                2 * len(OFFSETS) + 2 * d + side,
                offset,
            )
            travel.start()
            travels.append(travel)

    def finish(i, carry):
        here = pl.ds(pl.multiple_of(i * CHUNK, CHUNK), CHUNK)
        velocity_out[:, here] = gather_collide(1, here)[0:3]
        return carry

    lax.fori_loop(0, solvent_chunks, finish, 0, unroll=solvent_chunks)
    bead_out[...] = gather_collide(1, pl.ds(solvent, beads))[0:3]

    for travel in travels:
        travel.wait()
    for d in range(3):
        for side in range(2):
            arrivals_out[d, :, side, :] = leave_recv[d, side, 0:3, :]


def write(*refs):
    sems = refs[-1]
    count = len(refs) // 2
    copies = [
        pltpu.make_async_copy(refs[i], refs[count + i], sems.at[i]) for i in range(count)
    ]
    for copy in copies:
        copy.start()
    for copy in copies:
        copy.wait()


def per_device(
    velocity, position, bead_velocity, bead_mass, bead_position, grid_shift, rot_axis,
    leave_count, leave_index,
):
    solvent, beads = velocity.shape[1], bead_velocity.shape[1]
    count = solvent + beads
    vmem = pl.BlockSpec(memory_space=pltpu.VMEM)
    velocity_out, bead_out, arrivals = pl.pallas_call(
        kernel,
        out_shape=(
            pltpu.VMEM((3, solvent), F32),
            pltpu.VMEM((3, beads), F32),
            pltpu.VMEM((3, 3, 2, CAP), F32),
        ),
        in_specs=[pl.BlockSpec(memory_space=pltpu.HBM)] * 10,
        out_specs=(vmem, vmem, vmem),
        scratch_shapes=[
            pltpu.SMEM((2, 3), I32),
            pltpu.SMEM((2, 3), I32),
            pltpu.VMEM((3, solvent), F32),
            pltpu.VMEM((3, 2, solvent), I32),
            pltpu.VMEM((3, beads), F32),
            pltpu.VMEM((1, beads), F32),
            pltpu.VMEM((3, 2, beads), I32),
            pltpu.VMEM((2, 4, 16, 32), I32),
            pltpu.VMEM((3, 2, CAP), I32),
            pltpu.VMEM((3, 8, LANES), F32),
            pltpu.SemaphoreType.DMA((10,)),
            pltpu.VMEM((8, count), F32),
            pltpu.VMEM((1, count), F32),
            pltpu.VMEM((2, 1, count), I32),
            pltpu.VMEM((2, 1, count), I32),
            pltpu.VMEM((2, COLUMNS, count), BF16),
            pltpu.VMEM((8 * LAYERS, COLUMNS), F32),
            pltpu.VMEM((LAYERS, 8, WIDE), F32),
            pltpu.VMEM((8 * LAYERS, COLUMNS), BF16),
            pltpu.VMEM((2, 2, 16, LANES), F32),
            pltpu.VMEM((2, 2, 8, LANES), F32),
            pltpu.VMEM((2, 2, 6, 8, LANES), F32),
            pltpu.VMEM((2, 2, 6, 1, LANES), F32),
            pltpu.VMEM((2, 2, 2, 3, LANES), F32),
            pltpu.VMEM((2, 2, 8, LANES), F32),
            pltpu.VMEM((2, 6, 2, 8, LANES), F32),
            pltpu.VMEM((2, 2, 6, 8, LANES), F32),
            pltpu.VMEM((8 * solvent // LANES, LANES), BF16),
            pltpu.VMEM((3, 2, 8, CAP), F32),
            pltpu.VMEM((3, 2, 1, CAP), I32),
            pltpu.VMEM((3, 2, COLUMNS, CAP), BF16),
            pltpu.VMEM((3, 2, 8, CAP), F32),
            pltpu.VMEM((3, 2, 8, CAP), F32),
            pltpu.SemaphoreType.DMA((2 * len(OFFSETS) + 6,)),
            pltpu.SemaphoreType.DMA((2 * len(OFFSETS) + 6,)),
        ],
        compiler_params=pltpu.CompilerParams(
            collective_id=0, has_side_effects=True, vmem_limit_bytes=62 * 1024 * 1024
        ),
        cost_estimate=pl.CostEstimate(flops=10**9, bytes_accessed=10**6, transcendentals=0),
        name="collisions",
    )(
        grid_shift,
        leave_count.reshape(3, 2).T,
        velocity,
        jnp.transpose(position, (1, 0, 2)),
        bead_velocity,
        bead_mass.reshape(1, beads),
        jnp.transpose(bead_position, (1, 0, 2)),
        jnp.swapaxes(rot_axis, 2, 3),
        leave_index,
        jnp.asarray(rotation_table()),
    )
    made = (velocity_out, bead_out, arrivals)
    velocity_out, bead_out, arrivals = pl.pallas_call(
        write,
        out_shape=tuple(jax.ShapeDtypeStruct(x.shape, x.dtype) for x in made),
        in_specs=[vmem] * 3,
        out_specs=(pl.BlockSpec(memory_space=pltpu.HBM),) * 3,
        scratch_shapes=[pltpu.SemaphoreType.DMA((3,))],
        compiler_params=pltpu.CompilerParams(vmem_limit_bytes=4 * 1024 * 1024),
        name="write_results",
    )(*made)
    return velocity_out, bead_out, jnp.transpose(arrivals, (0, 2, 1, 3))


def solution(mesh):
    return jax.shard_map(
        per_device,
        mesh=mesh,
        in_specs=(
            P(None, ("gx", "gy", "gz")),
            P(None, None, ("gx", "gy", "gz")),
            P(None, ("gx", "gy", "gz")),
            P(("gx", "gy", "gz")),
            P(None, None, ("gx", "gy", "gz")),
            P(),
            P(None, "gx", "gy", "gz"),
            P(None, None, ("gx", "gy", "gz")),
            P(None, None, ("gx", "gy", "gz")),
        ),
        out_specs=(
            P(None, ("gx", "gy", "gz")),
            P(None, ("gx", "gy", "gz")),
            P(None, None, None, ("gx", "gy", "gz")),
        ),
        check_vma=False,
    )
```

```python
import math

import jax
import jax.numpy as jnp
import numpy as np
from jax import lax
from jax.experimental import pallas as pl
from jax.experimental.pallas import tpu as pltpu
from jax.sharding import PartitionSpec as P

STEPS = 2
AXES = 64
CAP = 256
COSINE = math.cos(130.0 * math.pi / 180.0)
SINE = math.sin(130.0 * math.pi / 180.0)
GOLDEN = math.pi * (3.0 - math.sqrt(5.0))

LANES = 128
CHUNK = 1024
COLUMNS = 176
LAYERS = 18
WIDE = 256
MESH = pl.DeviceIdType.MESH
F32 = jnp.float32
BF16 = jnp.bfloat16
I32 = jnp.int32


def rotation_table():
    ordinal = np.arange(AXES) + 0.5
    height = 1.0 - 2.0 * ordinal / AXES
    radius = np.sqrt(1.0 - height * height)
    n = np.stack([radius * np.cos(ordinal * GOLDEN), radius * np.sin(ordinal * GOLDEN), height])
    zero = np.zeros(AXES)
    skew = np.array([[zero, -n[2], n[1]], [n[2], zero, -n[0]], [-n[1], n[0], zero]])
    matrix = COSINE * np.eye(3)[:, :, None] + SINE * skew + (1.0 - COSINE) * n[:, None] * n[None]
    table = np.zeros((3, 8, LANES), np.float32)
    for c in range(3):
        table[c, 0:3, :AXES] = matrix[:, c]
        table[c, 4:7, :AXES] = matrix[:, c]
    return table


PLANE = [(dx, dy) for dx in (-1, 0, 1) for dy in (-1, 0, 1)]
OFFSETS = [(dx, dy, dz) for dz in (-1, 1) for dx, dy in PLANE] + [
    (dx, dy, 0) for dx, dy in PLANE if (dx, dy) != (0, 0)
]
EDGES = [(dx, dy) for dx in (-1, 0, 1) for dy in (-1, 1)]


def moved_edge(edge, place):
    dx, dy = edge
    target = {1: 0, -1: 5}[dy] + (4 if dx == 1 else 0)
    source = {1: 5, -1: 0}[dy] + (4 if dx == -1 else 0)
    if dx == 0:
        chosen = (place >= target) & (place < target + 5)
    else:
        chosen = place == target
    return (target - source) % LANES, chosen


def rows_of(shape):
    return lax.broadcasted_iota(I32, shape, 0)


def lanes_of(shape):
    return lax.broadcasted_iota(I32, shape, 1)


def lanes_from(tile, source):
    return jnp.take_along_axis(tile, source & (LANES - 1), axis=1)


def cell_rows(coords, shift_ref, step):
    layer = []
    for d in range(3):
        shift = shift_ref[step, d]
        offset = jnp.where(shift > 0, 1, 0)
        layer.append(lax.shift_right_arithmetic(coords[d] - shift, 4) + offset)
    return column_of(layer[0], layer[1]), layer[2]


def column_of(first, second):
    inner = first * 32 + second
    return jnp.where(second == 32, first + 160, jnp.where(second == 0, first + 165, inner))


def one_hot(column):
    n = column.shape[1]
    rest = column.astype(F32) - rows_of((16, n)).astype(F32)
    rest = rest.astype(BF16)
    one, zero = jnp.ones((16, n), BF16), jnp.zeros((16, n), BF16)
    return jnp.concatenate(
        [jnp.where(rest == float(16 * j), one, zero) for j in range(COLUMNS // 16)], axis=0
    )


def deposit_rows(moving, weight, layer):
    n = moving.shape[1]
    row8 = rows_of((8, n))
    summand = moving * weight
    high = summand.astype(BF16).astype(F32)
    parts = jnp.where(row8 < 4, high, summand - high)
    parts = jnp.concatenate([parts, parts], axis=0).astype(BF16)
    half = lax.shift_right_logical(rows_of((16, n)), 3)
    rest = (layer - half).astype(F32).astype(BF16)
    zero = jnp.zeros((16, n), BF16)
    return jnp.concatenate(
        [jnp.where(rest == float(2 * j), parts, zero) for j in range(LAYERS // 2)], axis=0
    )


def collide(moving, layer, gathered, tables):
    chosen = gathered[0:8]
    for z in range(1, 17):
        chosen = jnp.where(layer == z, gathered[8 * z : 8 * z + 8], chosen)
    return rotate(moving, chosen, tables)


def rotate(moving, chosen, tables):
    n = moving.shape[1]
    mean = chosen + pltpu.roll(chosen, 4, 0)
    axis = jnp.broadcast_to(mean[3:4], (8, n)).astype(I32)
    relative = moving - mean
    result = mean
    for c in range(3):
        columns = jnp.concatenate(
            [
                jnp.take_along_axis(tables[c], axis[:, i : i + LANES], axis=1)
                for i in range(0, n, LANES)
            ],
            axis=1,
        )
        result = result + columns * relative[c : c + 1]
    row8 = rows_of((8, n))
    return jnp.where((row8 & 3) == 3, 1.0, result)


def kernel(
    shift_hbm, count_hbm, velocity_hbm, position_hbm, bead_velocity_hbm, bead_mass_hbm,
    bead_position_hbm, rot_hbm, leave_hbm, table_hbm,
    velocity_out, bead_out, arrivals_out,
    shift_ref, count_ref, velocity_ref, position_ref, bead_velocity_ref, bead_mass_ref,
    bead_position_ref, rot_ref, leave_ref, table_ref, load_sem,
    moving, weight, cols, lays, onehots, totals, cells, results,
    send_z, send_y, send_x, recv_edge, recv_line, recv_z, recv_y, recv_x,
    leave_table, leave_moving, leave_layer, leave_column, leave_onehot, leave_send, leave_recv,
    send_sem, recv_sem,
):
    solvent = velocity_ref.shape[1]
    beads = bead_velocity_ref.shape[1]
    count = solvent + beads
    chunks = count // CHUNK

    names = ("gx", "gy", "gz")

    def device_at(offset):
        where = {}
        for name, step_by in zip(names, offset):
            if step_by is not None and not (isinstance(step_by, int) and step_by == 0):
                size, me = lax.axis_size(name), lax.axis_index(name)
                where[name] = lax.rem(me + size + step_by, size)
        return where

    barrier = pltpu.get_barrier_semaphore()
    for offset in OFFSETS:
        pl.semaphore_signal(barrier, inc=1, device_id=device_at(offset), device_id_type=MESH)

    loads = [
        pltpu.make_async_copy(src, dst, load_sem.at[i])
        for i, (src, dst) in enumerate(
            (
                (shift_hbm, shift_ref),
                (position_hbm, position_ref),
                (bead_position_hbm, bead_position_ref),
                (velocity_hbm, velocity_ref),
                (bead_velocity_hbm, bead_velocity_ref),
                (bead_mass_hbm, bead_mass_ref),
                (rot_hbm, rot_ref),
                (leave_hbm, leave_ref),
                (count_hbm, count_ref),
                (table_hbm, table_ref),
            )
        )
    ]
    for copy in loads:
        copy.start()
    for copy in loads:
        copy.wait()

    def remote(src, dst, number, offset):
        return pltpu.make_async_remote_copy(
            src_ref=src,
            dst_ref=dst,
            send_sem=send_sem.at[number],
            recv_sem=recv_sem.at[number],
            device_id=device_at(offset),
            device_id_type=MESH,
        )

    def load(velocity, where, length):
        moving[0:3, pl.ds(where, length)] = velocity
        moving[3:4, pl.ds(where, length)] = jnp.ones((1, length), F32)
        moving[4:7, pl.ds(where, length)] = velocity
        moving[7:8, pl.ds(where, length)] = jnp.ones((1, length), F32)

    load(velocity_ref[...], 0, solvent)
    load(bead_velocity_ref[...], solvent, beads)
    weight[:, 0:solvent] = jnp.ones((1, solvent), F32)
    weight[:, solvent:count] = bead_mass_ref[...]

    def place(step, first, number):
        def body(i, carry):
            here = pl.ds(pl.multiple_of(i * CHUNK, CHUNK), CHUNK)
            coords = [position_ref[d, step : step + 1, here] for d in range(3)]
            column, layer = cell_rows(coords, shift_ref, step)
            cols[step, :, here] = column
            lays[step, :, here] = layer
            onehots[step, :, here] = one_hot(column)
            return carry

        lax.fori_loop(first, first + number, body, 0, unroll=number)

    def place_beads(step):
        here = pl.ds(solvent, beads)
        coords = [bead_position_ref[d, step : step + 1, :] for d in range(3)]
        column, layer = cell_rows(coords, shift_ref, step)
        cols[step, :, here] = column
        lays[step, :, here] = layer
        onehots[step, :, here] = one_hot(column)

    def deposit(step, here, moved):
        rows = deposit_rows(moved, weight[:, here], lays[step, :, here])
        totals[...] += lax.dot_general(
            rows, onehots[step, :, here], (((1,), (1,)), ((), ())), preferred_element_type=F32
        )

    lane = lanes_of((8, LANES))

    def own_axes(step):
        offset = [jnp.where(shift_ref[step, d] > 0, 1, 0) for d in range(3)]
        local = rows_of((LANES, WIDE))
        target = column_of(
            lax.shift_right_logical(local, 5) + offset[0], (local & 31) + offset[1]
        )
        spread = jnp.where(lanes_of((LANES, WIDE)) == target, 1.0, 0.0).astype(BF16)
        held = jnp.concatenate([rot_ref[step, x] for x in range(4)], axis=1)
        by_layer = jnp.dot(
            held.astype(F32).astype(BF16), spread, preferred_element_type=F32
        )
        above = jnp.concatenate([jnp.zeros((1, WIDE), F32), by_layer], axis=0)
        below = jnp.concatenate([by_layer, jnp.zeros((1, WIDE), F32)], axis=0)
        return jnp.where(offset[2] > 0, above, below)

    last = lax.axis_index("gz") & 1
    first = 1 - last

    def exchange(step, between, early=None):
        axes = own_axes(step)
        row8w = rows_of((8, WIDE))
        row8 = rows_of((8, LANES))
        cells[:, :, COLUMNS:WIDE] = jnp.zeros((LAYERS, 8, WIDE - COLUMNS), F32)
        cells[17] = jnp.zeros((8, WIDE), F32)

        def settle(z):
            part = totals[8 * z : 8 * z + 8, :]
            cells[z, :, 0:COLUMNS] = part + pltpu.roll(part, 4, 0)
            cells[z] = jnp.where(row8w == 7, axes[z : z + 1], cells[z])

        settle(0)
        settle(16)
        for side in range(2):
            near, far = cells[16 * side, :, 0:LANES], cells[16 * side, :, LANES:WIDE]
            edge = lanes_from(far, lane + 32 - 10 * row8)
            edge = jnp.where((lane >= 10 * row8) & (lane < 10 * row8 + 10), edge, 0.0)
            send_z[step, side, 2:3] = jnp.sum(edge, axis=0, keepdims=True)
            for at, tile in ((0, near), (3, far)):
                line = lanes_from(tile, lane & 31)
                line = jnp.where(lax.shift_right_logical(lane, 5) == (row8 & 3), line, 0.0)
                for half in range(2):
                    send_z[step, side, at + half : at + half + 1] = jnp.sum(
                        line[4 * half : 4 * half + 4], axis=0, keepdims=True
                    )
            send_z[step, side, 5:9] = near[0:4]
            send_z[step, side, 9:10] = near[7:8]

        if step == 0:
            pl.semaphore_wait(barrier, len(OFFSETS))

        travels = {}

        def send(src, dst, offset):
            travel = remote(src, dst, len(OFFSETS) * step + OFFSETS.index(offset), offset)
            travel.start()
            travels[offset] = travel

        for side in range(2):
            dz = 2 * side - 1
            for dx in (-1, 0, 1):
                for dy in (-1, 1):
                    back = EDGES.index((-dx, -dy))
                    send(
                        send_z.at[step, side, pl.ds(2, 1)],
                        recv_edge.at[step, 1 - side, back],
                        (dx, dy, dz),
                    )
            for dx in (-1, 1):
                send(
                    send_z.at[step, side, pl.ds(1 + dx, 3)],
                    recv_line.at[step, 1 - side, (1 - dx) // 2],
                    (dx, 0, dz),
                )
            send(send_z.at[step, side, pl.ds(2, 8)], recv_z.at[step, 1 - side], (0, 0, dz))

        for z in range(1, 16):
            settle(z)
        for group in range(2):
            packed = jnp.zeros((8, LANES), F32)
            for j in range(9):
                z = 9 * group + j
                if z < 17:
                    turned = pltpu.roll(cells[z, :, LANES:WIDE], (12 * j - 32) % LANES, 1)
                    packed = jnp.where((lane >= 12 * j) & (lane < 12 * j + 10), turned, packed)
            send_y[step, group] = packed
        for dx in (-1, 0, 1):
            for dy in (-1, 1):
                back = EDGES.index((-dx, -dy))
                send(send_y.at[step], recv_y.at[step, back], (dx, dy, 0))

        for group in range(6):
            packed_low = jnp.zeros((8, LANES), F32)
            packed_high = jnp.zeros((8, LANES), F32)
            for j in range(3):
                z = 3 * group + j
                if z < 17:
                    near, far = cells[z, :, 0:LANES], cells[z, :, LANES:WIDE]
                    face_low = jnp.where(lane < 32, near, far)
                    face_high = jnp.where(lane < 32, far, pltpu.roll(far, LANES - 4, 1))
                    if j:
                        face_low = pltpu.roll(face_low, 42 * j, 1)
                        face_high = pltpu.roll(face_high, 42 * j, 1)
                    inside = (lane >= 42 * j) & (lane < 42 * j + 38)
                    packed_low = jnp.where(inside, face_low, packed_low)
                    packed_high = jnp.where(inside, face_high, packed_high)
            send_x[step, 0, group] = packed_low
            send_x[step, 1, group] = packed_high
        send(send_x.at[step, 0], recv_x.at[step, 1], (-1, 0, 0))
        send(send_x.at[step, 1], recv_x.at[step, 0], (1, 0, 0))

        between()

        for offset, travel in travels.items():
            if offset[2] == 0:
                travel.wait()
        place12 = lax.rem(lane, 12)
        both_groups = []
        for group in range(2):
            both = jnp.zeros((8, LANES), F32)
            for k, edge in enumerate(EDGES):
                turn_by, chosen = moved_edge(edge, place12)
                both += jnp.where(chosen, pltpu.roll(recv_y[step, k, group], turn_by, 1), 0.0)
            both_groups.append(both)
        ends = (lane == 32) | (lane == 37)
        ends_high = (lane == 36) | (lane == 41)
        for group in range(6):
            for j in range(3):
                z = 3 * group + j
                if z < 17:
                    from_low, from_high = recv_x[step, 0, group], recv_x[step, 1, group]
                    if j:
                        from_low = pltpu.roll(from_low, LANES - 42 * j, 1)
                        from_high = pltpu.roll(from_high, LANES - 42 * j, 1)
                    shift_by = (32 - 12 * (z % 9)) % LANES
                    from_second = pltpu.roll(both_groups[z // 9], shift_by, 1)
                    cells[z, :, 0:LANES] += jnp.where(lane < 32, from_low, 0.0)
                    cells[z, :, LANES:WIDE] += (
                        jnp.where(
                            lane < 32,
                            from_high,
                            jnp.where(
                                ends,
                                from_low,
                                jnp.where(ends_high, pltpu.roll(from_high, 4, 1), 0.0),
                            ),
                        )
                        + jnp.where((lane >= 32) & (lane < 42), from_second, 0.0)
                    )

        def entry_of(z):
            full = cells[z]
            full = jnp.where((row8w >= 4) & (row8w < 7), pltpu.roll(full, 4, 0), full)
            mean = full / jnp.maximum(full[3:4], 1.0)
            rounded = mean.astype(BF16).astype(F32)
            entry = jnp.where(row8w < 4, rounded, mean - rounded)
            return jnp.where(row8w == 3, full[7:8], jnp.where(row8w == 7, 0.0, entry))

        def finish_pair(z):
            pair = jnp.concatenate([entry_of(z), entry_of(z + 1)], axis=0).astype(BF16)
            where = 8 * z if isinstance(z, int) else pl.multiple_of(8 * z, 16)
            results[pl.ds(where, 16), :] = pair[:, 0:COLUMNS]

        for z in range(2, 16, 2):
            finish_pair(z)

        def collect(side):
            for dx, dy in PLANE:
                if dy:
                    landed = recv_edge.at[step, side, EDGES.index((dx, dy))]
                elif dx:
                    landed = recv_line.at[step, side, (1 + dx) // 2]
                else:
                    landed = recv_z.at[step, side]
                number = len(OFFSETS) * step + 9 * (1 - side) + PLANE.index((-dx, -dy))
                remote(landed, landed, number, (0, 0, 1)).wait_recv()
            face = recv_z[step, side]
            lane1 = lanes_of((1, LANES))
            place10 = lax.rem(lane1, 10)
            edge = face[0:1]
            for k, offset in enumerate(EDGES):
                turn_by, chosen = moved_edge(offset, place10)
                edge += jnp.where(chosen, pltpu.roll(recv_edge[step, side, k], turn_by, 1), 0.0)
            low, high = recv_line[step, side, 0], recv_line[step, side, 1]
            at_low, at_high = (place10 == 0) | (place10 == 5), (place10 == 4) | (place10 == 9)
            edge += jnp.where(at_low, pltpu.roll(low[0:1], LANES - 4, 1), 0.0)
            edge += jnp.where(at_high, pltpu.roll(high[2:3], 4, 1), 0.0)
            edge = lanes_from(jnp.broadcast_to(edge, (8, LANES)), lane - 32 + 10 * row8)
            lines = []
            for line in (low[1:3], face[1:3] + high[0:2]):
                wide = jnp.where(row8 < 4, line[0:1], line[1:2])
                lines.append(lanes_from(wide, (lane & 31) + 32 * (row8 & 3)))
            rest = jnp.where(row8 == 7, face, pltpu.roll(face, 5, 0))
            near = rest + jnp.where(lane < 32, lines[0], 0.0)
            far = jnp.where(lane < 32, lines[1], jnp.where(lane < 42, edge, 0.0))
            cells[16 * side, :, 0:LANES] += near
            cells[16 * side, :, LANES:WIDE] += far
            finish_pair(16 * side)

        collect(first)
        if early is not None:
            finish_pair(16 * last)
            early()
        collect(last)
        for offset, travel in travels.items():
            if offset[2] != 0:
                travel.wait_send()

    tables = [table_ref[c] for c in range(3)]

    def gather_collide(step, here):
        gathered = jnp.dot(results[...], onehots[step, :, here], preferred_element_type=F32)
        return collide(moving[:, here], lays[step, :, here], gathered, tables)

    solvent_chunks = solvent // CHUNK
    totals[...] = jnp.zeros_like(totals)
    place(0, 0, solvent_chunks)
    place_beads(0)

    def first_deposit(i, carry):
        here = pl.ds(pl.multiple_of(i * CHUNK, CHUNK), CHUNK)
        deposit(0, here, moving[:, here])
        return carry

    lax.fori_loop(0, chunks, first_deposit, 0, unroll=chunks)

    def between_first():
        place(1, 0, solvent_chunks)
        place_beads(1)

    exchange(0, between_first)

    totals[...] = jnp.zeros_like(totals)

    def turn(i, carry):
        here = pl.ds(pl.multiple_of(i * CHUNK, CHUNK), CHUNK)
        moved = gather_collide(0, here)
        moving[:, here] = moved
        deposit(1, here, moved)
        return carry

    lax.fori_loop(0, chunks, turn, 0, unroll=chunks)

    tiles = solvent // LANES

    def between_second():
        row8 = rows_of((8, LANES))

        def fill(i, carry):
            parts = []
            for k in range(2):
                here = pl.ds(pl.multiple_of((2 * i + k) * LANES, LANES), LANES)
                now = moving[:, here]
                rounded = now.astype(BF16).astype(F32)
                entry = jnp.where(row8 < 4, rounded, now - rounded)
                entry = jnp.where(row8 == 3, cols[1, :, here].astype(F32), entry)
                parts.append(jnp.where(row8 == 7, lays[1, :, here].astype(F32), entry))
            leave_table[pl.ds(pl.multiple_of(16 * i, 16), 16), :] = jnp.concatenate(
                parts, axis=0
            ).astype(BF16)
            return carry

        lax.fori_loop(0, tiles // 2, fill, 0, unroll=8)

        def pick(d, carry):
            for side in range(2):
                index = jnp.maximum(leave_ref[d, side : side + 1, :], 0)
                offset = (index & (LANES - 1)).astype(F32)
                rest = (offset - rows_of((16, CAP)).astype(F32)).astype(BF16)
                one, zero = jnp.ones((16, CAP), BF16), jnp.zeros((16, CAP), BF16)
                spot = jnp.concatenate(
                    [jnp.where(rest == float(16 * j), one, zero) for j in range(8)], axis=0
                )
                found = jnp.dot(leave_table[...], spot, preferred_element_type=F32)
                tile = lax.shift_right_logical(index, 7)
                chosen = found[0:8]
                for i in range(1, tiles):
                    chosen = jnp.where(tile == i, found[8 * i : 8 * i + 8], chosen)
                leave_moving[d, side] = chosen + pltpu.roll(chosen, 4, 0)
                leave_layer[d, side] = chosen[7:8].astype(I32)
                leave_column[d, side] = chosen[3:4]
                leave_onehot[d, side] = one_hot(chosen[3:4].astype(I32))
            return carry

        lax.fori_loop(0, 3, pick, 0, unroll=3)

    row8 = rows_of((8, CAP))
    slot = lanes_of((8, CAP))

    def leave(d, side, shared=None):
        gathered = jnp.dot(results[...], leave_onehot[d, side], preferred_element_type=F32)
        before, layer = leave_moving[d, side], leave_layer[d, side]
        moved = collide(before, layer, gathered, tables)
        unused = 0.0
        if shared is not None:
            open_ = jnp.broadcast_to(layer, (8, CAP)) == shared
            mark = jnp.where(open_, leave_column[d, side], -1.0)
            moved = jnp.where(row8 == 3, mark, jnp.where(open_, before, moved))
            unused = jnp.where(row8 == 3, -1.0, 0.0)
        leave_send[d, side] = jnp.where(slot < count_ref[side, d], moved, unused)
        step_by = 2 * side - 1
        offset = tuple(step_by if axis == d else None for axis in range(3))
        travel = remote(
            leave_send.at[d, side], leave_recv.at[d, 1 - side], leave_number(d, side), offset
        )
        travel.start()
        return travel

    def leave_number(d, side):
        return 2 * len(OFFSETS) + 2 * d + side

    travels = []
    exchange(1, between_second, lambda: travels.append(leave(2, last, 16 * last)))
    for d, side in ((0, 0), (0, 1), (2, first), (1, 0), (1, 1)):
        travels.append(leave(d, side))

    def finish(i, carry):
        here = pl.ds(pl.multiple_of(i * CHUNK, CHUNK), CHUNK)
        velocity_out[:, here] = gather_collide(1, here)[0:3]
        return carry

    lax.fori_loop(0, solvent_chunks, finish, 0, unroll=solvent_chunks)
    bead_out[...] = gather_collide(1, pl.ds(solvent, beads))[0:3]

    arrived = leave_recv.at[2, last]
    remote(arrived, arrived, leave_number(2, first), (0, 0, 1)).wait_recv()
    got = leave_recv[2, last]
    mark = got[3:4]
    shared = jnp.dot(
        results[pl.ds(pl.multiple_of(128 * last, 16), 16), :],
        one_hot(mark.astype(I32)),
        preferred_element_type=F32,
    )
    got = jnp.where(mark >= 0.0, rotate(got, shared[0:8], tables), got)
    arrived = leave_recv.at[2, first]
    remote(arrived, arrived, leave_number(2, last), (0, 0, 1)).wait_recv()
    for side in range(2):
        arrivals_out[2, :, side, :] = jnp.where(last == side, got, leave_recv[2, side])[0:3]
    for d in range(2):
        for side in range(2):
            arrived = leave_recv.at[d, side]
            remote(arrived, arrived, leave_number(d, 1 - side), (0, 0, 1)).wait_recv()
            arrivals_out[d, :, side, :] = leave_recv[d, side, 0:3, :]
    for travel in travels:
        travel.wait_send()


def write(*refs):
    sems = refs[-1]
    count = len(refs) // 2
    copies = [
        pltpu.make_async_copy(refs[i], refs[count + i], sems.at[i]) for i in range(count)
    ]
    for copy in copies:
        copy.start()
    for copy in copies:
        copy.wait()


def per_device(
    velocity, position, bead_velocity, bead_mass, bead_position, grid_shift, rot_axis,
    leave_count, leave_index,
):
    solvent, beads = velocity.shape[1], bead_velocity.shape[1]
    count = solvent + beads
    vmem = pl.BlockSpec(memory_space=pltpu.VMEM)
    velocity_out, bead_out, arrivals = pl.pallas_call(
        kernel,
        out_shape=(
            pltpu.VMEM((3, solvent), F32),
            pltpu.VMEM((3, beads), F32),
            pltpu.VMEM((3, 3, 2, CAP), F32),
        ),
        in_specs=[pl.BlockSpec(memory_space=pltpu.HBM)] * 10,
        out_specs=(vmem, vmem, vmem),
        scratch_shapes=[
            pltpu.SMEM((2, 3), I32),
            pltpu.SMEM((2, 3), I32),
            pltpu.VMEM((3, solvent), F32),
            pltpu.VMEM((3, 2, solvent), I32),
            pltpu.VMEM((3, beads), F32),
            pltpu.VMEM((1, beads), F32),
            pltpu.VMEM((3, 2, beads), I32),
            pltpu.VMEM((2, 4, 16, 32), I32),
            pltpu.VMEM((3, 2, CAP), I32),
            pltpu.VMEM((3, 8, LANES), F32),
            pltpu.SemaphoreType.DMA((10,)),
            pltpu.VMEM((8, count), F32),
            pltpu.VMEM((1, count), F32),
            pltpu.VMEM((2, 1, count), I32),
            pltpu.VMEM((2, 1, count), I32),
            pltpu.VMEM((2, COLUMNS, count), BF16),
            pltpu.VMEM((8 * LAYERS, COLUMNS), F32),
            pltpu.VMEM((LAYERS, 8, WIDE), F32),
            pltpu.VMEM((8 * LAYERS, COLUMNS), BF16),
            pltpu.VMEM((2, 2, 16, LANES), F32),
            pltpu.VMEM((2, 2, 8, LANES), F32),
            pltpu.VMEM((2, 2, 6, 8, LANES), F32),
            pltpu.VMEM((2, 2, 6, 1, LANES), F32),
            pltpu.VMEM((2, 2, 2, 3, LANES), F32),
            pltpu.VMEM((2, 2, 8, LANES), F32),
            pltpu.VMEM((2, 6, 2, 8, LANES), F32),
            pltpu.VMEM((2, 2, 6, 8, LANES), F32),
            pltpu.VMEM((8 * solvent // LANES, LANES), BF16),
            pltpu.VMEM((3, 2, 8, CAP), F32),
            pltpu.VMEM((3, 2, 1, CAP), I32),
            pltpu.VMEM((3, 2, 1, CAP), F32),
            pltpu.VMEM((3, 2, COLUMNS, CAP), BF16),
            pltpu.VMEM((3, 2, 8, CAP), F32),
            pltpu.VMEM((3, 2, 8, CAP), F32),
            pltpu.SemaphoreType.DMA((2 * len(OFFSETS) + 6,)),
            pltpu.SemaphoreType.DMA((2 * len(OFFSETS) + 6,)),
        ],
        compiler_params=pltpu.CompilerParams(
            collective_id=0, has_side_effects=True, vmem_limit_bytes=62 * 1024 * 1024
        ),
        cost_estimate=pl.CostEstimate(flops=10**9, bytes_accessed=10**6, transcendentals=0),
        name="collisions",
    )(
        grid_shift,
        leave_count.reshape(3, 2).T,
        velocity,
        jnp.transpose(position, (1, 0, 2)),
        bead_velocity,
        bead_mass.reshape(1, beads),
        jnp.transpose(bead_position, (1, 0, 2)),
        jnp.swapaxes(rot_axis, 2, 3),
        leave_index,
        jnp.asarray(rotation_table()),
    )
    made = (velocity_out, bead_out, arrivals)
    velocity_out, bead_out, arrivals = pl.pallas_call(
        write,
        out_shape=tuple(jax.ShapeDtypeStruct(x.shape, x.dtype) for x in made),
        in_specs=[vmem] * 3,
        out_specs=(pl.BlockSpec(memory_space=pltpu.HBM),) * 3,
        scratch_shapes=[pltpu.SemaphoreType.DMA((3,))],
        compiler_params=pltpu.CompilerParams(vmem_limit_bytes=4 * 1024 * 1024),
        name="write_results",
    )(*made)
    return velocity_out, bead_out, jnp.transpose(arrivals, (0, 2, 1, 3))


def solution(mesh):
    return jax.shard_map(
        per_device,
        mesh=mesh,
        in_specs=(
            P(None, ("gx", "gy", "gz")),
            P(None, None, ("gx", "gy", "gz")),
            P(None, ("gx", "gy", "gz")),
            P(("gx", "gy", "gz")),
            P(None, None, ("gx", "gy", "gz")),
            P(),
            P(None, "gx", "gy", "gz"),
            P(None, None, ("gx", "gy", "gz")),
            P(None, None, ("gx", "gy", "gz")),
        ),
        out_specs=(
            P(None, ("gx", "gy", "gz")),
            P(None, ("gx", "gy", "gz")),
            P(None, None, None, ("gx", "gy", "gz")),
        ),
        check_vma=False,
    )
```

```python
import math

import jax
import jax.numpy as jnp
import numpy as np
from jax import lax
from jax.experimental import pallas as pl
from jax.experimental.pallas import tpu as pltpu
from jax.sharding import PartitionSpec as P

STEPS = 2
AXES = 64
CAP = 256
COSINE = math.cos(130.0 * math.pi / 180.0)
SINE = math.sin(130.0 * math.pi / 180.0)
GOLDEN = math.pi * (3.0 - math.sqrt(5.0))

LANES = 128
CHUNK = 1024
COLUMNS = 176
LAYERS = 18
WIDE = 256
MESH = pl.DeviceIdType.MESH
F32 = jnp.float32
BF16 = jnp.bfloat16
I32 = jnp.int32


def rotation_table():
    ordinal = np.arange(AXES) + 0.5
    height = 1.0 - 2.0 * ordinal / AXES
    radius = np.sqrt(1.0 - height * height)
    n = np.stack([radius * np.cos(ordinal * GOLDEN), radius * np.sin(ordinal * GOLDEN), height])
    zero = np.zeros(AXES)
    skew = np.array([[zero, -n[2], n[1]], [n[2], zero, -n[0]], [-n[1], n[0], zero]])
    matrix = COSINE * np.eye(3)[:, :, None] + SINE * skew + (1.0 - COSINE) * n[:, None] * n[None]
    table = np.zeros((3, 8, LANES), np.float32)
    for c in range(3):
        table[c, 0:3, :AXES] = matrix[:, c]
        table[c, 4:7, :AXES] = matrix[:, c]
    return table


PLANE = [(dx, dy) for dx in (-1, 0, 1) for dy in (-1, 0, 1)]
OFFSETS = [(dx, dy, dz) for dz in (-1, 1) for dx, dy in PLANE] + [
    (dx, dy, 0) for dx, dy in PLANE if (dx, dy) != (0, 0)
]
EDGES = [(dx, dy) for dx in (-1, 0, 1) for dy in (-1, 1)]


def moved_edge(edge, place):
    dx, dy = edge
    target = {1: 0, -1: 5}[dy] + (4 if dx == 1 else 0)
    source = {1: 5, -1: 0}[dy] + (4 if dx == -1 else 0)
    if dx == 0:
        chosen = (place >= target) & (place < target + 5)
    else:
        chosen = place == target
    return (target - source) % LANES, chosen


def rows_of(shape):
    return lax.broadcasted_iota(I32, shape, 0)


def lanes_of(shape):
    return lax.broadcasted_iota(I32, shape, 1)


def lanes_from(tile, source):
    return jnp.take_along_axis(tile, source & (LANES - 1), axis=1)


def cell_rows(coords, shift_ref, step):
    layer = []
    for d in range(3):
        shift = shift_ref[step, d]
        offset = jnp.where(shift > 0, 1, 0)
        layer.append(lax.shift_right_arithmetic(coords[d] - shift, 4) + offset)
    return column_of(layer[0], layer[1]), layer[2]


def column_of(first, second):
    inner = first * 32 + second
    return jnp.where(second == 32, first + 160, jnp.where(second == 0, first + 165, inner))


def one_hot(column):
    n = column.shape[1]
    rest = column.astype(F32) - rows_of((16, n)).astype(F32)
    rest = rest.astype(BF16)
    one, zero = jnp.ones((16, n), BF16), jnp.zeros((16, n), BF16)
    return jnp.concatenate(
        [jnp.where(rest == float(16 * j), one, zero) for j in range(COLUMNS // 16)], axis=0
    )


def deposit_rows(moving, weight, layer):
    n = moving.shape[1]
    row8 = rows_of((8, n))
    summand = moving * weight
    high = summand.astype(BF16).astype(F32)
    parts = jnp.where(row8 < 4, high, summand - high)
    parts = jnp.concatenate([parts, parts], axis=0).astype(BF16)
    half = lax.shift_right_logical(rows_of((16, n)), 3)
    rest = (layer - half).astype(F32).astype(BF16)
    zero = jnp.zeros((16, n), BF16)
    return jnp.concatenate(
        [jnp.where(rest == float(2 * j), parts, zero) for j in range(LAYERS // 2)], axis=0
    )


def collide(moving, layer, gathered, tables):
    chosen = gathered[0:8]
    for z in range(1, 17):
        chosen = jnp.where(layer == z, gathered[8 * z : 8 * z + 8], chosen)
    return rotate(moving, chosen, tables)


def rotate(moving, chosen, tables):
    n = moving.shape[1]
    mean = chosen + pltpu.roll(chosen, 4, 0)
    axis = jnp.broadcast_to(mean[3:4], (8, n)).astype(I32)
    relative = moving - mean
    result = mean
    for c in range(3):
        columns = jnp.concatenate(
            [
                jnp.take_along_axis(tables[c], axis[:, i : i + LANES], axis=1)
                for i in range(0, n, LANES)
            ],
            axis=1,
        )
        result = result + columns * relative[c : c + 1]
    row8 = rows_of((8, n))
    return jnp.where((row8 & 3) == 3, 1.0, result)


def kernel(
    shift_hbm, count_hbm, velocity_hbm, position_hbm, bead_velocity_hbm, bead_mass_hbm,
    bead_position_hbm, rot_hbm, leave_hbm, table_hbm,
    velocity_out, bead_out, arrivals_out,
    shift_ref, count_ref, velocity_ref, position_ref, bead_velocity_ref, bead_mass_ref,
    bead_position_ref, rot_ref, leave_ref, table_ref, load_sem,
    moving, weight, cols, lays, onehots, turned_onehots, totals, cells, results,
    send_z, send_y, send_x, recv_edge, recv_line, recv_z, recv_y, recv_x,
    leave_table, leave_moving, leave_layer, leave_column, leave_onehot, leave_send, leave_recv,
    ahead_send, ahead_recv,
    send_sem, recv_sem,
):
    solvent = velocity_ref.shape[1]
    beads = bead_velocity_ref.shape[1]
    count = solvent + beads
    chunks = count // CHUNK

    names = ("gx", "gy", "gz")

    def device_at(offset):
        where = {}
        for name, step_by in zip(names, offset):
            if step_by is not None and not (isinstance(step_by, int) and step_by == 0):
                size, me = lax.axis_size(name), lax.axis_index(name)
                where[name] = lax.rem(me + size + step_by, size)
        return where

    last = lax.axis_index("gz") & 1
    first = 1 - last

    barrier = pltpu.get_barrier_semaphore()
    for dz in (2 * last - 1, 0, 2 * first - 1):
        for dx, dy in PLANE:
            if dx or dy or not isinstance(dz, int):
                pl.semaphore_signal(
                    barrier, inc=1, device_id=device_at((dx, dy, dz)), device_id_type=MESH
                )

    loads = [
        pltpu.make_async_copy(src, dst, load_sem.at[i])
        for i, (src, dst) in enumerate(
            (
                (shift_hbm, shift_ref),
                (position_hbm, position_ref),
                (bead_position_hbm, bead_position_ref),
                (velocity_hbm, velocity_ref),
                (bead_velocity_hbm, bead_velocity_ref),
                (bead_mass_hbm, bead_mass_ref),
                (rot_hbm, rot_ref),
                (leave_hbm, leave_ref),
                (count_hbm, count_ref),
                (table_hbm, table_ref),
            )
        )
    ]
    for copy in loads:
        copy.start()
    for copy in loads:
        copy.wait()

    def remote(src, dst, number, offset):
        return pltpu.make_async_remote_copy(
            src_ref=src,
            dst_ref=dst,
            send_sem=send_sem.at[number],
            recv_sem=recv_sem.at[number],
            device_id=device_at(offset),
            device_id_type=MESH,
        )

    def load(velocity, where, length):
        moving[0:3, pl.ds(where, length)] = velocity
        moving[3:4, pl.ds(where, length)] = jnp.ones((1, length), F32)
        moving[4:7, pl.ds(where, length)] = velocity
        moving[7:8, pl.ds(where, length)] = jnp.ones((1, length), F32)

    load(velocity_ref[...], 0, solvent)
    load(bead_velocity_ref[...], solvent, beads)
    weight[:, 0:solvent] = jnp.ones((1, solvent), F32)
    weight[:, solvent:count] = bead_mass_ref[...]

    def place(step, first, number):
        def body(i, carry):
            here = pl.ds(pl.multiple_of(i * CHUNK, CHUNK), CHUNK)
            coords = [position_ref[d, step : step + 1, here] for d in range(3)]
            column, layer = cell_rows(coords, shift_ref, step)
            cols[step, :, here] = column
            lays[step, :, here] = layer
            onehots[step, :, here] = one_hot(column)
            return carry

        lax.fori_loop(first, first + number, body, 0, unroll=number)

    def place_beads(step):
        here = pl.ds(solvent, beads)
        coords = [bead_position_ref[d, step : step + 1, :] for d in range(3)]
        column, layer = cell_rows(coords, shift_ref, step)
        cols[step, :, here] = column
        lays[step, :, here] = layer
        onehots[step, :, here] = one_hot(column)

    def deposit(step, here, moved):
        rows = deposit_rows(moved, weight[:, here], lays[step, :, here])
        if step == 0:
            totals[...] += lax.dot_general(
                rows, onehots[0, :, here], (((1,), (1,)), ((), ())), preferred_element_type=F32
            )
        else:
            totals[...] += jnp.dot(rows, turned_onehots[here, :], preferred_element_type=F32)

    lane = lanes_of((8, LANES))

    def own_axes(step):
        offset = [jnp.where(shift_ref[step, d] > 0, 1, 0) for d in range(3)]
        local = rows_of((LANES, WIDE))
        target = column_of(
            lax.shift_right_logical(local, 5) + offset[0], (local & 31) + offset[1]
        )
        spread = jnp.where(lanes_of((LANES, WIDE)) == target, 1.0, 0.0).astype(BF16)
        held = jnp.concatenate([rot_ref[step, x] for x in range(4)], axis=1)
        by_layer = jnp.dot(
            held.astype(F32).astype(BF16), spread, preferred_element_type=F32
        )
        above = jnp.concatenate([jnp.zeros((1, WIDE), F32), by_layer], axis=0)
        below = jnp.concatenate([by_layer, jnp.zeros((1, WIDE), F32)], axis=0)
        return jnp.where(offset[2] > 0, above, below)

    def exchange(step, between, early=None):
        axes = own_axes(step)
        row8w = rows_of((8, WIDE))
        row8 = rows_of((8, LANES))
        cells[:, :, COLUMNS:WIDE] = jnp.zeros((LAYERS, 8, WIDE - COLUMNS), F32)
        cells[17] = jnp.zeros((8, WIDE), F32)

        def settle(z):
            part = totals[8 * z : 8 * z + 8, :]
            cells[z, :, 0:COLUMNS] = part + pltpu.roll(part, 4, 0)
            cells[z] = jnp.where(row8w == 7, axes[z : z + 1], cells[z])

        settle(0)
        settle(16)

        def pack_end(side):
            near, far = cells[16 * side, :, 0:LANES], cells[16 * side, :, LANES:WIDE]
            edge = lanes_from(far, lane + 32 - 10 * row8)
            edge = jnp.where((lane >= 10 * row8) & (lane < 10 * row8 + 10), edge, 0.0)
            send_z[step, side, 2:3] = jnp.sum(edge, axis=0, keepdims=True)
            for at, tile in ((0, near), (3, far)):
                line = lanes_from(tile, lane & 31)
                line = jnp.where(lax.shift_right_logical(lane, 5) == (row8 & 3), line, 0.0)
                for half in range(2):
                    send_z[step, side, at + half : at + half + 1] = jnp.sum(
                        line[4 * half : 4 * half + 4], axis=0, keepdims=True
                    )
            send_z[step, side, 5:9] = near[0:4]
            send_z[step, side, 9:10] = near[7:8]

        plane_travels, end_travels = [], []

        def send(src, dst, number, offset):
            travel = remote(src, dst, len(OFFSETS) * step + number, offset)
            travel.start()
            return travel

        def send_end(side):
            for dx, dy in sorted(PLANE, key=lambda place: -abs(place[1])):
                if dy:
                    src = send_z.at[step, side, pl.ds(2, 1)]
                    dst = recv_edge.at[step, 1 - side, EDGES.index((-dx, -dy))]
                elif dx:
                    src = send_z.at[step, side, pl.ds(1 + dx, 3)]
                    dst = recv_line.at[step, 1 - side, (1 - dx) // 2]
                else:
                    src = send_z.at[step, side, pl.ds(2, 8)]
                    dst = recv_z.at[step, 1 - side]
                number = 9 * side + PLANE.index((dx, dy))
                end_travels.append(send(src, dst, number, (dx, dy, 2 * side - 1)))

        pack_end(last)
        if step == 0:
            pl.semaphore_wait(barrier, len(OFFSETS))
        send_end(last)
        pack_end(first)
        send_end(first)

        for z in range(1, 16):
            settle(z)
        for group in range(2):
            packed = jnp.zeros((8, LANES), F32)
            for j in range(9):
                z = 9 * group + j
                if z < 17:
                    turned = pltpu.roll(cells[z, :, LANES:WIDE], (12 * j - 32) % LANES, 1)
                    packed = jnp.where((lane >= 12 * j) & (lane < 12 * j + 10), turned, packed)
            send_y[step, group] = packed
        for dx in (-1, 0, 1):
            for dy in (-1, 1):
                back = EDGES.index((-dx, -dy))
                plane_travels.append(
                    send(
                        send_y.at[step],
                        recv_y.at[step, back],
                        OFFSETS.index((dx, dy, 0)),
                        (dx, dy, 0),
                    )
                )

        for group in range(6):
            packed_low = jnp.zeros((8, LANES), F32)
            packed_high = jnp.zeros((8, LANES), F32)
            for j in range(3):
                z = 3 * group + j
                if z < 17:
                    near, far = cells[z, :, 0:LANES], cells[z, :, LANES:WIDE]
                    face_low = jnp.where(lane < 32, near, far)
                    face_high = jnp.where(lane < 32, far, pltpu.roll(far, LANES - 4, 1))
                    if j:
                        face_low = pltpu.roll(face_low, 42 * j, 1)
                        face_high = pltpu.roll(face_high, 42 * j, 1)
                    inside = (lane >= 42 * j) & (lane < 42 * j + 38)
                    packed_low = jnp.where(inside, face_low, packed_low)
                    packed_high = jnp.where(inside, face_high, packed_high)
            send_x[step, 0, group] = packed_low
            send_x[step, 1, group] = packed_high
        for side in range(2):
            offset = (2 * side - 1, 0, 0)
            plane_travels.append(
                send(
                    send_x.at[step, side],
                    recv_x.at[step, 1 - side],
                    OFFSETS.index(offset),
                    offset,
                )
            )

        between()

        for travel in plane_travels:
            travel.wait()
        place12 = lax.rem(lane, 12)
        both_groups = []
        for group in range(2):
            both = jnp.zeros((8, LANES), F32)
            for k, edge in enumerate(EDGES):
                turn_by, chosen = moved_edge(edge, place12)
                both += jnp.where(chosen, pltpu.roll(recv_y[step, k, group], turn_by, 1), 0.0)
            both_groups.append(both)
        ends = (lane == 32) | (lane == 37)
        ends_high = (lane == 36) | (lane == 41)
        for group in range(6):
            for j in range(3):
                z = 3 * group + j
                if z < 17:
                    from_low, from_high = recv_x[step, 0, group], recv_x[step, 1, group]
                    if j:
                        from_low = pltpu.roll(from_low, LANES - 42 * j, 1)
                        from_high = pltpu.roll(from_high, LANES - 42 * j, 1)
                    shift_by = (32 - 12 * (z % 9)) % LANES
                    from_second = pltpu.roll(both_groups[z // 9], shift_by, 1)
                    cells[z, :, 0:LANES] += jnp.where(lane < 32, from_low, 0.0)
                    cells[z, :, LANES:WIDE] += (
                        jnp.where(
                            lane < 32,
                            from_high,
                            jnp.where(
                                ends,
                                from_low,
                                jnp.where(ends_high, pltpu.roll(from_high, 4, 1), 0.0),
                            ),
                        )
                        + jnp.where((lane >= 32) & (lane < 42), from_second, 0.0)
                    )

        def entry_of(z):
            full = cells[z]
            full = jnp.where((row8w >= 4) & (row8w < 7), pltpu.roll(full, 4, 0), full)
            mean = full / jnp.maximum(full[3:4], 1.0)
            rounded = mean.astype(BF16).astype(F32)
            entry = jnp.where(row8w < 4, rounded, mean - rounded)
            return jnp.where(row8w == 3, full[7:8], jnp.where(row8w == 7, 0.0, entry))

        def finish_pair(z):
            pair = jnp.concatenate([entry_of(z), entry_of(z + 1)], axis=0).astype(BF16)
            where = 8 * z if isinstance(z, int) else pl.multiple_of(8 * z, 16)
            results[pl.ds(where, 16), :] = pair[:, 0:COLUMNS]

        for z in range(2, 16, 2):
            finish_pair(z)

        def collect(side):
            for dx, dy in PLANE:
                if dy:
                    landed = recv_edge.at[step, side, EDGES.index((dx, dy))]
                elif dx:
                    landed = recv_line.at[step, side, (1 + dx) // 2]
                else:
                    landed = recv_z.at[step, side]
                number = len(OFFSETS) * step + 9 * (1 - side) + PLANE.index((-dx, -dy))
                remote(landed, landed, number, (0, 0, 1)).wait_recv()
            face = recv_z[step, side]
            lane1 = lanes_of((1, LANES))
            place10 = lax.rem(lane1, 10)
            edge = face[0:1]
            for k, offset in enumerate(EDGES):
                turn_by, chosen = moved_edge(offset, place10)
                edge += jnp.where(chosen, pltpu.roll(recv_edge[step, side, k], turn_by, 1), 0.0)
            low, high = recv_line[step, side, 0], recv_line[step, side, 1]
            at_low, at_high = (place10 == 0) | (place10 == 5), (place10 == 4) | (place10 == 9)
            edge += jnp.where(at_low, pltpu.roll(low[0:1], LANES - 4, 1), 0.0)
            edge += jnp.where(at_high, pltpu.roll(high[2:3], 4, 1), 0.0)
            edge = lanes_from(jnp.broadcast_to(edge, (8, LANES)), lane - 32 + 10 * row8)
            lines = []
            for line in (low[1:3], face[1:3] + high[0:2]):
                wide = jnp.where(row8 < 4, line[0:1], line[1:2])
                lines.append(lanes_from(wide, (lane & 31) + 32 * (row8 & 3)))
            rest = jnp.where(row8 == 7, face, pltpu.roll(face, 5, 0))
            near = rest + jnp.where(lane < 32, lines[0], 0.0)
            far = jnp.where(lane < 32, lines[1], jnp.where(lane < 42, edge, 0.0))
            cells[16 * side, :, 0:LANES] += near
            cells[16 * side, :, LANES:WIDE] += far
            finish_pair(16 * side)

        collect(first)
        if early is not None:
            finish_pair(16 * last)
            early()
        collect(last)
        for travel in end_travels:
            travel.wait_send()

    tables = [table_ref[c] for c in range(3)]

    def gather_collide(step, here):
        gathered = jnp.dot(results[...], onehots[step, :, here], preferred_element_type=F32)
        return collide(moving[:, here], lays[step, :, here], gathered, tables)

    solvent_chunks = solvent // CHUNK
    totals[...] = jnp.zeros_like(totals)
    place(0, 0, solvent_chunks)
    place_beads(0)

    def first_deposit(i, carry):
        here = pl.ds(pl.multiple_of(i * CHUNK, CHUNK), CHUNK)
        deposit(0, here, moving[:, here])
        return carry

    lax.fori_loop(0, chunks, first_deposit, 0, unroll=chunks)

    def between_first():
        place(1, 0, solvent_chunks)
        place_beads(1)

        def transpose(i, carry):
            here = pl.ds(pl.multiple_of(i * CHUNK, CHUNK), CHUNK)
            turned_onehots[here, :] = onehots[1, :, here].T
            return carry

        lax.fori_loop(0, chunks, transpose, 0, unroll=chunks)

    exchange(0, between_first)

    totals[...] = jnp.zeros_like(totals)

    def turn(i, carry):
        here = pl.ds(pl.multiple_of(i * CHUNK, CHUNK), CHUNK)
        moved = gather_collide(0, here)
        moving[:, here] = moved
        deposit(1, here, moved)
        return carry

    lax.fori_loop(0, chunks, turn, 0, unroll=chunks)

    tiles = solvent // LANES

    def between_second():
        row8 = rows_of((8, LANES))

        def fill(i, carry):
            parts = []
            for k in range(2):
                here = pl.ds(pl.multiple_of((2 * i + k) * LANES, LANES), LANES)
                now = moving[:, here]
                rounded = now.astype(BF16).astype(F32)
                entry = jnp.where(row8 < 4, rounded, now - rounded)
                entry = jnp.where(row8 == 3, cols[1, :, here].astype(F32), entry)
                parts.append(jnp.where(row8 == 7, lays[1, :, here].astype(F32), entry))
            leave_table[pl.ds(pl.multiple_of(16 * i, 16), 16), :] = jnp.concatenate(
                parts, axis=0
            ).astype(BF16)
            return carry

        lax.fori_loop(0, tiles // 2, fill, 0, unroll=8)

        def pick(d, carry):
            for side in range(2):
                index = jnp.maximum(leave_ref[d, side : side + 1, :], 0)
                offset = (index & (LANES - 1)).astype(F32)
                rest = (offset - rows_of((16, CAP)).astype(F32)).astype(BF16)
                one, zero = jnp.ones((16, CAP), BF16), jnp.zeros((16, CAP), BF16)
                spot = jnp.concatenate(
                    [jnp.where(rest == float(16 * j), one, zero) for j in range(8)], axis=0
                )
                found = jnp.dot(leave_table[...], spot, preferred_element_type=F32)
                tile = lax.shift_right_logical(index, 7)
                chosen = found[0:8]
                for i in range(1, tiles):
                    chosen = jnp.where(tile == i, found[8 * i : 8 * i + 8], chosen)
                leave_moving[d, side] = chosen + pltpu.roll(chosen, 4, 0)
                leave_layer[d, side] = chosen[7:8].astype(I32)
                leave_column[d, side] = chosen[3:4]
                leave_onehot[d, side] = one_hot(chosen[3:4].astype(I32))
            return carry

        lax.fori_loop(0, 3, pick, 0, unroll=3)

    row8 = rows_of((8, CAP))
    slot = lanes_of((8, CAP))

    def leave_number(d, side):
        return 2 * len(OFFSETS) + 2 * d + side

    def send_leaving(src, dst, number, d, side):
        offset = tuple(2 * side - 1 if axis == d else None for axis in range(3))
        travel = remote(src, dst, number, offset)
        travel.start()
        return travel

    def leave(d, side):
        gathered = jnp.dot(results[...], leave_onehot[d, side], preferred_element_type=F32)
        moved = collide(leave_moving[d, side], leave_layer[d, side], gathered, tables)
        leave_send[d, side] = jnp.where(slot < count_ref[side, d], moved, 0.0)
        return send_leaving(
            leave_send.at[d, side], leave_recv.at[d, 1 - side], leave_number(d, side), d, side
        )

    travels = []

    def ahead():
        shared = jnp.broadcast_to(leave_layer[2, last], (8, CAP)) == 16 * last
        shared &= slot < count_ref[last, 2]
        mark = jnp.where(shared, leave_column[2, last], -1.0)
        ahead_send[...] = jnp.where(row8 == 3, mark, leave_moving[2, last])
        travels.append(send_leaving(ahead_send, ahead_recv, 2 * len(OFFSETS) + 6, 2, last))

    def between_all():
        between_second()
        ahead()

    exchange(1, between_all, lambda: travels.append(leave(2, last)))
    for d, side in ((0, 0), (0, 1), (2, first), (1, 0), (1, 1)):
        travels.append(leave(d, side))

    def finish(i, carry):
        here = pl.ds(pl.multiple_of(i * CHUNK, CHUNK), CHUNK)
        velocity_out[:, here] = gather_collide(1, here)[0:3]
        return carry

    lax.fori_loop(0, solvent_chunks, finish, 0, unroll=solvent_chunks)
    bead_out[...] = gather_collide(1, pl.ds(solvent, beads))[0:3]

    remote(ahead_recv, ahead_recv, 2 * len(OFFSETS) + 6, (0, 0, 1)).wait_recv()
    got = ahead_recv[...]
    mark = got[3:4]
    shared = jnp.dot(
        results[pl.ds(pl.multiple_of(128 * last, 16), 16), :],
        one_hot(mark.astype(I32)),
        preferred_element_type=F32,
    )
    got = rotate(got, shared[0:8], tables)
    arrived = leave_recv.at[2, last]
    remote(arrived, arrived, leave_number(2, first), (0, 0, 1)).wait_recv()
    got = jnp.where(mark >= 0.0, got, leave_recv[2, last])
    arrived = leave_recv.at[2, first]
    remote(arrived, arrived, leave_number(2, last), (0, 0, 1)).wait_recv()
    for side in range(2):
        arrivals_out[2, :, side, :] = jnp.where(last == side, got, leave_recv[2, side])[0:3]
    for d in range(2):
        for side in range(2):
            arrived = leave_recv.at[d, side]
            remote(arrived, arrived, leave_number(d, 1 - side), (0, 0, 1)).wait_recv()
            arrivals_out[d, :, side, :] = leave_recv[d, side, 0:3, :]
    for travel in travels:
        travel.wait_send()


def write(*refs):
    sems = refs[-1]
    count = len(refs) // 2
    copies = [
        pltpu.make_async_copy(refs[i], refs[count + i], sems.at[i]) for i in range(count)
    ]
    for copy in copies:
        copy.start()
    for copy in copies:
        copy.wait()


def per_device(
    velocity, position, bead_velocity, bead_mass, bead_position, grid_shift, rot_axis,
    leave_count, leave_index,
):
    solvent, beads = velocity.shape[1], bead_velocity.shape[1]
    count = solvent + beads
    vmem = pl.BlockSpec(memory_space=pltpu.VMEM)
    velocity_out, bead_out, arrivals = pl.pallas_call(
        kernel,
        out_shape=(
            pltpu.VMEM((3, solvent), F32),
            pltpu.VMEM((3, beads), F32),
            pltpu.VMEM((3, 3, 2, CAP), F32),
        ),
        in_specs=[pl.BlockSpec(memory_space=pltpu.HBM)] * 10,
        out_specs=(vmem, vmem, vmem),
        scratch_shapes=[
            pltpu.SMEM((2, 3), I32),
            pltpu.SMEM((2, 3), I32),
            pltpu.VMEM((3, solvent), F32),
            pltpu.VMEM((3, 2, solvent), I32),
            pltpu.VMEM((3, beads), F32),
            pltpu.VMEM((1, beads), F32),
            pltpu.VMEM((3, 2, beads), I32),
            pltpu.VMEM((2, 4, 16, 32), I32),
            pltpu.VMEM((3, 2, CAP), I32),
            pltpu.VMEM((3, 8, LANES), F32),
            pltpu.SemaphoreType.DMA((10,)),
            pltpu.VMEM((8, count), F32),
            pltpu.VMEM((1, count), F32),
            pltpu.VMEM((2, 1, count), I32),
            pltpu.VMEM((2, 1, count), I32),
            pltpu.VMEM((2, COLUMNS, count), BF16),
            pltpu.VMEM((count, COLUMNS), BF16),
            pltpu.VMEM((8 * LAYERS, COLUMNS), F32),
            pltpu.VMEM((LAYERS, 8, WIDE), F32),
            pltpu.VMEM((8 * LAYERS, COLUMNS), BF16),
            pltpu.VMEM((2, 2, 16, LANES), F32),
            pltpu.VMEM((2, 2, 8, LANES), F32),
            pltpu.VMEM((2, 2, 6, 8, LANES), F32),
            pltpu.VMEM((2, 2, 6, 1, LANES), F32),
            pltpu.VMEM((2, 2, 2, 3, LANES), F32),
            pltpu.VMEM((2, 2, 8, LANES), F32),
            pltpu.VMEM((2, 6, 2, 8, LANES), F32),
            pltpu.VMEM((2, 2, 6, 8, LANES), F32),
            pltpu.VMEM((8 * solvent // LANES, LANES), BF16),
            pltpu.VMEM((3, 2, 8, CAP), F32),
            pltpu.VMEM((3, 2, 1, CAP), I32),
            pltpu.VMEM((3, 2, 1, CAP), F32),
            pltpu.VMEM((3, 2, COLUMNS, CAP), BF16),
            pltpu.VMEM((3, 2, 8, CAP), F32),
            pltpu.VMEM((3, 2, 8, CAP), F32),
            pltpu.VMEM((8, CAP), F32),
            pltpu.VMEM((8, CAP), F32),
            pltpu.SemaphoreType.DMA((2 * len(OFFSETS) + 7,)),
            pltpu.SemaphoreType.DMA((2 * len(OFFSETS) + 7,)),
        ],
        compiler_params=pltpu.CompilerParams(
            collective_id=0, has_side_effects=True, vmem_limit_bytes=62 * 1024 * 1024
        ),
        cost_estimate=pl.CostEstimate(flops=10**9, bytes_accessed=10**6, transcendentals=0),
        name="collisions",
    )(
        grid_shift,
        leave_count.reshape(3, 2).T,
        velocity,
        jnp.transpose(position, (1, 0, 2)),
        bead_velocity,
        bead_mass.reshape(1, beads),
        jnp.transpose(bead_position, (1, 0, 2)),
        jnp.swapaxes(rot_axis, 2, 3),
        leave_index,
        jnp.asarray(rotation_table()),
    )
    made = (velocity_out, bead_out, arrivals)
    velocity_out, bead_out, arrivals = pl.pallas_call(
        write,
        out_shape=tuple(jax.ShapeDtypeStruct(x.shape, x.dtype) for x in made),
        in_specs=[vmem] * 3,
        out_specs=(pl.BlockSpec(memory_space=pltpu.HBM),) * 3,
        scratch_shapes=[pltpu.SemaphoreType.DMA((3,))],
        compiler_params=pltpu.CompilerParams(vmem_limit_bytes=4 * 1024 * 1024),
        name="write_results",
    )(*made)
    return velocity_out, bead_out, jnp.transpose(arrivals, (0, 2, 1, 3))


def solution(mesh):
    return jax.shard_map(
        per_device,
        mesh=mesh,
        in_specs=(
            P(None, ("gx", "gy", "gz")),
            P(None, None, ("gx", "gy", "gz")),
            P(None, ("gx", "gy", "gz")),
            P(("gx", "gy", "gz")),
            P(None, None, ("gx", "gy", "gz")),
            P(),
            P(None, "gx", "gy", "gz"),
            P(None, None, ("gx", "gy", "gz")),
            P(None, None, ("gx", "gy", "gz")),
        ),
        out_specs=(
            P(None, ("gx", "gy", "gz")),
            P(None, ("gx", "gy", "gz")),
            P(None, None, None, ("gx", "gy", "gz")),
        ),
        check_vma=False,
    )
```

```python
import math

import jax
import jax.numpy as jnp
import numpy as np
from jax import lax
from jax.experimental import pallas as pl
from jax.experimental.pallas import tpu as pltpu
from jax.sharding import PartitionSpec as P

STEPS = 2
AXES = 64
CAP = 256
COSINE = math.cos(130.0 * math.pi / 180.0)
SINE = math.sin(130.0 * math.pi / 180.0)
GOLDEN = math.pi * (3.0 - math.sqrt(5.0))

LANES = 128
CHUNK = 1024
COLUMNS = 176
LAYERS = 18
WIDE = 256
MESH = pl.DeviceIdType.MESH
F32 = jnp.float32
BF16 = jnp.bfloat16
I32 = jnp.int32


def rotation_table():
    ordinal = np.arange(AXES) + 0.5
    height = 1.0 - 2.0 * ordinal / AXES
    radius = np.sqrt(1.0 - height * height)
    n = np.stack([radius * np.cos(ordinal * GOLDEN), radius * np.sin(ordinal * GOLDEN), height])
    zero = np.zeros(AXES)
    skew = np.array([[zero, -n[2], n[1]], [n[2], zero, -n[0]], [-n[1], n[0], zero]])
    matrix = COSINE * np.eye(3)[:, :, None] + SINE * skew + (1.0 - COSINE) * n[:, None] * n[None]
    table = np.zeros((3, 8, LANES), np.float32)
    for c in range(3):
        table[c, 0:3, :AXES] = matrix[:, c]
        table[c, 4:7, :AXES] = matrix[:, c]
    return table


PLANE = [(dx, dy) for dx in (-1, 0, 1) for dy in (-1, 0, 1)]
OFFSETS = [(dx, dy, dz) for dz in (-1, 1) for dx, dy in PLANE] + [
    (dx, dy, 0) for dx, dy in PLANE if (dx, dy) != (0, 0)
]
EDGES = [(dx, dy) for dx in (-1, 0, 1) for dy in (-1, 1)]


def moved_edge(edge, place):
    dx, dy = edge
    target = {1: 0, -1: 5}[dy] + (4 if dx == 1 else 0)
    source = {1: 5, -1: 0}[dy] + (4 if dx == -1 else 0)
    if dx == 0:
        chosen = (place >= target) & (place < target + 5)
    else:
        chosen = place == target
    return (target - source) % LANES, chosen


def rows_of(shape):
    return lax.broadcasted_iota(I32, shape, 0)


def lanes_of(shape):
    return lax.broadcasted_iota(I32, shape, 1)


def lanes_from(tile, source):
    return jnp.take_along_axis(tile, source & (LANES - 1), axis=1)


def cell_rows(coords, shift_ref, step):
    layer = []
    for d in range(3):
        shift = shift_ref[step, d]
        offset = jnp.where(shift > 0, 1, 0)
        layer.append(lax.shift_right_arithmetic(coords[d] - shift, 4) + offset)
    return column_of(layer[0], layer[1]), layer[2]


def column_of(first, second):
    inner = first * 32 + second
    return jnp.where(second == 32, first + 160, jnp.where(second == 0, first + 165, inner))


def one_hot(column):
    n = column.shape[1]
    rest = column.astype(F32) - rows_of((16, n)).astype(F32)
    rest = rest.astype(BF16)
    one, zero = jnp.ones((16, n), BF16), jnp.zeros((16, n), BF16)
    return jnp.concatenate(
        [jnp.where(rest == float(16 * j), one, zero) for j in range(COLUMNS // 16)], axis=0
    )


def deposit_rows(moving, weight, layer):
    n = moving.shape[1]
    row8 = rows_of((8, n))
    summand = moving * weight
    high = summand.astype(BF16).astype(F32)
    parts = jnp.where(row8 < 4, high, summand - high)
    parts = jnp.concatenate([parts, parts], axis=0).astype(BF16)
    half = lax.shift_right_logical(rows_of((16, n)), 3)
    rest = (layer - half).astype(F32).astype(BF16)
    zero = jnp.zeros((16, n), BF16)
    return jnp.concatenate(
        [jnp.where(rest == float(2 * j), parts, zero) for j in range(LAYERS // 2)], axis=0
    )


def collide(moving, layer, gathered, tables):
    found = [gathered[8 * z : 8 * z + 8] for z in range(17)]
    top = found.pop()
    wide = jnp.broadcast_to(layer, (8, layer.shape[1]))
    for bit in range(4):
        odd = (wide & (1 << bit)) != 0
        found = [jnp.where(odd, found[z + 1], found[z]) for z in range(0, len(found), 2)]
    chosen = jnp.where(wide == 16, top, found[0])
    return rotate(moving, chosen, tables)


def rotate(moving, chosen, tables):
    n = moving.shape[1]
    mean = chosen + pltpu.roll(chosen, 4, 0)
    axis = jnp.broadcast_to(mean[3:4], (8, n)).astype(I32)
    relative = moving - mean
    result = mean
    for c in range(3):
        columns = jnp.concatenate(
            [
                jnp.take_along_axis(tables[c], axis[:, i : i + LANES], axis=1)
                for i in range(0, n, LANES)
            ],
            axis=1,
        )
        result = result + columns * relative[c : c + 1]
    row8 = rows_of((8, n))
    return jnp.where((row8 & 3) == 3, 1.0, result)


def kernel(
    shift_hbm, count_hbm, velocity_hbm, position_hbm, bead_velocity_hbm, bead_mass_hbm,
    bead_position_hbm, rot_hbm, leave_hbm, table_hbm,
    velocity_out, bead_out, arrivals_out,
    shift_ref, count_ref, velocity_ref, position_ref, bead_velocity_ref, bead_mass_ref,
    bead_position_ref, rot_ref, leave_ref, table_ref, load_sem,
    moving, weight, cols, lays, onehots, turned_onehots, totals, cells, results,
    send_z, send_y, send_x, recv_edge, recv_line, recv_z, recv_y, recv_x,
    leave_table, leave_moving, leave_layer, leave_column, leave_onehot, leave_send, leave_recv,
    ahead_send, ahead_recv,
    send_sem, recv_sem,
):
    solvent = velocity_ref.shape[1]
    beads = bead_velocity_ref.shape[1]
    count = solvent + beads
    chunks = count // CHUNK

    names = ("gx", "gy", "gz")

    def device_at(offset):
        where = {}
        for name, step_by in zip(names, offset):
            if step_by is not None and not (isinstance(step_by, int) and step_by == 0):
                size, me = lax.axis_size(name), lax.axis_index(name)
                where[name] = lax.rem(me + size + step_by, size)
        return where

    last = lax.axis_index("gz") & 1
    first = 1 - last

    barrier = pltpu.get_barrier_semaphore()
    for dz in (2 * last - 1, 0, 2 * first - 1):
        for dx, dy in PLANE:
            if dx or dy or not isinstance(dz, int):
                pl.semaphore_signal(
                    barrier, inc=1, device_id=device_at((dx, dy, dz)), device_id_type=MESH
                )

    loads = [
        pltpu.make_async_copy(src, dst, load_sem.at[i])
        for i, (src, dst) in enumerate(
            (
                (shift_hbm, shift_ref),
                (position_hbm, position_ref),
                (bead_position_hbm, bead_position_ref),
                (velocity_hbm, velocity_ref),
                (bead_velocity_hbm, bead_velocity_ref),
                (bead_mass_hbm, bead_mass_ref),
                (rot_hbm, rot_ref),
                (leave_hbm, leave_ref),
                (count_hbm, count_ref),
                (table_hbm, table_ref),
            )
        )
    ]
    for copy in loads:
        copy.start()
    for copy in loads:
        copy.wait()

    def remote(src, dst, number, offset):
        return pltpu.make_async_remote_copy(
            src_ref=src,
            dst_ref=dst,
            send_sem=send_sem.at[number],
            recv_sem=recv_sem.at[number],
            device_id=device_at(offset),
            device_id_type=MESH,
        )

    def load(velocity, where, length):
        moving[0:3, pl.ds(where, length)] = velocity
        moving[3:4, pl.ds(where, length)] = jnp.ones((1, length), F32)
        moving[4:7, pl.ds(where, length)] = velocity
        moving[7:8, pl.ds(where, length)] = jnp.ones((1, length), F32)

    load(velocity_ref[...], 0, solvent)
    load(bead_velocity_ref[...], solvent, beads)
    weight[:, 0:solvent] = jnp.ones((1, solvent), F32)
    weight[:, solvent:count] = bead_mass_ref[...]

    def place(step, first, number):
        def body(i, carry):
            here = pl.ds(pl.multiple_of(i * CHUNK, CHUNK), CHUNK)
            coords = [position_ref[d, step : step + 1, here] for d in range(3)]
            column, layer = cell_rows(coords, shift_ref, step)
            cols[step, :, here] = column
            lays[step, :, here] = layer
            onehots[step, :, here] = one_hot(column)
            return carry

        lax.fori_loop(first, first + number, body, 0, unroll=number)

    def place_beads(step):
        here = pl.ds(solvent, beads)
        coords = [bead_position_ref[d, step : step + 1, :] for d in range(3)]
        column, layer = cell_rows(coords, shift_ref, step)
        cols[step, :, here] = column
        lays[step, :, here] = layer
        onehots[step, :, here] = one_hot(column)

    def deposit(step, here, moved):
        rows = deposit_rows(moved, weight[:, here], lays[step, :, here])
        if step == 0:
            totals[...] += lax.dot_general(
                rows, onehots[0, :, here], (((1,), (1,)), ((), ())), preferred_element_type=F32
            )
        else:
            totals[...] += jnp.dot(rows, turned_onehots[here, :], preferred_element_type=F32)

    lane = lanes_of((8, LANES))

    def own_axes(step):
        offset = [jnp.where(shift_ref[step, d] > 0, 1, 0) for d in range(3)]
        local = rows_of((LANES, WIDE))
        target = column_of(
            lax.shift_right_logical(local, 5) + offset[0], (local & 31) + offset[1]
        )
        spread = jnp.where(lanes_of((LANES, WIDE)) == target, 1.0, 0.0).astype(BF16)
        held = jnp.concatenate([rot_ref[step, x] for x in range(4)], axis=1)
        by_layer = jnp.dot(
            held.astype(F32).astype(BF16), spread, preferred_element_type=F32
        )
        above = jnp.concatenate([jnp.zeros((1, WIDE), F32), by_layer], axis=0)
        below = jnp.concatenate([by_layer, jnp.zeros((1, WIDE), F32)], axis=0)
        return jnp.where(offset[2] > 0, above, below)

    def exchange(step, between, early=None):
        axes = own_axes(step)
        row8w = rows_of((8, WIDE))
        row8 = rows_of((8, LANES))
        cells[:, :, COLUMNS:WIDE] = jnp.zeros((LAYERS, 8, WIDE - COLUMNS), F32)
        cells[17] = jnp.zeros((8, WIDE), F32)

        def settle(z):
            part = totals[8 * z : 8 * z + 8, :]
            cells[z, :, 0:COLUMNS] = part + pltpu.roll(part, 4, 0)
            cells[z] = jnp.where(row8w == 7, axes[z : z + 1], cells[z])

        settle(0)
        settle(16)

        def pack_end(side):
            near, far = cells[16 * side, :, 0:LANES], cells[16 * side, :, LANES:WIDE]
            edge = lanes_from(far, lane + 32 - 10 * row8)
            edge = jnp.where((lane >= 10 * row8) & (lane < 10 * row8 + 10), edge, 0.0)
            send_z[step, side, 2:3] = jnp.sum(edge, axis=0, keepdims=True)
            for at, tile in ((0, near), (3, far)):
                line = lanes_from(tile, lane & 31)
                line = jnp.where(lax.shift_right_logical(lane, 5) == (row8 & 3), line, 0.0)
                for half in range(2):
                    send_z[step, side, at + half : at + half + 1] = jnp.sum(
                        line[4 * half : 4 * half + 4], axis=0, keepdims=True
                    )
            send_z[step, side, 5:9] = near[0:4]
            send_z[step, side, 9:10] = near[7:8]

        plane_travels, end_travels = [], []

        def send(src, dst, number, offset):
            travel = remote(src, dst, len(OFFSETS) * step + number, offset)
            travel.start()
            return travel

        def send_end(side):
            for dx, dy in sorted(PLANE, key=lambda place: -abs(place[1])):
                if dy:
                    src = send_z.at[step, side, pl.ds(2, 1)]
                    dst = recv_edge.at[step, 1 - side, EDGES.index((-dx, -dy))]
                elif dx:
                    src = send_z.at[step, side, pl.ds(1 + dx, 3)]
                    dst = recv_line.at[step, 1 - side, (1 - dx) // 2]
                else:
                    src = send_z.at[step, side, pl.ds(2, 8)]
                    dst = recv_z.at[step, 1 - side]
                number = 9 * side + PLANE.index((dx, dy))
                end_travels.append(send(src, dst, number, (dx, dy, 2 * side - 1)))

        pack_end(last)
        if step == 0:
            pl.semaphore_wait(barrier, len(OFFSETS))
        send_end(last)
        pack_end(first)
        send_end(first)

        for z in range(1, 16):
            settle(z)
        for group in range(2):
            packed = jnp.zeros((8, LANES), F32)
            for j in range(9):
                z = 9 * group + j
                if z < 17:
                    turned = pltpu.roll(cells[z, :, LANES:WIDE], (12 * j - 32) % LANES, 1)
                    packed = jnp.where((lane >= 12 * j) & (lane < 12 * j + 10), turned, packed)
            send_y[step, group] = packed
        for dx in (-1, 0, 1):
            for dy in (-1, 1):
                back = EDGES.index((-dx, -dy))
                plane_travels.append(
                    send(
                        send_y.at[step],
                        recv_y.at[step, back],
                        OFFSETS.index((dx, dy, 0)),
                        (dx, dy, 0),
                    )
                )

        for group in range(6):
            packed_low = jnp.zeros((8, LANES), F32)
            packed_high = jnp.zeros((8, LANES), F32)
            for j in range(3):
                z = 3 * group + j
                if z < 17:
                    near, far = cells[z, :, 0:LANES], cells[z, :, LANES:WIDE]
                    face_low = jnp.where(lane < 32, near, far)
                    face_high = jnp.where(lane < 32, far, pltpu.roll(far, LANES - 4, 1))
                    if j:
                        face_low = pltpu.roll(face_low, 42 * j, 1)
                        face_high = pltpu.roll(face_high, 42 * j, 1)
                    inside = (lane >= 42 * j) & (lane < 42 * j + 38)
                    packed_low = jnp.where(inside, face_low, packed_low)
                    packed_high = jnp.where(inside, face_high, packed_high)
            send_x[step, 0, group] = packed_low
            send_x[step, 1, group] = packed_high
        for side in range(2):
            offset = (2 * side - 1, 0, 0)
            plane_travels.append(
                send(
                    send_x.at[step, side],
                    recv_x.at[step, 1 - side],
                    OFFSETS.index(offset),
                    offset,
                )
            )

        between()

        for travel in plane_travels:
            travel.wait()
        place12 = lax.rem(lane, 12)
        both_groups = []
        for group in range(2):
            both = jnp.zeros((8, LANES), F32)
            for k, edge in enumerate(EDGES):
                turn_by, chosen = moved_edge(edge, place12)
                both += jnp.where(chosen, pltpu.roll(recv_y[step, k, group], turn_by, 1), 0.0)
            both_groups.append(both)
        ends = (lane == 32) | (lane == 37)
        ends_high = (lane == 36) | (lane == 41)
        for group in range(6):
            for j in range(3):
                z = 3 * group + j
                if z < 17:
                    from_low, from_high = recv_x[step, 0, group], recv_x[step, 1, group]
                    if j:
                        from_low = pltpu.roll(from_low, LANES - 42 * j, 1)
                        from_high = pltpu.roll(from_high, LANES - 42 * j, 1)
                    shift_by = (32 - 12 * (z % 9)) % LANES
                    from_second = pltpu.roll(both_groups[z // 9], shift_by, 1)
                    cells[z, :, 0:LANES] += jnp.where(lane < 32, from_low, 0.0)
                    cells[z, :, LANES:WIDE] += (
                        jnp.where(
                            lane < 32,
                            from_high,
                            jnp.where(
                                ends,
                                from_low,
                                jnp.where(ends_high, pltpu.roll(from_high, 4, 1), 0.0),
                            ),
                        )
                        + jnp.where((lane >= 32) & (lane < 42), from_second, 0.0)
                    )

        def entry_of(z):
            full = cells[z]
            full = jnp.where((row8w >= 4) & (row8w < 7), pltpu.roll(full, 4, 0), full)
            mean = full / jnp.maximum(full[3:4], 1.0)
            rounded = mean.astype(BF16).astype(F32)
            entry = jnp.where(row8w < 4, rounded, mean - rounded)
            return jnp.where(row8w == 3, full[7:8], jnp.where(row8w == 7, 0.0, entry))

        def finish_pair(z):
            pair = jnp.concatenate([entry_of(z), entry_of(z + 1)], axis=0).astype(BF16)
            where = 8 * z if isinstance(z, int) else pl.multiple_of(8 * z, 16)
            results[pl.ds(where, 16), :] = pair[:, 0:COLUMNS]

        for z in range(2, 16, 2):
            finish_pair(z)

        def collect(side):
            for dx, dy in PLANE:
                if dy:
                    landed = recv_edge.at[step, side, EDGES.index((dx, dy))]
                elif dx:
                    landed = recv_line.at[step, side, (1 + dx) // 2]
                else:
                    landed = recv_z.at[step, side]
                number = len(OFFSETS) * step + 9 * (1 - side) + PLANE.index((-dx, -dy))
                remote(landed, landed, number, (0, 0, 1)).wait_recv()
            face = recv_z[step, side]
            lane1 = lanes_of((1, LANES))
            place10 = lax.rem(lane1, 10)
            edge = face[0:1]
            for k, offset in enumerate(EDGES):
                turn_by, chosen = moved_edge(offset, place10)
                edge += jnp.where(chosen, pltpu.roll(recv_edge[step, side, k], turn_by, 1), 0.0)
            low, high = recv_line[step, side, 0], recv_line[step, side, 1]
            at_low, at_high = (place10 == 0) | (place10 == 5), (place10 == 4) | (place10 == 9)
            edge += jnp.where(at_low, pltpu.roll(low[0:1], LANES - 4, 1), 0.0)
            edge += jnp.where(at_high, pltpu.roll(high[2:3], 4, 1), 0.0)
            edge = lanes_from(jnp.broadcast_to(edge, (8, LANES)), lane - 32 + 10 * row8)
            lines = []
            for line in (low[1:3], face[1:3] + high[0:2]):
                wide = jnp.where(row8 < 4, line[0:1], line[1:2])
                lines.append(lanes_from(wide, (lane & 31) + 32 * (row8 & 3)))
            rest = jnp.where(row8 == 7, face, pltpu.roll(face, 5, 0))
            near = rest + jnp.where(lane < 32, lines[0], 0.0)
            far = jnp.where(lane < 32, lines[1], jnp.where(lane < 42, edge, 0.0))
            cells[16 * side, :, 0:LANES] += near
            cells[16 * side, :, LANES:WIDE] += far
            finish_pair(16 * side)

        collect(first)
        if early is not None:
            finish_pair(16 * last)
            early()
        collect(last)
        for travel in end_travels:
            travel.wait_send()

    tables = [table_ref[c] for c in range(3)]

    def gather_collide(step, here):
        gathered = jnp.dot(results[...], onehots[step, :, here], preferred_element_type=F32)
        return collide(moving[:, here], lays[step, :, here], gathered, tables)

    solvent_chunks = solvent // CHUNK
    totals[...] = jnp.zeros_like(totals)
    place(0, 0, solvent_chunks)
    place_beads(0)

    def first_deposit(i, carry):
        here = pl.ds(pl.multiple_of(i * CHUNK, CHUNK), CHUNK)
        deposit(0, here, moving[:, here])
        return carry

    lax.fori_loop(0, chunks, first_deposit, 0, unroll=chunks)

    def between_first():
        place(1, 0, solvent_chunks)
        place_beads(1)

        def transpose(i, carry):
            here = pl.ds(pl.multiple_of(i * CHUNK, CHUNK), CHUNK)
            turned_onehots[here, :] = onehots[1, :, here].T
            return carry

        lax.fori_loop(0, chunks, transpose, 0, unroll=chunks)

    exchange(0, between_first)

    totals[...] = jnp.zeros_like(totals)

    def turn(i, carry):
        here = pl.ds(pl.multiple_of(i * CHUNK, CHUNK), CHUNK)
        moved = gather_collide(0, here)
        moving[:, here] = moved
        deposit(1, here, moved)
        return carry

    lax.fori_loop(0, chunks, turn, 0, unroll=chunks)

    tiles = solvent // LANES

    def between_second():
        row8 = rows_of((8, LANES))

        def fill(i, carry):
            parts = []
            for k in range(2):
                here = pl.ds(pl.multiple_of((2 * i + k) * LANES, LANES), LANES)
                now = moving[:, here]
                rounded = now.astype(BF16).astype(F32)
                entry = jnp.where(row8 < 4, rounded, now - rounded)
                entry = jnp.where(row8 == 3, cols[1, :, here].astype(F32), entry)
                parts.append(jnp.where(row8 == 7, lays[1, :, here].astype(F32), entry))
            leave_table[pl.ds(pl.multiple_of(16 * i, 16), 16), :] = jnp.concatenate(
                parts, axis=0
            ).astype(BF16)
            return carry

        lax.fori_loop(0, tiles // 2, fill, 0, unroll=8)

        def pick(d, carry):
            for side in range(2):
                index = jnp.maximum(leave_ref[d, side : side + 1, :], 0)
                offset = (index & (LANES - 1)).astype(F32)
                rest = (offset - rows_of((16, CAP)).astype(F32)).astype(BF16)
                one, zero = jnp.ones((16, CAP), BF16), jnp.zeros((16, CAP), BF16)
                spot = jnp.concatenate(
                    [jnp.where(rest == float(16 * j), one, zero) for j in range(8)], axis=0
                )
                found = jnp.dot(leave_table[...], spot, preferred_element_type=F32)
                tile = lax.shift_right_logical(index, 7)
                chosen = found[0:8]
                for i in range(1, tiles):
                    chosen = jnp.where(tile == i, found[8 * i : 8 * i + 8], chosen)
                leave_moving[d, side] = chosen + pltpu.roll(chosen, 4, 0)
                leave_layer[d, side] = chosen[7:8].astype(I32)
                leave_column[d, side] = chosen[3:4]
                leave_onehot[d, side] = one_hot(chosen[3:4].astype(I32))
            return carry

        lax.fori_loop(0, 3, pick, 0, unroll=3)

    row8 = rows_of((8, CAP))
    slot = lanes_of((8, CAP))

    def leave_number(d, side):
        return 2 * len(OFFSETS) + 2 * d + side

    def send_leaving(src, dst, number, d, side):
        offset = tuple(2 * side - 1 if axis == d else None for axis in range(3))
        travel = remote(src, dst, number, offset)
        travel.start()
        return travel

    travels = []

    def leave(*faces):
        found = [
            jnp.dot(results[...], leave_onehot[face], preferred_element_type=F32)
            for face in faces
        ]
        for (d, side), gathered in zip(faces, found):
            moved = collide(leave_moving[d, side], leave_layer[d, side], gathered, tables)
            leave_send[d, side] = jnp.where(slot < count_ref[side, d], moved, 0.0)
        for d, side in faces:
            travels.append(
                send_leaving(
                    leave_send.at[d, side],
                    leave_recv.at[d, 1 - side],
                    leave_number(d, side),
                    d,
                    side,
                )
            )

    def ahead():
        shared = jnp.broadcast_to(leave_layer[2, last], (8, CAP)) == 16 * last
        shared &= slot < count_ref[last, 2]
        mark = jnp.where(shared, leave_column[2, last], -1.0)
        ahead_send[...] = jnp.where(row8 == 3, mark, leave_moving[2, last])
        travels.append(send_leaving(ahead_send, ahead_recv, 2 * len(OFFSETS) + 6, 2, last))

    def between_all():
        between_second()
        ahead()

    exchange(1, between_all, lambda: leave((2, last)))
    leave((0, 0), (0, 1))
    leave((2, first), (1, 0), (1, 1))

    def finish(i, carry):
        here = pl.ds(pl.multiple_of(i * CHUNK, CHUNK), CHUNK)
        velocity_out[:, here] = gather_collide(1, here)[0:3]
        return carry

    lax.fori_loop(0, solvent_chunks, finish, 0, unroll=solvent_chunks)
    bead_out[...] = gather_collide(1, pl.ds(solvent, beads))[0:3]

    remote(ahead_recv, ahead_recv, 2 * len(OFFSETS) + 6, (0, 0, 1)).wait_recv()
    got = ahead_recv[...]
    mark = got[3:4]
    shared = jnp.dot(
        results[pl.ds(pl.multiple_of(128 * last, 16), 16), :],
        one_hot(mark.astype(I32)),
        preferred_element_type=F32,
    )
    got = rotate(got, shared[0:8], tables)
    arrived = leave_recv.at[2, last]
    remote(arrived, arrived, leave_number(2, first), (0, 0, 1)).wait_recv()
    got = jnp.where(mark >= 0.0, got, leave_recv[2, last])
    arrived = leave_recv.at[2, first]
    remote(arrived, arrived, leave_number(2, last), (0, 0, 1)).wait_recv()
    for side in range(2):
        arrivals_out[2, :, side, :] = jnp.where(last == side, got, leave_recv[2, side])[0:3]
    for d in range(2):
        for side in range(2):
            arrived = leave_recv.at[d, side]
            remote(arrived, arrived, leave_number(d, 1 - side), (0, 0, 1)).wait_recv()
            arrivals_out[d, :, side, :] = leave_recv[d, side, 0:3, :]
    for travel in travels:
        travel.wait_send()


def write(*refs):
    sems = refs[-1]
    count = len(refs) // 2
    copies = [
        pltpu.make_async_copy(refs[i], refs[count + i], sems.at[i]) for i in range(count)
    ]
    for copy in copies:
        copy.start()
    for copy in copies:
        copy.wait()


def per_device(
    velocity, position, bead_velocity, bead_mass, bead_position, grid_shift, rot_axis,
    leave_count, leave_index,
):
    solvent, beads = velocity.shape[1], bead_velocity.shape[1]
    count = solvent + beads
    vmem = pl.BlockSpec(memory_space=pltpu.VMEM)
    velocity_out, bead_out, arrivals = pl.pallas_call(
        kernel,
        out_shape=(
            pltpu.VMEM((3, solvent), F32),
            pltpu.VMEM((3, beads), F32),
            pltpu.VMEM((3, 3, 2, CAP), F32),
        ),
        in_specs=[pl.BlockSpec(memory_space=pltpu.HBM)] * 10,
        out_specs=(vmem, vmem, vmem),
        scratch_shapes=[
            pltpu.SMEM((2, 3), I32),
            pltpu.SMEM((2, 3), I32),
            pltpu.VMEM((3, solvent), F32),
            pltpu.VMEM((3, 2, solvent), I32),
            pltpu.VMEM((3, beads), F32),
            pltpu.VMEM((1, beads), F32),
            pltpu.VMEM((3, 2, beads), I32),
            pltpu.VMEM((2, 4, 16, 32), I32),
            pltpu.VMEM((3, 2, CAP), I32),
            pltpu.VMEM((3, 8, LANES), F32),
            pltpu.SemaphoreType.DMA((10,)),
            pltpu.VMEM((8, count), F32),
            pltpu.VMEM((1, count), F32),
            pltpu.VMEM((2, 1, count), I32),
            pltpu.VMEM((2, 1, count), I32),
            pltpu.VMEM((2, COLUMNS, count), BF16),
            pltpu.VMEM((count, COLUMNS), BF16),
            pltpu.VMEM((8 * LAYERS, COLUMNS), F32),
            pltpu.VMEM((LAYERS, 8, WIDE), F32),
            pltpu.VMEM((8 * LAYERS, COLUMNS), BF16),
            pltpu.VMEM((2, 2, 16, LANES), F32),
            pltpu.VMEM((2, 2, 8, LANES), F32),
            pltpu.VMEM((2, 2, 6, 8, LANES), F32),
            pltpu.VMEM((2, 2, 6, 1, LANES), F32),
            pltpu.VMEM((2, 2, 2, 3, LANES), F32),
            pltpu.VMEM((2, 2, 8, LANES), F32),
            pltpu.VMEM((2, 6, 2, 8, LANES), F32),
            pltpu.VMEM((2, 2, 6, 8, LANES), F32),
            pltpu.VMEM((8 * solvent // LANES, LANES), BF16),
            pltpu.VMEM((3, 2, 8, CAP), F32),
            pltpu.VMEM((3, 2, 1, CAP), I32),
            pltpu.VMEM((3, 2, 1, CAP), F32),
            pltpu.VMEM((3, 2, COLUMNS, CAP), BF16),
            pltpu.VMEM((3, 2, 8, CAP), F32),
            pltpu.VMEM((3, 2, 8, CAP), F32),
            pltpu.VMEM((8, CAP), F32),
            pltpu.VMEM((8, CAP), F32),
            pltpu.SemaphoreType.DMA((2 * len(OFFSETS) + 7,)),
            pltpu.SemaphoreType.DMA((2 * len(OFFSETS) + 7,)),
        ],
        compiler_params=pltpu.CompilerParams(
            collective_id=0, has_side_effects=True, vmem_limit_bytes=62 * 1024 * 1024
        ),
        cost_estimate=pl.CostEstimate(flops=10**9, bytes_accessed=10**6, transcendentals=0),
        name="collisions",
    )(
        grid_shift,
        leave_count.reshape(3, 2).T,
        velocity,
        jnp.transpose(position, (1, 0, 2)),
        bead_velocity,
        bead_mass.reshape(1, beads),
        jnp.transpose(bead_position, (1, 0, 2)),
        jnp.swapaxes(rot_axis, 2, 3),
        leave_index,
        jnp.asarray(rotation_table()),
    )
    made = (velocity_out, bead_out, arrivals)
    velocity_out, bead_out, arrivals = pl.pallas_call(
        write,
        out_shape=tuple(jax.ShapeDtypeStruct(x.shape, x.dtype) for x in made),
        in_specs=[vmem] * 3,
        out_specs=(pl.BlockSpec(memory_space=pltpu.HBM),) * 3,
        scratch_shapes=[pltpu.SemaphoreType.DMA((3,))],
        compiler_params=pltpu.CompilerParams(vmem_limit_bytes=4 * 1024 * 1024),
        name="write_results",
    )(*made)
    return velocity_out, bead_out, jnp.transpose(arrivals, (0, 2, 1, 3))


def solution(mesh):
    return jax.shard_map(
        per_device,
        mesh=mesh,
        in_specs=(
            P(None, ("gx", "gy", "gz")),
            P(None, None, ("gx", "gy", "gz")),
            P(None, ("gx", "gy", "gz")),
            P(("gx", "gy", "gz")),
            P(None, None, ("gx", "gy", "gz")),
            P(),
            P(None, "gx", "gy", "gz"),
            P(None, None, ("gx", "gy", "gz")),
            P(None, None, ("gx", "gy", "gz")),
        ),
        out_specs=(
            P(None, ("gx", "gy", "gz")),
            P(None, ("gx", "gy", "gz")),
            P(None, None, None, ("gx", "gy", "gz")),
        ),
        check_vma=False,
    )
```

```python
import math

import jax
import jax.numpy as jnp
import numpy as np
from jax import lax
from jax.experimental import pallas as pl
from jax.experimental.pallas import tpu as pltpu
from jax.sharding import PartitionSpec as P

STEPS = 2
AXES = 64
CAP = 256
COSINE = math.cos(130.0 * math.pi / 180.0)
SINE = math.sin(130.0 * math.pi / 180.0)
GOLDEN = math.pi * (3.0 - math.sqrt(5.0))

LANES = 128
CHUNK = 1024
COLUMNS = 176
LAYERS = 18
WIDE = 256
MESH = pl.DeviceIdType.MESH
F32 = jnp.float32
BF16 = jnp.bfloat16
I32 = jnp.int32


def rotation_table():
    ordinal = np.arange(AXES) + 0.5
    height = 1.0 - 2.0 * ordinal / AXES
    radius = np.sqrt(1.0 - height * height)
    n = np.stack([radius * np.cos(ordinal * GOLDEN), radius * np.sin(ordinal * GOLDEN), height])
    zero = np.zeros(AXES)
    skew = np.array([[zero, -n[2], n[1]], [n[2], zero, -n[0]], [-n[1], n[0], zero]])
    matrix = COSINE * np.eye(3)[:, :, None] + SINE * skew + (1.0 - COSINE) * n[:, None] * n[None]
    table = np.zeros((3, 8, LANES), np.float32)
    for c in range(3):
        table[c, 0:3, :AXES] = matrix[:, c]
        table[c, 4:7, :AXES] = matrix[:, c]
    return table


PLANE = [(dx, dy) for dx in (-1, 0, 1) for dy in (-1, 0, 1)]
OFFSETS = [(dx, dy, dz) for dz in (-1, 1) for dx, dy in PLANE] + [
    (dx, dy, 0) for dx, dy in PLANE if (dx, dy) != (0, 0)
]
EDGES = [(dx, dy) for dx in (-1, 0, 1) for dy in (-1, 1)]


def moved_edge(edge, place):
    dx, dy = edge
    target = {1: 0, -1: 5}[dy] + (4 if dx == 1 else 0)
    source = {1: 5, -1: 0}[dy] + (4 if dx == -1 else 0)
    if dx == 0:
        chosen = (place >= target) & (place < target + 5)
    else:
        chosen = place == target
    return (target - source) % LANES, chosen


def rows_of(shape):
    return lax.broadcasted_iota(I32, shape, 0)


def lanes_of(shape):
    return lax.broadcasted_iota(I32, shape, 1)


def lanes_from(tile, source):
    return jnp.take_along_axis(tile, source & (LANES - 1), axis=1)


def cell_rows(coords, shift_ref, step):
    layer = []
    for d in range(3):
        shift = shift_ref[step, d]
        offset = jnp.where(shift > 0, 1, 0)
        layer.append(lax.shift_right_arithmetic(coords[d] - shift, 4) + offset)
    return column_of(layer[0], layer[1]), layer[2]


def column_of(first, second):
    inner = first * 32 + second
    return jnp.where(second == 32, first + 160, jnp.where(second == 0, first + 165, inner))


def one_hot(column):
    n = column.shape[1]
    rest = column.astype(F32) - rows_of((16, n)).astype(F32)
    rest = rest.astype(BF16)
    one, zero = jnp.ones((16, n), BF16), jnp.zeros((16, n), BF16)
    return jnp.concatenate(
        [jnp.where(rest == float(16 * j), one, zero) for j in range(COLUMNS // 16)], axis=0
    )


def deposit_rows(moving, weight, layer):
    n = moving.shape[1]
    row8 = rows_of((8, n))
    summand = moving * weight
    high = summand.astype(BF16).astype(F32)
    parts = jnp.where(row8 < 4, high, summand - high)
    parts = jnp.concatenate([parts, parts], axis=0).astype(BF16)
    half = lax.shift_right_logical(rows_of((16, n)), 3)
    rest = (layer - half).astype(F32).astype(BF16)
    zero = jnp.zeros((16, n), BF16)
    return jnp.concatenate(
        [jnp.where(rest == float(2 * j), parts, zero) for j in range(LAYERS // 2)], axis=0
    )


def collide(moving, layer, gathered, tables):
    found = [gathered[8 * z : 8 * z + 8] for z in range(17)]
    top = found.pop()
    wide = jnp.broadcast_to(layer, (8, layer.shape[1]))
    for bit in range(4):
        odd = (wide & (1 << bit)) != 0
        found = [jnp.where(odd, found[z + 1], found[z]) for z in range(0, len(found), 2)]
    chosen = jnp.where(wide == 16, top, found[0])
    return rotate(moving, chosen, tables)


def rotate(moving, chosen, tables):
    n = moving.shape[1]
    mean = chosen + pltpu.roll(chosen, 4, 0)
    axis = jnp.broadcast_to(mean[3:4], (8, n)).astype(I32)
    relative = moving - mean
    result = mean
    for c in range(3):
        columns = jnp.concatenate(
            [
                jnp.take_along_axis(tables[c], axis[:, i : i + LANES], axis=1)
                for i in range(0, n, LANES)
            ],
            axis=1,
        )
        result = result + columns * relative[c : c + 1]
    row8 = rows_of((8, n))
    return jnp.where((row8 & 3) == 3, 1.0, result)


def kernel(
    shift_hbm, count_hbm, velocity_hbm, position_hbm, bead_velocity_hbm, bead_mass_hbm,
    bead_position_hbm, rot_hbm, leave_hbm, table_hbm,
    velocity_out, bead_out, arrivals_out,
    shift_ref, count_ref, velocity_ref, position_ref, bead_velocity_ref, bead_mass_ref,
    bead_position_ref, rot_ref, leave_ref, table_ref, load_sem,
    moving, weight, cols, lays, onehots, turned_onehots, totals, cells, results,
    send_z, send_y, send_x, recv_edge, recv_line, recv_z, recv_y, recv_x,
    leave_table, leave_moving, leave_layer, leave_column, leave_onehot, leave_send, leave_recv,
    ahead_send, ahead_recv,
    send_sem, recv_sem,
):
    solvent = velocity_ref.shape[1]
    beads = bead_velocity_ref.shape[1]
    count = solvent + beads
    chunks = count // CHUNK

    names = ("gx", "gy", "gz")

    def device_at(offset):
        where = {}
        for name, step_by in zip(names, offset):
            if step_by is not None and not (isinstance(step_by, int) and step_by == 0):
                size, me = lax.axis_size(name), lax.axis_index(name)
                where[name] = lax.rem(me + size + step_by, size)
        return where

    last = lax.axis_index("gz") & 1
    first = 1 - last

    barrier = pltpu.get_barrier_semaphore()
    for dz in (2 * last - 1, 0, 2 * first - 1):
        for dx, dy in PLANE:
            if dx or dy or not isinstance(dz, int):
                pl.semaphore_signal(
                    barrier, inc=1, device_id=device_at((dx, dy, dz)), device_id_type=MESH
                )

    loads = [
        pltpu.make_async_copy(src, dst, load_sem.at[i])
        for i, (src, dst) in enumerate(
            (
                (shift_hbm, shift_ref),
                (position_hbm, position_ref),
                (bead_position_hbm, bead_position_ref),
                (velocity_hbm, velocity_ref),
                (bead_velocity_hbm, bead_velocity_ref),
                (bead_mass_hbm, bead_mass_ref),
                (rot_hbm, rot_ref),
                (leave_hbm, leave_ref),
                (count_hbm, count_ref),
                (table_hbm, table_ref),
            )
        )
    ]
    for copy in loads:
        copy.start()
    for copy in loads:
        copy.wait()

    def remote(src, dst, number, offset):
        return pltpu.make_async_remote_copy(
            src_ref=src,
            dst_ref=dst,
            send_sem=send_sem.at[number],
            recv_sem=recv_sem.at[number],
            device_id=device_at(offset),
            device_id_type=MESH,
        )

    def load(velocity, where, length):
        moving[0:3, pl.ds(where, length)] = velocity
        moving[3:4, pl.ds(where, length)] = jnp.ones((1, length), F32)
        moving[4:7, pl.ds(where, length)] = velocity
        moving[7:8, pl.ds(where, length)] = jnp.ones((1, length), F32)

    load(velocity_ref[...], 0, solvent)
    load(bead_velocity_ref[...], solvent, beads)
    weight[:, 0:solvent] = jnp.ones((1, solvent), F32)
    weight[:, solvent:count] = bead_mass_ref[...]

    def place(step, first, number):
        def body(i, carry):
            here = pl.ds(pl.multiple_of(i * CHUNK, CHUNK), CHUNK)
            coords = [position_ref[d, step : step + 1, here] for d in range(3)]
            column, layer = cell_rows(coords, shift_ref, step)
            cols[step, :, here] = column
            lays[step, :, here] = layer
            onehots[step, :, here] = one_hot(column)
            return carry

        lax.fori_loop(first, first + number, body, 0, unroll=number)

    def place_beads(step):
        here = pl.ds(solvent, beads)
        coords = [bead_position_ref[d, step : step + 1, :] for d in range(3)]
        column, layer = cell_rows(coords, shift_ref, step)
        cols[step, :, here] = column
        lays[step, :, here] = layer
        onehots[step, :, here] = one_hot(column)

    def deposit(step, here, moved):
        rows = deposit_rows(moved, weight[:, here], lays[step, :, here])
        if step == 0:
            totals[...] += lax.dot_general(
                rows, onehots[0, :, here], (((1,), (1,)), ((), ())), preferred_element_type=F32
            )
        else:
            totals[...] += jnp.dot(rows, turned_onehots[here, :], preferred_element_type=F32)

    lane = lanes_of((8, LANES))

    def own_axes(step):
        offset = [jnp.where(shift_ref[step, d] > 0, 1, 0) for d in range(3)]
        local = rows_of((LANES, WIDE))
        target = column_of(
            lax.shift_right_logical(local, 5) + offset[0], (local & 31) + offset[1]
        )
        spread = jnp.where(lanes_of((LANES, WIDE)) == target, 1.0, 0.0).astype(BF16)
        held = jnp.concatenate([rot_ref[step, x] for x in range(4)], axis=1)
        by_layer = jnp.dot(
            held.astype(F32).astype(BF16), spread, preferred_element_type=F32
        )
        above = jnp.concatenate([jnp.zeros((1, WIDE), F32), by_layer], axis=0)
        below = jnp.concatenate([by_layer, jnp.zeros((1, WIDE), F32)], axis=0)
        return jnp.where(offset[2] > 0, above, below)

    def exchange(step, between, early=None):
        axes = own_axes(step)
        row8w = rows_of((8, WIDE))
        row8 = rows_of((8, LANES))
        cells[:, :, COLUMNS:WIDE] = jnp.zeros((LAYERS, 8, WIDE - COLUMNS), F32)
        cells[17] = jnp.zeros((8, WIDE), F32)

        def settle(z):
            part = totals[8 * z : 8 * z + 8, :]
            cells[z, :, 0:COLUMNS] = part + pltpu.roll(part, 4, 0)
            cells[z] = jnp.where(row8w == 7, axes[z : z + 1], cells[z])

        settle(0)
        settle(16)

        def pack_end(side):
            near, far = cells[16 * side, :, 0:LANES], cells[16 * side, :, LANES:WIDE]
            edge = lanes_from(far, lane + 32 - 10 * row8)
            edge = jnp.where((lane >= 10 * row8) & (lane < 10 * row8 + 10), edge, 0.0)
            send_z[step, side, 2:3] = jnp.sum(edge, axis=0, keepdims=True)
            for at, tile in ((0, near), (3, far)):
                line = lanes_from(tile, lane & 31)
                line = jnp.where(lax.shift_right_logical(lane, 5) == (row8 & 3), line, 0.0)
                for half in range(2):
                    send_z[step, side, at + half : at + half + 1] = jnp.sum(
                        line[4 * half : 4 * half + 4], axis=0, keepdims=True
                    )
            send_z[step, side, 5:9] = near[0:4]
            send_z[step, side, 9:10] = near[7:8]

        plane_travels, end_travels = [], []

        def send(src, dst, number, offset):
            travel = remote(src, dst, len(OFFSETS) * step + number, offset)
            travel.start()
            return travel

        def send_end(side):
            for dx, dy in sorted(PLANE, key=lambda place: -abs(place[1])):
                if dy:
                    src = send_z.at[step, side, pl.ds(2, 1)]
                    dst = recv_edge.at[step, 1 - side, EDGES.index((-dx, -dy))]
                elif dx:
                    src = send_z.at[step, side, pl.ds(1 + dx, 3)]
                    dst = recv_line.at[step, 1 - side, (1 - dx) // 2]
                else:
                    src = send_z.at[step, side, pl.ds(2, 8)]
                    dst = recv_z.at[step, 1 - side]
                number = 9 * side + PLANE.index((dx, dy))
                end_travels.append(send(src, dst, number, (dx, dy, 2 * side - 1)))

        pack_end(last)
        if step > 0:
            send_end(last)
        pack_end(first)
        if step > 0:
            send_end(first)

        for z in range(1, 16):
            settle(z)
        for group in range(2):
            packed = jnp.zeros((8, LANES), F32)
            for j in range(9):
                z = 9 * group + j
                if z < 17:
                    turned = pltpu.roll(cells[z, :, LANES:WIDE], (12 * j - 32) % LANES, 1)
                    packed = jnp.where((lane >= 12 * j) & (lane < 12 * j + 10), turned, packed)
            send_y[step, group] = packed
        def send_second():
            for dx in (-1, 0, 1):
                for dy in (-1, 1):
                    back = EDGES.index((-dx, -dy))
                    plane_travels.append(
                        send(
                            send_y.at[step],
                            recv_y.at[step, back],
                            OFFSETS.index((dx, dy, 0)),
                            (dx, dy, 0),
                        )
                    )

        if step > 0:
            send_second()

        for group in range(6):
            packed_low = jnp.zeros((8, LANES), F32)
            packed_high = jnp.zeros((8, LANES), F32)
            for j in range(3):
                z = 3 * group + j
                if z < 17:
                    near, far = cells[z, :, 0:LANES], cells[z, :, LANES:WIDE]
                    face_low = jnp.where(lane < 32, near, far)
                    face_high = jnp.where(lane < 32, far, pltpu.roll(far, LANES - 4, 1))
                    if j:
                        face_low = pltpu.roll(face_low, 42 * j, 1)
                        face_high = pltpu.roll(face_high, 42 * j, 1)
                    inside = (lane >= 42 * j) & (lane < 42 * j + 38)
                    packed_low = jnp.where(inside, face_low, packed_low)
                    packed_high = jnp.where(inside, face_high, packed_high)
            send_x[step, 0, group] = packed_low
            send_x[step, 1, group] = packed_high
        if step == 0:
            pl.semaphore_wait(barrier, len(OFFSETS))
            send_end(last)
            send_end(first)
            send_second()
        for side in range(2):
            offset = (2 * side - 1, 0, 0)
            plane_travels.append(
                send(
                    send_x.at[step, side],
                    recv_x.at[step, 1 - side],
                    OFFSETS.index(offset),
                    offset,
                )
            )

        between()

        for travel in plane_travels:
            travel.wait()
        place12 = lax.rem(lane, 12)
        both_groups = []
        for group in range(2):
            both = jnp.zeros((8, LANES), F32)
            for k, edge in enumerate(EDGES):
                turn_by, chosen = moved_edge(edge, place12)
                both += jnp.where(chosen, pltpu.roll(recv_y[step, k, group], turn_by, 1), 0.0)
            both_groups.append(both)
        ends = (lane == 32) | (lane == 37)
        ends_high = (lane == 36) | (lane == 41)
        for group in range(6):
            for j in range(3):
                z = 3 * group + j
                if z < 17:
                    from_low, from_high = recv_x[step, 0, group], recv_x[step, 1, group]
                    if j:
                        from_low = pltpu.roll(from_low, LANES - 42 * j, 1)
                        from_high = pltpu.roll(from_high, LANES - 42 * j, 1)
                    shift_by = (32 - 12 * (z % 9)) % LANES
                    from_second = pltpu.roll(both_groups[z // 9], shift_by, 1)
                    cells[z, :, 0:LANES] += jnp.where(lane < 32, from_low, 0.0)
                    cells[z, :, LANES:WIDE] += (
                        jnp.where(
                            lane < 32,
                            from_high,
                            jnp.where(
                                ends,
                                from_low,
                                jnp.where(ends_high, pltpu.roll(from_high, 4, 1), 0.0),
                            ),
                        )
                        + jnp.where((lane >= 32) & (lane < 42), from_second, 0.0)
                    )

        def entry_of(z):
            full = cells[z]
            full = jnp.where((row8w >= 4) & (row8w < 7), pltpu.roll(full, 4, 0), full)
            mean = full / jnp.maximum(full[3:4], 1.0)
            rounded = mean.astype(BF16).astype(F32)
            entry = jnp.where(row8w < 4, rounded, mean - rounded)
            return jnp.where(row8w == 3, full[7:8], jnp.where(row8w == 7, 0.0, entry))

        def finish_pair(z):
            pair = jnp.concatenate([entry_of(z), entry_of(z + 1)], axis=0).astype(BF16)
            where = 8 * z if isinstance(z, int) else pl.multiple_of(8 * z, 16)
            results[pl.ds(where, 16), :] = pair[:, 0:COLUMNS]

        for z in range(2, 16, 2):
            finish_pair(z)

        def collect(side):
            for dx, dy in PLANE:
                if dy:
                    landed = recv_edge.at[step, side, EDGES.index((dx, dy))]
                elif dx:
                    landed = recv_line.at[step, side, (1 + dx) // 2]
                else:
                    landed = recv_z.at[step, side]
                number = len(OFFSETS) * step + 9 * (1 - side) + PLANE.index((-dx, -dy))
                remote(landed, landed, number, (0, 0, 1)).wait_recv()
            face = recv_z[step, side]
            lane1 = lanes_of((1, LANES))
            place10 = lax.rem(lane1, 10)
            edge = face[0:1]
            for k, offset in enumerate(EDGES):
                turn_by, chosen = moved_edge(offset, place10)
                edge += jnp.where(chosen, pltpu.roll(recv_edge[step, side, k], turn_by, 1), 0.0)
            low, high = recv_line[step, side, 0], recv_line[step, side, 1]
            at_low, at_high = (place10 == 0) | (place10 == 5), (place10 == 4) | (place10 == 9)
            edge += jnp.where(at_low, pltpu.roll(low[0:1], LANES - 4, 1), 0.0)
            edge += jnp.where(at_high, pltpu.roll(high[2:3], 4, 1), 0.0)
            edge = lanes_from(jnp.broadcast_to(edge, (8, LANES)), lane - 32 + 10 * row8)
            lines = []
            for line in (low[1:3], face[1:3] + high[0:2]):
                wide = jnp.where(row8 < 4, line[0:1], line[1:2])
                lines.append(lanes_from(wide, (lane & 31) + 32 * (row8 & 3)))
            rest = jnp.where(row8 == 7, face, pltpu.roll(face, 5, 0))
            near = rest + jnp.where(lane < 32, lines[0], 0.0)
            far = jnp.where(lane < 32, lines[1], jnp.where(lane < 42, edge, 0.0))
            cells[16 * side, :, 0:LANES] += near
            cells[16 * side, :, LANES:WIDE] += far
            finish_pair(16 * side)

        collect(first)
        if early is not None:
            finish_pair(16 * last)
            early()
        collect(last)
        for travel in end_travels:
            travel.wait_send()

    tables = [table_ref[c] for c in range(3)]

    def gather_collide(step, here):
        gathered = jnp.dot(results[...], onehots[step, :, here], preferred_element_type=F32)
        return collide(moving[:, here], lays[step, :, here], gathered, tables)

    solvent_chunks = solvent // CHUNK
    totals[...] = jnp.zeros_like(totals)
    place(0, 0, solvent_chunks)
    place_beads(0)

    def first_deposit(i, carry):
        here = pl.ds(pl.multiple_of(i * CHUNK, CHUNK), CHUNK)
        deposit(0, here, moving[:, here])
        return carry

    lax.fori_loop(0, chunks, first_deposit, 0, unroll=chunks)

    def between_first():
        place(1, 0, solvent_chunks)
        place_beads(1)

        def transpose(i, carry):
            here = pl.ds(pl.multiple_of(i * CHUNK, CHUNK), CHUNK)
            turned_onehots[here, :] = onehots[1, :, here].T
            return carry

        lax.fori_loop(0, chunks, transpose, 0, unroll=chunks)

    exchange(0, between_first)

    totals[...] = jnp.zeros_like(totals)

    def turn(i, carry):
        here = pl.ds(pl.multiple_of(i * CHUNK, CHUNK), CHUNK)
        moved = gather_collide(0, here)
        moving[:, here] = moved
        deposit(1, here, moved)
        return carry

    lax.fori_loop(0, chunks, turn, 0, unroll=chunks)

    tiles = solvent // LANES

    def between_second():
        row8 = rows_of((8, LANES))

        def fill(i, carry):
            parts = []
            for k in range(2):
                here = pl.ds(pl.multiple_of((2 * i + k) * LANES, LANES), LANES)
                now = moving[:, here]
                rounded = now.astype(BF16).astype(F32)
                entry = jnp.where(row8 < 4, rounded, now - rounded)
                entry = jnp.where(row8 == 3, cols[1, :, here].astype(F32), entry)
                parts.append(jnp.where(row8 == 7, lays[1, :, here].astype(F32), entry))
            leave_table[pl.ds(pl.multiple_of(16 * i, 16), 16), :] = jnp.concatenate(
                parts, axis=0
            ).astype(BF16)
            return carry

        lax.fori_loop(0, tiles // 2, fill, 0, unroll=8)

        def pick(d, carry):
            for side in range(2):
                index = jnp.maximum(leave_ref[d, side : side + 1, :], 0)
                offset = (index & (LANES - 1)).astype(F32)
                rest = (offset - rows_of((16, CAP)).astype(F32)).astype(BF16)
                one, zero = jnp.ones((16, CAP), BF16), jnp.zeros((16, CAP), BF16)
                spot = jnp.concatenate(
                    [jnp.where(rest == float(16 * j), one, zero) for j in range(8)], axis=0
                )
                found = jnp.dot(leave_table[...], spot, preferred_element_type=F32)
                tile = lax.shift_right_logical(index, 7)
                chosen = found[0:8]
                for i in range(1, tiles):
                    chosen = jnp.where(tile == i, found[8 * i : 8 * i + 8], chosen)
                leave_moving[d, side] = chosen + pltpu.roll(chosen, 4, 0)
                leave_layer[d, side] = chosen[7:8].astype(I32)
                leave_column[d, side] = chosen[3:4]
                leave_onehot[d, side] = one_hot(chosen[3:4].astype(I32))
            return carry

        lax.fori_loop(0, 3, pick, 0, unroll=3)

    row8 = rows_of((8, CAP))
    slot = lanes_of((8, CAP))

    def leave_number(d, side):
        return 2 * len(OFFSETS) + 2 * d + side

    def send_leaving(src, dst, number, d, side):
        offset = tuple(2 * side - 1 if axis == d else None for axis in range(3))
        travel = remote(src, dst, number, offset)
        travel.start()
        return travel

    travels = []

    def leave(*faces):
        found = [
            jnp.dot(results[...], leave_onehot[face], preferred_element_type=F32)
            for face in faces
        ]
        for (d, side), gathered in zip(faces, found):
            moved = collide(leave_moving[d, side], leave_layer[d, side], gathered, tables)
            leave_send[d, side] = jnp.where(slot < count_ref[side, d], moved, 0.0)
        for d, side in faces:
            travels.append(
                send_leaving(
                    leave_send.at[d, side],
                    leave_recv.at[d, 1 - side],
                    leave_number(d, side),
                    d,
                    side,
                )
            )

    def ahead():
        shared = jnp.broadcast_to(leave_layer[2, last], (8, CAP)) == 16 * last
        shared &= slot < count_ref[last, 2]
        mark = jnp.where(shared, leave_column[2, last], -1.0)
        ahead_send[...] = jnp.where(row8 == 3, mark, leave_moving[2, last])
        travels.append(send_leaving(ahead_send, ahead_recv, 2 * len(OFFSETS) + 6, 2, last))

    def between_all():
        between_second()
        ahead()

    exchange(1, between_all, lambda: leave((2, last)))
    leave((0, 0), (0, 1))
    leave((2, first), (1, 0), (1, 1))

    def finish(i, carry):
        here = pl.ds(pl.multiple_of(i * CHUNK, CHUNK), CHUNK)
        velocity_out[:, here] = gather_collide(1, here)[0:3]
        return carry

    lax.fori_loop(0, solvent_chunks, finish, 0, unroll=solvent_chunks)
    bead_out[...] = gather_collide(1, pl.ds(solvent, beads))[0:3]

    remote(ahead_recv, ahead_recv, 2 * len(OFFSETS) + 6, (0, 0, 1)).wait_recv()
    got = ahead_recv[...]
    mark = got[3:4]
    shared = jnp.dot(
        results[pl.ds(pl.multiple_of(128 * last, 16), 16), :],
        one_hot(mark.astype(I32)),
        preferred_element_type=F32,
    )
    got = rotate(got, shared[0:8], tables)
    arrived = leave_recv.at[2, last]
    remote(arrived, arrived, leave_number(2, first), (0, 0, 1)).wait_recv()
    got = jnp.where(mark >= 0.0, got, leave_recv[2, last])
    arrived = leave_recv.at[2, first]
    remote(arrived, arrived, leave_number(2, last), (0, 0, 1)).wait_recv()
    for side in range(2):
        arrivals_out[2, :, side, :] = jnp.where(last == side, got, leave_recv[2, side])[0:3]
    for d in range(2):
        for side in range(2):
            arrived = leave_recv.at[d, side]
            remote(arrived, arrived, leave_number(d, 1 - side), (0, 0, 1)).wait_recv()
            arrivals_out[d, :, side, :] = leave_recv[d, side, 0:3, :]
    for travel in travels:
        travel.wait_send()


def write(*refs):
    sems = refs[-1]
    count = len(refs) // 2
    copies = [
        pltpu.make_async_copy(refs[i], refs[count + i], sems.at[i]) for i in range(count)
    ]
    for copy in copies:
        copy.start()
    for copy in copies:
        copy.wait()


def per_device(
    velocity, position, bead_velocity, bead_mass, bead_position, grid_shift, rot_axis,
    leave_count, leave_index,
):
    solvent, beads = velocity.shape[1], bead_velocity.shape[1]
    count = solvent + beads
    vmem = pl.BlockSpec(memory_space=pltpu.VMEM)
    velocity_out, bead_out, arrivals = pl.pallas_call(
        kernel,
        out_shape=(
            pltpu.VMEM((3, solvent), F32),
            pltpu.VMEM((3, beads), F32),
            pltpu.VMEM((3, 3, 2, CAP), F32),
        ),
        in_specs=[pl.BlockSpec(memory_space=pltpu.HBM)] * 10,
        out_specs=(vmem, vmem, vmem),
        scratch_shapes=[
            pltpu.SMEM((2, 3), I32),
            pltpu.SMEM((2, 3), I32),
            pltpu.VMEM((3, solvent), F32),
            pltpu.VMEM((3, 2, solvent), I32),
            pltpu.VMEM((3, beads), F32),
            pltpu.VMEM((1, beads), F32),
            pltpu.VMEM((3, 2, beads), I32),
            pltpu.VMEM((2, 4, 16, 32), I32),
            pltpu.VMEM((3, 2, CAP), I32),
            pltpu.VMEM((3, 8, LANES), F32),
            pltpu.SemaphoreType.DMA((10,)),
            pltpu.VMEM((8, count), F32),
            pltpu.VMEM((1, count), F32),
            pltpu.VMEM((2, 1, count), I32),
            pltpu.VMEM((2, 1, count), I32),
            pltpu.VMEM((2, COLUMNS, count), BF16),
            pltpu.VMEM((count, COLUMNS), BF16),
            pltpu.VMEM((8 * LAYERS, COLUMNS), F32),
            pltpu.VMEM((LAYERS, 8, WIDE), F32),
            pltpu.VMEM((8 * LAYERS, COLUMNS), BF16),
            pltpu.VMEM((2, 2, 16, LANES), F32),
            pltpu.VMEM((2, 2, 8, LANES), F32),
            pltpu.VMEM((2, 2, 6, 8, LANES), F32),
            pltpu.VMEM((2, 2, 6, 1, LANES), F32),
            pltpu.VMEM((2, 2, 2, 3, LANES), F32),
            pltpu.VMEM((2, 2, 8, LANES), F32),
            pltpu.VMEM((2, 6, 2, 8, LANES), F32),
            pltpu.VMEM((2, 2, 6, 8, LANES), F32),
            pltpu.VMEM((8 * solvent // LANES, LANES), BF16),
            pltpu.VMEM((3, 2, 8, CAP), F32),
            pltpu.VMEM((3, 2, 1, CAP), I32),
            pltpu.VMEM((3, 2, 1, CAP), F32),
            pltpu.VMEM((3, 2, COLUMNS, CAP), BF16),
            pltpu.VMEM((3, 2, 8, CAP), F32),
            pltpu.VMEM((3, 2, 8, CAP), F32),
            pltpu.VMEM((8, CAP), F32),
            pltpu.VMEM((8, CAP), F32),
            pltpu.SemaphoreType.DMA((2 * len(OFFSETS) + 7,)),
            pltpu.SemaphoreType.DMA((2 * len(OFFSETS) + 7,)),
        ],
        compiler_params=pltpu.CompilerParams(
            collective_id=0, has_side_effects=True, vmem_limit_bytes=62 * 1024 * 1024
        ),
        cost_estimate=pl.CostEstimate(flops=10**9, bytes_accessed=10**6, transcendentals=0),
        name="collisions",
    )(
        grid_shift,
        leave_count.reshape(3, 2).T,
        velocity,
        jnp.transpose(position, (1, 0, 2)),
        bead_velocity,
        bead_mass.reshape(1, beads),
        jnp.transpose(bead_position, (1, 0, 2)),
        jnp.swapaxes(rot_axis, 2, 3),
        leave_index,
        jnp.asarray(rotation_table()),
    )
    made = (velocity_out, bead_out, arrivals)
    velocity_out, bead_out, arrivals = pl.pallas_call(
        write,
        out_shape=tuple(jax.ShapeDtypeStruct(x.shape, x.dtype) for x in made),
        in_specs=[vmem] * 3,
        out_specs=(pl.BlockSpec(memory_space=pltpu.HBM),) * 3,
        scratch_shapes=[pltpu.SemaphoreType.DMA((3,))],
        compiler_params=pltpu.CompilerParams(vmem_limit_bytes=4 * 1024 * 1024),
        name="write_results",
    )(*made)
    return velocity_out, bead_out, jnp.transpose(arrivals, (0, 2, 1, 3))


def solution(mesh):
    return jax.shard_map(
        per_device,
        mesh=mesh,
        in_specs=(
            P(None, ("gx", "gy", "gz")),
            P(None, None, ("gx", "gy", "gz")),
            P(None, ("gx", "gy", "gz")),
            P(("gx", "gy", "gz")),
            P(None, None, ("gx", "gy", "gz")),
            P(),
            P(None, "gx", "gy", "gz"),
            P(None, None, ("gx", "gy", "gz")),
            P(None, None, ("gx", "gy", "gz")),
        ),
        out_specs=(
            P(None, ("gx", "gy", "gz")),
            P(None, ("gx", "gy", "gz")),
            P(None, None, None, ("gx", "gy", "gz")),
        ),
        check_vma=False,
    )
```
